128 devices in a mesh: row: 8 (over z, core), col: 16 (over x, y).
Axes of the slice: x: 4, y: 4, z: 4, core: 2. Of those that a mesh axis runs over, the one named last changes fastest.
Arguments:
- acts: bfloat16 [1024, 12288], P('col', 'row'), may hold values from -6 to 6
- up_weight: bfloat16 [12288, 49152], P('row', 'col'), may hold values from -0.0546875 to 0.0546875
- out_grad: bfloat16 [1024, 49152], P('row', 'col'), may hold values from -6 to 6
Outputs:
- input_grad: bfloat16 [1024, 12288], P('col', 'row')
- weight_grad: bfloat16 [12288, 49152], P('row', 'col')
The draws below stay inside these ranges and needn't reach their ends.
All inputs are finite; a program needn't handle non-finite values.
Results may differ from the reference program's by a relative error of at most 0.023.
Values may be sent and summed in bfloat16 or wider, within the bound.
A program may use at most 128 MiB of HBM per device.

```python
import jax
import jax.numpy as jnp
from jax import lax

D = 12288
FF = 49152
TOKENS = 1024
N_ROW = 8
N_COL = 16


def steps_of(key, shape, split, smallest, top_value):
    level, own = 1.0, jax.random.fold_in(key, 6)
    for axis_at, blocks in split:
        heights = jnp.exp(jax.random.uniform(jax.random.fold_in(own, axis_at), (blocks,), jnp.float32, smallest / len(split), top_value / len(split)))
        level = level * jnp.repeat(heights, shape[axis_at] // blocks).reshape([-1 if axis == axis_at else 1 for axis in range(len(shape))])
    return level


def bell_draw(own_key, dims, deviation, bound, pieces=(), dtype=jnp.bfloat16):
    level = steps_of(own_key, dims, pieces, -0.22, 0.18) if pieces else 1.0
    drawn = jax.random.normal(own_key, dims, jnp.float32) * deviation * level
    return jnp.minimum(jnp.maximum(drawn, -bound), bound).astype(dtype)


def setup_inputs(seed: int = 0) -> dict:
    key_of = jax.random.split(jax.random.key(seed), 4)
    return {
        "acts": bell_draw(key_of[0], (TOKENS, D), 1.0, 6.0, ((0, 16), (1, 8))),
        "up_weight": bell_draw(key_of[1], (D, FF), D ** -0.5, 0.0546875, ((0, 8), (1, 16))),
        "out_grad": bell_draw(key_of[2], (TOKENS, FF), 1.0, 6.0, ((0, 8), (1, 16))),
    }


def gelu_slope(pre):
    cdf = 0.5 * (1.0 + lax.erf(pre * 0.7071067811865476))
    dens = jnp.exp(-0.5 * pre * pre) * 0.3989422804014327
    return cdf + pre * dens


def rounded(term):
    return lax.optimization_barrier(term.astype(jnp.bfloat16)).astype(jnp.float32)


def reference(acts, up_weight, out_grad):
    width_block = D // N_ROW
    pre = jnp.zeros((TOKENS, FF), jnp.float32)
    for block in range(N_ROW):
        lower = block * width_block
        term = jnp.dot(acts[:, lower:lower + width_block], up_weight[lower:lower + width_block], preferred_element_type=jnp.float32)
        pre = pre + rounded(term)
    hidden_grad = (out_grad.astype(jnp.float32) * gelu_slope(pre)).astype(jnp.bfloat16)
    hidden_block = FF // N_COL
    summed = jnp.zeros((TOKENS, D), jnp.float32)
    for block in range(N_COL):
        lower = block * hidden_block
        term = lax.dot_general(hidden_grad[:, lower:lower + hidden_block], up_weight[:, lower:lower + hidden_block], (((1,), (1,)), ((), ())), preferred_element_type=jnp.float32)
        summed = summed + rounded(term)
    input_grad = summed.astype(jnp.bfloat16)
    weight_grad = lax.dot_general(acts, hidden_grad, (((0,), (0,)), ((), ())), preferred_element_type=jnp.float32).astype(jnp.bfloat16)
    return input_grad, weight_grad
```

```python
import functools

import jax
import jax.numpy as jnp
from jax import lax
from jax.experimental import pallas as pl
from jax.experimental.pallas import tpu as pltpu
from jax.sharding import PartitionSpec as P

F32, BF16 = jnp.float32, jnp.bfloat16
MESH = pl.DeviceIdType.MESH
N_SEMS = 128


def gelu_slope(pre):
    cdf = 0.5 * (1.0 + lax.erf(pre * 0.7071067811865476))
    dens = jnp.exp(-0.5 * pre * pre) * 0.3989422804014327
    return cdf + pre * dens


def tile_of(size, want):
    return want if size % want == 0 else size


def kernel(
    acts_ref, w_ref, og_ref, ig_ref, wg_ref,
    acts, w, og, acts_t, part, sib_in, z_in_m, z_in_p, hidden, ig, y_in_m, y_in_p, xs, x_in_m, x_in_p,
    local_sem, send_sem, recv_sem,
):
    tb, feats = acts_ref.shape
    ob, hid = og_ref.shape
    half, quarter = ob // 2, ob // 4
    grp = 4 * tb
    tn = tile_of(hid, 512)
    tf = tile_of(feats, 512)
    tm = tile_of(feats, 256)

    row, col = lax.axis_index("row"), lax.axis_index("col")
    z, k = lax.div(row, 2), lax.rem(row, 2)
    x, y = lax.div(col, 4), lax.rem(col, 4)
    nxt = lambda v, by: lax.rem(v + by, 4)
    sib = {"row": z * 2 + (1 - k)}
    zp, zm = {"row": nxt(z, 1) * 2 + k}, {"row": nxt(z, 3) * 2 + k}
    xp, xm = {"col": nxt(x, 1) * 4 + y}, {"col": nxt(x, 3) * 4 + y}
    yp, ym = {"col": x * 4 + nxt(y, 1)}, {"col": x * 4 + nxt(y, 3)}

    sent = []

    def send(src, dst, to):
        i = len(sent)
        copy = pltpu.make_async_remote_copy(
            src_ref=src, dst_ref=dst, send_sem=send_sem.at[i], recv_sem=recv_sem.at[i],
            device_id=to, device_id_type=MESH,
        )
        copy.start()
        sent.append(copy)
        return copy

    def at(ref, start, size):
        return ref.at[pl.ds(pl.multiple_of(start, size), size)]

    barrier = pltpu.get_barrier_semaphore()
    for to in (sib, zp, zm, xp, xm, yp, ym):
        pl.semaphore_signal(barrier, inc=1, device_id=to, device_id_type=MESH)
    own_acts = at(acts, (x * 4 + y) * tb, tb)
    load_acts = pltpu.make_async_copy(acts_ref, own_acts, local_sem.at[0])
    load_w = pltpu.make_async_copy(w_ref, w, local_sem.at[1])
    load_og = pltpu.make_async_copy(og_ref, og, local_sem.at[2])
    load_acts.start()
    load_w.start()
    load_og.start()
    load_acts.wait()
    pl.semaphore_wait(barrier, 7)

    hb = tb // 2

    def ag_start(block, to_p, to_m):
        a = lambda by: at(acts, block(by), hb)
        b = lambda by: at(acts, block(by) + hb, hb)
        pa = send(a(0), a(0), to_p)
        mb = send(b(0), b(0), to_m)
        pb = send(b(0), b(0), to_p)
        ma = send(a(0), a(0), to_m)
        return a, b, pa, mb, pb, ma, to_p, to_m

    def ag_forward(state):
        a, b, pa, mb, pb, ma, to_p, to_m = state
        pa.wait_recv()
        fa = send(a(3), a(3), to_p)
        mb.wait_recv()
        fb = send(b(1), b(1), to_m)
        return pb, ma, fa, fb

    def ag_finish(copies):
        for copy in copies:
            copy.wait_recv()

    ag_finish(ag_forward(ag_start(lambda by: (nxt(x, by) * 4 + y) * tb, xp, xm)))
    order = [nxt(z, 2), nxt(z, 1), nxt(z, 3), z]
    y_start = lambda s: ag_start(lambda by: (order[s] * 4 + nxt(y, by)) * tb, yp, ym)

    def dot1(s):
        rows = pl.ds(pl.multiple_of(order[s] * grp, grp), grp)
        theirs = part.at[s, pl.ds(pl.multiple_of((1 - k) * ob, ob), ob)]
        sem = len(sent)

        def tile(n, carry):
            cols = pl.ds(pl.multiple_of(n * tn, tn), tn)
            part[s, :, cols] = jnp.dot(acts[rows, :], w[:, cols], preferred_element_type=F32).astype(BF16)
            pltpu.make_async_remote_copy(
                src_ref=theirs.at[:, cols], dst_ref=sib_in.at[s, :, cols], send_sem=send_sem.at[sem],
                recv_sem=recv_sem.at[sem], device_id=sib, device_id_type=MESH,
            ).start()
            return carry

        lax.fori_loop(0, hid // tn, tile, 0)
        whole = pltpu.make_async_remote_copy(
            src_ref=theirs, dst_ref=sib_in.at[s], send_sem=send_sem.at[sem],
            recv_sem=recv_sem.at[sem], device_id=sib, device_id_type=MESH,
        )
        sent.append(whole)
        return whole

    own_row = pl.multiple_of(k * ob, ob)

    def add_into(dst, dst_row, src, src_row, rows):
        step = min(rows, 32)
        for r in range(0, rows, step):
            def tile(n, carry):
                cols = pl.ds(pl.multiple_of(n * tn, tn), tn)
                into = pl.ds(pl.multiple_of(dst_row + r, step), step)
                total = dst[into, cols].astype(F32) + src[src_row + r:src_row + r + step, cols].astype(F32)
                dst[into, cols] = total.astype(BF16)
                return carry

            lax.fori_loop(0, dst.shape[-1] // tn, tile, 0)

    def core_sum(s, copy):
        copy.wait_recv()
        add_into(part.at[s], own_row, sib_in.at[s], 0, ob)

    mine = lambda s, start, size: part.at[s, pl.ds(pl.multiple_of(own_row + start, size), size)]

    g = ag_forward(y_start(0))
    nx = y_start(1)
    load_w.wait()
    ag_finish(g)
    c = dot1(0)
    g = ag_forward(nx)
    nx = y_start(2)
    core_sum(0, c)
    opp_p = send(mine(0, 0, half), z_in_m.at[0], zp)
    opp_m = send(mine(0, half, half), z_in_p.at[0], zm)
    ag_finish(g)
    c = dot1(1)
    g = ag_forward(nx)
    nx = y_start(3)
    core_sum(1, c)
    dir_p = send(mine(1, half, half), z_in_m.at[1], zp)
    ag_finish(g)
    c = dot1(2)
    g = ag_forward(nx)
    core_sum(2, c)
    dir_m = send(mine(2, 0, half), z_in_p.at[1], zm)
    ag_finish(g)
    c = dot1(3)
    opp_p.wait_recv()
    add_into(part.at[1], own_row, z_in_m.at[0], 0, half)
    acc_p = [send(mine(1, j * quarter, quarter), z_in_m.at[2, pl.ds(j * quarter, quarter)], zp) for j in range(2)]
    opp_m.wait_recv()
    add_into(part.at[2], own_row + half, z_in_p.at[0], 0, half)
    acc_m = [send(mine(2, half + j * quarter, quarter), z_in_p.at[2, pl.ds(j * quarter, quarter)], zm) for j in range(2)]
    core_sum(3, c)
    load_og.wait()

    def turn(n, carry):
        cols = pl.ds(pl.multiple_of(n * tm, tm), tm)
        for t in range(4):
            acts_t[cols, t * grp:(t + 1) * grp] = acts[t * grp:(t + 1) * grp, cols].T
        return carry

    lax.fori_loop(0, feats // tm, turn, 0)

    dir_p.wait_recv()
    dir_m.wait_recv()
    base = lambda zz, kk: zz * 2 * ob + kk * ob
    piece = lambda first, start: at(hidden, first + start, quarter)
    own_base = base(z, k)

    def slope_piece(start, from_m, from_p):
        def tile(n, carry):
            cols = pl.ds(pl.multiple_of(n * tn, tn), tn)
            own = part[3, pl.ds(pl.multiple_of(own_row + start, quarter), quarter), cols]
            pre = own.astype(F32) + from_m[:, cols].astype(F32) + from_p[:, cols].astype(F32)
            grad = og[start:start + quarter, cols].astype(F32) * gelu_slope(pre)
            hidden[pl.ds(pl.multiple_of(own_base + start, quarter), quarter), cols] = grad.astype(BF16)
            return carry

        lax.fori_loop(0, hid // tn, tile, 0)
        here = piece(own_base, start)
        return send(here, here, sib), send(here, here, zp), send(here, here, zm)

    starts = (0, half, quarter, half + quarter)
    own_sends = []
    for j in range(2):
        q = pl.ds(j * quarter, quarter)
        acc_p[j].wait_recv()
        own_sends.append(slope_piece(j * quarter, z_in_m.at[2, q], z_in_p.at[1, q]))
        acc_m[j].wait_recv()
        own_sends.append(slope_piece(half + j * quarter, z_in_m.at[1, q], z_in_p.at[2, q]))

    def dot2(s, g):
        rows = pl.ds(pl.multiple_of(g * grp, grp), grp)

        def tile(n, carry):
            cols = pl.ds(pl.multiple_of(n * tf, tf), tf)
            ig[s, :, cols] = lax.dot_general(
                hidden[rows, :], w[cols, :], (((1,), (1,)), ((), ())), preferred_element_type=F32
            ).astype(BF16)
            return carry

        lax.fori_loop(0, feats // tf, tile, 0)

    def rs_start(src, row_of, in_m, in_p, to_p, to_m):
        blk = lambda by, start: src.at[pl.ds(pl.multiple_of(row_of(by) + start, hb), hb)]
        op = send(blk(2, 0), in_m.at[0], to_p)
        om = send(blk(2, hb), in_p.at[0], to_m)
        dp = send(blk(1, hb), in_m.at[1], to_p)
        dm = send(blk(3, 0), in_p.at[1], to_m)
        return src, row_of, blk, in_m, in_p, to_p, to_m, op, om, dp, dm

    def rs_middle(state):
        src, row_of, blk, in_m, in_p, to_p, to_m, op, om, dp, dm = state
        op.wait_recv()
        add_into(src, row_of(1), in_m.at[0], 0, hb)
        ap = send(blk(1, 0), in_m.at[2], to_p)
        om.wait_recv()
        add_into(src, row_of(3) + hb, in_p.at[0], 0, hb)
        am = send(blk(3, hb), in_p.at[2], to_m)
        return src, row_of, in_m, in_p, (dp, dm, ap, am)

    def rs_finish(state, out):
        src, row_of, in_m, in_p, copies = state
        for copy in copies:
            copy.wait_recv()
        for start, from_m, from_p in ((0, in_m.at[2], in_p.at[1]), (hb, in_m.at[1], in_p.at[2])):
            def tile(n, carry):
                cols = pl.ds(pl.multiple_of(n * tf, tf), tf)
                own = src[pl.ds(pl.multiple_of(row_of(0) + start, hb), hb), cols]
                total = own.astype(F32) + from_m[:, cols].astype(F32) + from_p[:, cols].astype(F32)
                out[start:start + hb, cols] = total.astype(BF16)
                return carry

            lax.fori_loop(0, feats // tf, tile, 0)

    y_rs = lambda s: rs_start(ig.at[s], lambda by: nxt(y, by) * tb, y_in_m.at[s], y_in_p.at[s], yp, ym)

    for s3 in own_sends:
        s3[0].wait_recv()
    dot2(0, z)
    y0 = y_rs(0)

    low, high = nxt(z, 3), nxt(z, 1)
    to_sib, fwd_p, fwd_m = [], [], []
    for n, start in enumerate(starts):
        own_sends[n][1].wait_recv()
        here = piece(base(low, k), start)
        if start < half:
            fwd_p.append(send(here, here, zp))
        to_sib.append(send(here, here, sib))
        own_sends[n][2].wait_recv()
        here = piece(base(high, k), start)
        if start >= half:
            fwd_m.append(send(here, here, zm))
        to_sib.append(send(here, here, sib))
    y0 = rs_middle(y0)
    for copy in to_sib:
        copy.wait_recv()
    dot2(1, low)
    y1 = y_rs(1)
    dot2(2, high)
    y2 = y_rs(2)
    rs_finish(y0, xs.at[z])
    y1 = rs_middle(y1)

    opp = nxt(z, 2)
    to_sib = []
    for j in range(2):
        fwd_p[j].wait_recv()
        here = piece(base(opp, k), j * quarter)
        to_sib.append(send(here, here, sib))
        fwd_m[j].wait_recv()
        here = piece(base(opp, k), half + j * quarter)
        to_sib.append(send(here, here, sib))
    y2 = rs_middle(y2)
    for copy in to_sib:
        copy.wait_recv()
    dot2(3, opp)
    y3 = y_rs(3)
    rs_finish(y1, xs.at[low])
    rs_finish(y2, xs.at[high])

    def dot3(m):
        rows = pl.ds(m * tm, tm)

        def tile(n, carry):
            cols = pl.ds(pl.multiple_of(n * tn, tn), tn)
            w[rows, cols] = jnp.dot(acts_t[rows, :], hidden[:, cols], preferred_element_type=F32).astype(BF16)
            return carry

        lax.fori_loop(0, hid // tn, tile, 0)
        out = pltpu.make_async_copy(w.at[rows], wg_ref.at[rows], local_sem.at[3 + m])
        out.start()
        return out

    blocks = feats // tm
    stores = []
    stages = [None] * blocks
    stores.append(dot3(0))
    y3 = rs_middle(y3)
    for m in range(1, min(3, blocks)):
        stores.append(dot3(m))
    rs_finish(y3, xs.at[opp])
    xr = rs_start(
        xs.reshape(4 * tb, feats), lambda by: nxt(x, by) * tb, x_in_m, x_in_p, xp, xm
    )
    for m in range(3, min(4, blocks)):
        stores.append(dot3(m))
    xr = rs_middle(xr)
    for m in range(4, blocks):
        stores.append(dot3(m))
    rs_finish(xr, ig_ref)

    for copy in sent:
        copy.wait_send()
    for out in stores:
        out.wait()


def per_device(acts, up_weight, out_grad):
    tb, feats = acts.shape
    ob, hid = out_grad.shape
    tokens = 16 * tb
    hb, half = tb // 2, ob // 2
    vmem = lambda *shape: pltpu.VMEM(shape, BF16)
    anywhere = pl.BlockSpec(memory_space=pl.ANY)
    flops = 3 * 2 * tokens * feats * hid
    input_grad, weight_grad = pl.pallas_call(
        kernel,
        out_shape=(
            jax.ShapeDtypeStruct((tb, feats), BF16),
            jax.ShapeDtypeStruct((feats, hid), BF16),
        ),
        in_specs=[anywhere] * 3,
        out_specs=(pl.BlockSpec(memory_space=pltpu.VMEM), anywhere),
        scratch_shapes=[
            vmem(tokens, feats),
            vmem(feats, hid),
            vmem(ob, hid),
            vmem(feats, tokens),
            vmem(4, 2 * ob, hid),
            vmem(4, ob, hid),
            vmem(3, half, hid),
            vmem(3, half, hid),
            vmem(tokens, hid),
            vmem(4, 4 * tb, feats),
            vmem(4, 3, hb, feats),
            vmem(4, 3, hb, feats),
            vmem(4, tb, feats),
            vmem(3, hb, feats),
            vmem(3, hb, feats),
            pltpu.SemaphoreType.DMA((16,)),
            pltpu.SemaphoreType.DMA((N_SEMS,)),
            pltpu.SemaphoreType.DMA((N_SEMS,)),
        ],
        compiler_params=pltpu.CompilerParams(
            collective_id=0, has_side_effects=True, vmem_limit_bytes=60 * 2**20
        ),
        cost_estimate=pl.CostEstimate(flops=flops, bytes_accessed=4 * feats * hid, transcendentals=2 * ob * hid),
    )(acts, up_weight, out_grad)
    return input_grad, weight_grad


def solution(mesh):
    in_specs = (P("col", "row"), P("row", "col"), P("row", "col"))
    out_specs = (P("col", "row"), P("row", "col"))
    return jax.shard_map(
        per_device, mesh=mesh, in_specs=in_specs, out_specs=out_specs, check_vma=False
    )
```

```python
import functools

import jax
import jax.numpy as jnp
from jax import lax
from jax.experimental import pallas as pl
from jax.experimental.pallas import tpu as pltpu
from jax.sharding import PartitionSpec as P

F32, BF16 = jnp.float32, jnp.bfloat16
MESH = pl.DeviceIdType.MESH
N_SEMS = 144


def gelu_slope(pre):
    cdf = 0.5 * (1.0 + lax.erf(pre * 0.7071067811865476))
    dens = jnp.exp(-0.5 * pre * pre) * 0.3989422804014327
    return cdf + pre * dens


def tile_of(size, want):
    return want if size % want == 0 else size


def kernel(
    acts_ref, w_ref, og_ref, ig_ref, wg_ref,
    acts, w, og, acts_t, part, sib_in, z_in_m, z_in_p, hidden, ig, y_in_m, y_in_p, xs, x_in,
    local_sem, send_sem, recv_sem,
):
    tb, feats = acts_ref.shape
    ob, hid = og_ref.shape
    half, quarter = ob // 2, ob // 4
    grp = 4 * tb
    tn = tile_of(hid // 2, 512)
    tf = tile_of(feats, 512)
    tm = tile_of(feats, 256)

    row, col = lax.axis_index("row"), lax.axis_index("col")
    z, k = lax.div(row, 2), lax.rem(row, 2)
    x, y = lax.div(col, 4), lax.rem(col, 4)
    nxt = lambda v, by: lax.rem(v + by, 4)
    sib = {"row": z * 2 + (1 - k)}
    zp, zm = {"row": nxt(z, 1) * 2 + k}, {"row": nxt(z, 3) * 2 + k}
    xp, xm = {"col": nxt(x, 1) * 4 + y}, {"col": nxt(x, 3) * 4 + y}
    yp, ym = {"col": x * 4 + nxt(y, 1)}, {"col": x * 4 + nxt(y, 3)}

    sent = []

    def ready(src, dst, to):
        i = len(sent)
        sent.append(None)
        return pltpu.make_async_remote_copy(
            src_ref=src, dst_ref=dst, send_sem=send_sem.at[i], recv_sem=recv_sem.at[i],
            device_id=to, device_id_type=MESH,
        )

    def send(src, dst, to):
        copy = ready(src, dst, to)
        copy.start()
        sent[-1] = copy
        return copy

    def at(ref, start, size):
        return ref.at[pl.ds(pl.multiple_of(start, size), size)]

    barrier = pltpu.get_barrier_semaphore()
    for to in (sib, zp, zm, xp, xm, yp, ym):
        pl.semaphore_signal(barrier, inc=1, device_id=to, device_id_type=MESH)
    own_acts = at(acts, (x * 4 + y) * tb, tb)
    load_acts = pltpu.make_async_copy(acts_ref, own_acts, local_sem.at[0])
    load_w = pltpu.make_async_copy(w_ref, w, local_sem.at[1])
    load_og = pltpu.make_async_copy(og_ref, og, local_sem.at[2])
    load_acts.start()
    load_w.start()
    load_og.start()
    load_acts.wait()
    pl.semaphore_wait(barrier, 7)

    hb = tb // 2

    def ag_start(block, to_p, to_m):
        a = lambda by: at(acts, block(by), hb)
        b = lambda by: at(acts, block(by) + hb, hb)
        pa = send(a(0), a(0), to_p)
        mb = send(b(0), b(0), to_m)
        pb = send(b(0), b(0), to_p)
        ma = send(a(0), a(0), to_m)
        return a, b, pa, mb, pb, ma, to_p, to_m

    def ag_forward(state):
        a, b, pa, mb, pb, ma, to_p, to_m = state
        pa.wait_recv()
        fa = send(a(3), a(3), to_p)
        mb.wait_recv()
        fb = send(b(1), b(1), to_m)
        return pb, ma, fa, fb

    def ag_finish(copies):
        for copy in copies:
            copy.wait_recv()

    ag_finish(ag_forward(ag_start(lambda by: (nxt(x, by) * 4 + y) * tb, xp, xm)))
    order = [nxt(z, 2), nxt(z, 1), nxt(z, 3), z]
    y_gather = lambda s: ag_start(lambda by: (order[s] * 4 + nxt(y, by)) * tb, yp, ym)

    def dot1(s, lo=0, hi=hid):
        rows = pl.ds(pl.multiple_of(order[s] * grp, grp), grp)
        theirs = part.at[s, pl.ds(pl.multiple_of((1 - k) * ob, ob), ob)]
        sem = len(sent)

        def to_sib(cols):
            return pltpu.make_async_remote_copy(
                src_ref=theirs.at[:, cols], dst_ref=sib_in.at[s, :, cols], send_sem=send_sem.at[sem],
                recv_sem=recv_sem.at[sem], device_id=sib, device_id_type=MESH,
            )

        def tile(n, carry):
            cols = pl.ds(pl.multiple_of(n * tn, tn), tn)
            part[s, :, cols] = jnp.dot(acts[rows, :], w[:, cols], preferred_element_type=F32).astype(BF16)
            to_sib(cols).start()
            return carry

        lax.fori_loop(lo // tn, hi // tn, tile, 0)
        sent.append(to_sib(pl.ds(lo, hi - lo)))
        return sent[-1]

    own_row = pl.multiple_of(k * ob, ob)

    def add_into(dst, dst_row, src, src_row, rows, lo=0, hi=hid):
        step = min(rows, 32)
        for r in range(0, rows, step):
            def tile(n, carry):
                cols = pl.ds(pl.multiple_of(n * tn, tn), tn)
                into = pl.ds(pl.multiple_of(dst_row + r, step), step)
                total = dst[into, cols].astype(F32) + src[src_row + r:src_row + r + step, cols].astype(F32)
                dst[into, cols] = total.astype(BF16)
                return carry

            lax.fori_loop(lo // tn, hi // tn, tile, 0)

    def core_sum(s, copy, lo=0, hi=hid):
        copy.wait_recv()
        add_into(part.at[s], own_row, sib_in.at[s], 0, ob, lo, hi)

    mine = lambda s, start, size: part.at[s, pl.ds(pl.multiple_of(own_row + start, size), size)]

    g = ag_forward(y_gather(0))
    nx = y_gather(1)
    load_w.wait()
    ag_finish(g)
    opp_p, opp_m = [], []
    for lo, hi in ((0, hid // 2), (hid // 2, hid)):
        c = dot1(0, lo, hi)
        if lo == 0:
            g = ag_forward(nx)
            nx = y_gather(2)
        core_sum(0, c, lo, hi)
        cols = pl.ds(lo, hi - lo)
        opp_p.append(send(mine(0, 0, half).at[:, cols], z_in_m.at[0, :, cols], zp))
        opp_m.append(send(mine(0, half, half).at[:, cols], z_in_p.at[0, :, cols], zm))
    ag_finish(g)
    c = dot1(1)
    g = ag_forward(nx)
    nx = y_gather(3)
    core_sum(1, c)
    dir_p = send(mine(1, half, half), z_in_m.at[1], zp)
    ag_finish(g)
    c = dot1(2)
    g = ag_forward(nx)
    core_sum(2, c)
    dir_m = send(mine(2, 0, half), z_in_p.at[1], zm)
    ag_finish(g)
    c = dot1(3)
    for copy in opp_p:
        copy.wait_recv()
    add_into(part.at[1], own_row, z_in_m.at[0], 0, half)
    acc_p = [send(mine(1, j * quarter, quarter), z_in_m.at[2, pl.ds(j * quarter, quarter)], zp) for j in range(2)]
    for copy in opp_m:
        copy.wait_recv()
    add_into(part.at[2], own_row + half, z_in_p.at[0], 0, half)
    acc_m = [send(mine(2, half + j * quarter, quarter), z_in_p.at[2, pl.ds(j * quarter, quarter)], zm) for j in range(2)]
    core_sum(3, c)
    load_og.wait()

    tokens_of = [
        (z, 0), (z, 1), (nxt(z, 3), 0), (nxt(z, 1), 0),
        (nxt(z, 3), 1), (nxt(z, 1), 1), (nxt(z, 2), 0), (nxt(z, 2), 1),
    ]

    def turn(n, carry):
        cols = pl.ds(pl.multiple_of(n * tm, tm), tm)
        for t, (g, j) in enumerate(tokens_of):
            rows = [at(acts, g * grp + b * tb + j * hb, hb)[:, cols] for b in range(4)]
            acts_t[cols, t * 4 * hb:(t + 1) * 4 * hb] = jnp.concatenate(rows, axis=0).T
        return carry

    lax.fori_loop(0, feats // tm, turn, 0)

    dir_p.wait_recv()
    dir_m.wait_recv()
    piece = lambda zz, kk, q: hidden.at[zz, 2 * kk + q // 2, q % 2]

    def slope_piece(q, from_m, from_p):
        start = q * quarter

        def tile(n, carry):
            cols = pl.ds(pl.multiple_of(n * tn, tn), tn)
            own = part[3, pl.ds(pl.multiple_of(own_row + start, quarter), quarter), cols]
            pre = own.astype(F32) + from_m[:, cols].astype(F32) + from_p[:, cols].astype(F32)
            grad = og[start:start + quarter, cols].astype(F32) * gelu_slope(pre)
            hidden[z, 2 * k + q // 2, q % 2, :, cols] = grad.astype(BF16)
            return carry

        lax.fori_loop(0, hid // tn, tile, 0)
        here = piece(z, k, q)
        return send(here, here, sib), send(here, here, zp), send(here, here, zm)

    arrivals = (0, 2, 1, 3)
    own_sends = {}
    for j in range(2):
        rows = pl.ds(j * quarter, quarter)
        acc_p[j].wait_recv()
        own_sends[j] = slope_piece(j, z_in_m.at[2, rows], z_in_p.at[1, rows])
        acc_m[j].wait_recv()
        own_sends[2 + j] = slope_piece(2 + j, z_in_m.at[1, rows], z_in_p.at[2, rows])

    low, high, opp = nxt(z, 3), nxt(z, 1), nxt(z, 2)

    def dot2(units):
        def tile(n, carry):
            cols = pl.ds(pl.multiple_of(n * tf, tf), tf)
            rows = [hidden[g, :, j].reshape(4 * hb, hid) for _, g, js in units for j in js]
            rows = rows[0] if len(rows) == 1 else jnp.concatenate(rows, axis=0)
            share = lax.dot_general(
                rows, w[cols, :], (((1,), (1,)), ((), ())), preferred_element_type=F32
            ).astype(BF16)
            at_row = 0
            for s, _, js in units:
                for j in js:
                    ig[s, j, :, :, cols] = share[at_row:at_row + 4 * hb].reshape(4, hb, tf)
                    at_row += 4 * hb
            return carry

        lax.fori_loop(0, feats // tf, tile, 0)

    def sum_into(out, terms):
        def tile(n, carry):
            cols = pl.ds(pl.multiple_of(n * tf, tf), tf)
            for p in range(out.shape[0]):
                for q in range(out.shape[1]):
                    total = terms[0][p, q, :, cols].astype(F32)
                    for term in terms[1:]:
                        total = total + term[p, q, :, cols].astype(F32)
                    out[p, q, :, cols] = total.astype(BF16)
            return carry

        lax.fori_loop(0, feats // tf, tile, 0)

    ha, hz = pl.ds(0, hb // 2), pl.ds(hb // 2, hb // 2)

    def y_start(s0, ns, j0, nj):
        ss, js = pl.ds(s0, ns), pl.ds(j0, nj)
        blk = lambda by, rows: ig.at[ss, js, nxt(y, by), rows]
        im = lambda n: y_in_m.at[n, ss, js]
        ip = lambda n: y_in_p.at[n, ss, js]
        op = send(blk(2, ha), im(0), yp)
        om = send(blk(2, hz), ip(0), ym)
        dp = send(blk(1, hz), im(1), yp)
        dm = send(blk(3, ha), ip(1), ym)
        return ss, js, blk, im, ip, op, om, dp, dm

    def y_middle(state):
        ss, js, blk, im, ip, op, om, dp, dm = state
        op.wait_recv()
        sum_into(blk(1, ha), [blk(1, ha), im(0)])
        ap = send(blk(1, ha), im(2), yp)
        om.wait_recv()
        sum_into(blk(3, hz), [blk(3, hz), ip(0)])
        am = send(blk(3, hz), ip(2), ym)
        return ss, js, blk, im, ip, (dp, dm, ap, am)

    def y_finish(state):
        ss, js, blk, im, ip, copies = state
        for copy in copies:
            copy.wait_recv()
        sum_into(xs.at[ss, js, ha], [blk(0, ha), im(2), ip(1)])
        sum_into(xs.at[ss, js, hz], [blk(0, hz), im(1), ip(2)])

    def x_copies(s, g, j0, nj):
        one, js = pl.ds(s, 1), pl.ds(j0, nj)
        mine_x = lambda rows: xs.at[one, js, rows]
        slot = lambda n: x_in.at[n, one, js]
        make = lambda rows, n, to: ready(mine_x(rows), slot(n), to)
        copies = (
            make(ha, 0, xp), make(hz, 1, xm), make(hz, 2, xp), make(ha, 3, xp), make(ha, 4, xm), make(hz, 5, xm)
        )
        return nxt(x, 4 - g), mine_x, slot, copies, (j0, nj)

    def x_start(s, g, j0, nj):
        state = x_copies(s, g, j0, nj)
        away, _, _, copies, _ = state

        @pl.when(away == 2)
        def _():
            copies[0].start()
            copies[1].start()

        @pl.when(away == 3)
        def _():
            copies[2].start()

        @pl.when(away == 1)
        def _():
            copies[4].start()

        return state

    def x_middle(state):
        away, mine_x, slot, copies, _ = state

        @pl.when(away == 3)
        def _():
            copies[0].wait_recv()
            sum_into(mine_x(ha), [mine_x(ha), slot(0)])
            copies[3].start()

        @pl.when(away == 1)
        def _():
            copies[1].wait_recv()
            sum_into(mine_x(hz), [mine_x(hz), slot(1)])
            copies[5].start()

    def x_finish(state):
        away, mine_x, slot, copies, (j0, nj) = state
        result = lambda rows: ig_ref.at[pl.ds(0, 1), pl.ds(j0, nj), rows]

        @pl.when(away == 0)
        def _():
            for n in (2, 3, 4, 5):
                copies[n].wait_recv()
            sum_into(result(ha), [mine_x(ha), slot(3), slot(4)])
            sum_into(result(hz), [mine_x(hz), slot(2), slot(5)])

        for role, used in ((2, (0, 1)), (3, (2, 3)), (1, (4, 5))):
            @pl.when(away == role)
            def _(used=used):
                for n in used:
                    copies[n].wait_send()

    def dot3(m, rows_of, first, later):
        rows = pl.ds(m * tm, tm)
        span = 8 * hb * 2

        def tile(n, carry):
            cols = pl.ds(pl.multiple_of(n * tn, tn), tn)
            units = jnp.concatenate([hidden[g, :, j, :, cols].reshape(4 * hb, tn) for g, j in rows_of], axis=0)
            total = jnp.dot(acts_t[rows, first:first + span], units, preferred_element_type=F32)
            if later:
                total = total + wg_ref[rows, cols].astype(F32)
            wg_ref[rows, cols] = total.astype(BF16)
            return carry

        lax.fori_loop(0, hid // tn, tile, 0)

    blocks = feats // tm

    def early(lo, hi):
        for m in range(lo, hi):
            dot3(m, tokens_of[:4], 0, False)

    def late(lo, hi):
        for m in range(lo, hi):
            dot3(m, tokens_of[4:], 8 * hb * 2, True)

    def neighbours(qs):
        copies = []
        for q in qs:
            own_sends[q][1].wait_recv()
            here = piece(low, k, q)
            if q < 2:
                fwd[q] = send(here, here, zp)
            copies.append(send(here, here, sib))
            own_sends[q][2].wait_recv()
            here = piece(high, k, q)
            if q >= 2:
                fwd[q] = send(here, here, zm)
            copies.append(send(here, here, sib))
        return copies

    def opposite(qs):
        copies = []
        for q in qs:
            fwd[q].wait_recv()
            here = piece(opp, k, q)
            copies.append(send(here, here, sib))
        return copies

    def arrived(copies):
        for copy in copies:
            copy.wait_recv()

    fwd = {}
    arrived([own_sends[q][0] for q in arrivals])
    dot2([(0, z, (0, 1))])
    y0 = y_start(0, 1, 0, 2)
    from_sib = neighbours((0, 2))
    y0 = y_middle(y0)
    arrived(from_sib)
    dot2([(1, low, (0,)), (2, high, (0,))])
    y1 = y_start(1, 2, 0, 1)
    y_finish(y0)
    x0 = x_start(0, z, 0, 2)
    early(0, 2)
    y1 = y_middle(y1)
    x_middle(x0)
    early(2, blocks)
    y_finish(y1)
    from_sib = neighbours((1, 3))
    x_finish(x0)
    arrived(from_sib)
    dot2([(1, low, (1,)), (2, high, (1,))])
    y2 = y_start(1, 2, 1, 1)
    from_sib = opposite((0, 2))
    y2 = y_middle(y2)
    arrived(from_sib)
    dot2([(3, opp, (0,))])
    y3 = y_start(3, 1, 0, 1)
    y_finish(y2)
    x1 = x_start(1, low, 0, 2)
    x2 = x_start(2, high, 0, 2)
    from_sib = opposite((1, 3))
    y3 = y_middle(y3)
    arrived(from_sib)
    dot2([(3, opp, (1,))])
    y4 = y_start(3, 1, 1, 1)
    x_middle(x1)
    x_middle(x2)
    y_finish(y3)
    x3 = x_start(3, opp, 0, 1)
    late(0, 1)
    y4 = y_middle(y4)
    x_middle(x3)
    late(1, 2)
    y_finish(y4)
    x4 = x_start(3, opp, 1, 1)
    late(2, 3)
    x_middle(x4)
    x_finish(x1)
    x_finish(x2)
    x_finish(x3)
    late(3, blocks)
    x_finish(x4)

    for copy in sent:
        if copy is not None:
            copy.wait_send()


def write_out(ig_ref, wg_ref, ig_out, wg_out, sem):
    rows = wg_ref.shape[0] // 4
    copies = [pltpu.make_async_copy(ig_ref, ig_out, sem.at[4])]
    for n in range(4):
        part = pl.ds(n * rows, rows)
        copies.append(pltpu.make_async_copy(wg_ref.at[part], wg_out.at[part], sem.at[n]))
    for copy in copies:
        copy.start()
    for copy in copies:
        copy.wait()


def per_device(acts, up_weight, out_grad):
    tb, feats = acts.shape
    ob, hid = out_grad.shape
    tokens = 16 * tb
    hb, half = tb // 2, ob // 2
    vmem = lambda *shape: pltpu.VMEM(shape, BF16)
    in_hbm = pl.BlockSpec(memory_space=pltpu.HBM)
    in_vmem = pl.BlockSpec(memory_space=pltpu.VMEM)
    flops = 3 * 2 * tokens * feats * hid
    acts, up_weight, out_grad = (
        pltpu.with_memory_space_constraint(a, pltpu.HBM) for a in (acts, up_weight, out_grad)
    )
    input_grad, weight_grad = pl.pallas_call(
        kernel,
        out_shape=(
            vmem(1, 2, hb, feats),
            vmem(feats, hid),
        ),
        in_specs=[in_hbm] * 3,
        out_specs=(in_vmem, in_vmem),
        scratch_shapes=[
            vmem(tokens, feats),
            vmem(feats, hid),
            vmem(ob, hid),
            vmem(feats, tokens),
            vmem(4, 2 * ob, hid),
            vmem(4, ob, hid),
            vmem(3, half, hid),
            vmem(3, half, hid),
            vmem(4, 4, 2, hb, hid),
            vmem(4, 2, 4, hb, feats),
            vmem(3, 4, 2, hb // 2, feats),
            vmem(3, 4, 2, hb // 2, feats),
            vmem(4, 2, hb, feats),
            vmem(6, 4, 2, hb // 2, feats),
            pltpu.SemaphoreType.DMA((3,)),
            pltpu.SemaphoreType.DMA((N_SEMS,)),
            pltpu.SemaphoreType.DMA((N_SEMS,)),
        ],
        compiler_params=pltpu.CompilerParams(
            collective_id=0, has_side_effects=True, vmem_limit_bytes=44 * 2**20
        ),
        cost_estimate=pl.CostEstimate(flops=flops, bytes_accessed=4 * feats * hid, transcendentals=2 * ob * hid),
    )(acts, up_weight, out_grad)
    return pl.pallas_call(
        write_out,
        out_shape=(
            jax.ShapeDtypeStruct((tb, feats), BF16),
            jax.ShapeDtypeStruct((feats, hid), BF16),
        ),
        in_specs=[in_vmem] * 2,
        out_specs=(in_hbm, in_hbm),
        scratch_shapes=[pltpu.SemaphoreType.DMA((5,))],
        compiler_params=pltpu.CompilerParams(vmem_limit_bytes=2 * 2**20),
        cost_estimate=pl.CostEstimate(flops=0, bytes_accessed=2 * feats * hid, transcendentals=0),
    )(input_grad.reshape(tb, feats), weight_grad)


def solution(mesh):
    in_specs = (P("col", "row"), P("row", "col"), P("row", "col"))
    out_specs = (P("col", "row"), P("row", "col"))
    return jax.shard_map(
        per_device, mesh=mesh, in_specs=in_specs, out_specs=out_specs, check_vma=False
    )
```

```python
import functools

import jax
import jax.numpy as jnp
from jax import lax
from jax.experimental import pallas as pl
from jax.experimental.pallas import tpu as pltpu
from jax.sharding import PartitionSpec as P

F32, BF16 = jnp.float32, jnp.bfloat16
MESH = pl.DeviceIdType.MESH
N_SEMS = 144


def gelu_slope(pre):
    cdf = 0.5 * (1.0 + lax.erf(pre * 0.7071067811865476))
    dens = jnp.exp(-0.5 * pre * pre) * 0.3989422804014327
    return cdf + pre * dens


def tile_of(size, want):
    return want if size % want == 0 else size


def kernel(
    acts_ref, w_ref, og_ref, ig_ref, wg_ref,
    acts, w_t, og, acts_t, part, sib_in, z_in_m, z_in_p, hidden, ig, y_in_m, y_in_p, xs, x_in,
    local_sem, send_sem, recv_sem,
):
    tb, feats = acts_ref.shape
    ob, hid = og_ref.shape
    half, quarter = ob // 2, ob // 4
    grp = 4 * tb
    tv, tn, t3 = tile_of(hid // 2, 512), tile_of(hid // 2, 768), tile_of(hid, 1536)
    tf, tm = tile_of(feats, 768), tile_of(feats, 256)
    w = wg_ref

    row, col = lax.axis_index("row"), lax.axis_index("col")
    z, k = lax.div(row, 2), lax.rem(row, 2)
    x, y = lax.div(col, 4), lax.rem(col, 4)
    nxt = lambda v, by: lax.rem(v + by, 4)
    sib = {"row": z * 2 + (1 - k)}
    zp, zm = {"row": nxt(z, 1) * 2 + k}, {"row": nxt(z, 3) * 2 + k}
    xp, xm = {"col": nxt(x, 1) * 4 + y}, {"col": nxt(x, 3) * 4 + y}
    yp, ym = {"col": x * 4 + nxt(y, 1)}, {"col": x * 4 + nxt(y, 3)}

    sent = []

    def ready(src, dst, to):
        i = len(sent)
        sent.append(None)
        return pltpu.make_async_remote_copy(
            src_ref=src, dst_ref=dst, send_sem=send_sem.at[i], recv_sem=recv_sem.at[i],
            device_id=to, device_id_type=MESH,
        )

    def send(src, dst, to):
        copy = ready(src, dst, to)
        copy.start()
        sent[-1] = copy
        return copy

    def at(ref, start, size):
        return ref.at[pl.ds(pl.multiple_of(start, size), size)]

    barrier = pltpu.get_barrier_semaphore()
    for to in (sib, zp, zm, xp, xm, yp, ym):
        pl.semaphore_signal(barrier, inc=1, device_id=to, device_id_type=MESH)
    own_acts = at(acts, (x * 4 + y) * tb, tb)
    load_acts = pltpu.make_async_copy(acts_ref, own_acts, local_sem.at[0])
    load_og = pltpu.make_async_copy(og_ref, og, local_sem.at[1])
    load_w = [
        pltpu.make_async_copy(w_ref.at[pl.ds(m * tm, tm)], w.at[pl.ds(m * tm, tm)], local_sem.at[2 + m])
        for m in range(feats // tm)
    ]
    load_acts.start()
    for load in load_w:
        load.start()
    load_og.start()
    load_acts.wait()
    pl.semaphore_wait(barrier, 7)

    hb = tb // 2

    def ag_start(block, to_p, to_m):
        a = lambda by: at(acts, block(by), hb)
        b = lambda by: at(acts, block(by) + hb, hb)
        pa = send(a(0), a(0), to_p)
        mb = send(b(0), b(0), to_m)
        pb = send(b(0), b(0), to_p)
        ma = send(a(0), a(0), to_m)
        return a, b, pa, mb, pb, ma, to_p, to_m

    def ag_forward(state):
        a, b, pa, mb, pb, ma, to_p, to_m = state
        pa.wait_recv()
        fa = send(a(3), a(3), to_p)
        mb.wait_recv()
        fb = send(b(1), b(1), to_m)
        return pb, ma, fa, fb

    def ag_finish(copies):
        for copy in copies:
            copy.wait_recv()

    def turn_w(m, loaded=False):
        if not loaded:
            load_w[m].wait()

        def tile(n, carry):
            cols = pl.ds(pl.multiple_of(n * tm, tm), tm)
            w_t[cols, m * tm:(m + 1) * tm] = w[m * tm:(m + 1) * tm, cols].T
            return carry

        lax.fori_loop(0, hid // tm, tile, 0)

    g = ag_start(lambda by: (nxt(x, by) * 4 + y) * tb, xp, xm)
    turn_w(0)
    g = ag_forward(g)
    turn_w(1)
    ag_finish(g)
    order = [nxt(z, 2), nxt(z, 1), nxt(z, 3), z]
    y_gather = lambda s: ag_start(lambda by: (order[s] * 4 + nxt(y, by)) * tb, yp, ym)

    def dot1(s, lo=0, hi=hid):
        rows = pl.ds(pl.multiple_of(order[s] * grp, grp), grp)
        theirs = part.at[s, pl.ds(pl.multiple_of((1 - k) * ob, ob), ob)]
        sem = len(sent)

        def to_sib(cols):
            return pltpu.make_async_remote_copy(
                src_ref=theirs.at[:, cols], dst_ref=sib_in.at[s, :, cols], send_sem=send_sem.at[sem],
                recv_sem=recv_sem.at[sem], device_id=sib, device_id_type=MESH,
            )

        def tile(n, carry):
            cols = pl.ds(pl.multiple_of(n * tn, tn), tn)
            part[s, :, cols] = jnp.dot(acts[rows, :], w[:, cols], preferred_element_type=F32).astype(BF16)
            to_sib(cols).start()
            return carry

        lax.fori_loop(lo // tn, hi // tn, tile, 0)
        sent.append(to_sib(pl.ds(lo, hi - lo)))
        return sent[-1]

    own_row = pl.multiple_of(k * ob, ob)

    def add_into(dst, dst_row, src, src_row, rows, lo=0, hi=hid):
        step = min(rows, 32)
        for r in range(0, rows, step):
            def tile(n, carry):
                cols = pl.ds(pl.multiple_of(n * tv, tv), tv)
                into = pl.ds(pl.multiple_of(dst_row + r, step), step)
                total = dst[into, cols].astype(F32) + src[src_row + r:src_row + r + step, cols].astype(F32)
                dst[into, cols] = total.astype(BF16)
                return carry

            lax.fori_loop(lo // tv, hi // tv, tile, 0)

    def core_sum(s, copy, lo=0, hi=hid):
        copy.wait_recv()
        add_into(part.at[s], own_row, sib_in.at[s], 0, ob, lo, hi)

    mine = lambda s, start, size: part.at[s, pl.ds(pl.multiple_of(own_row + start, size), size)]

    g = y_gather(0)
    turn_w(2)
    g = ag_forward(g)
    nx = y_gather(1)
    turn_w(3)
    for load in load_w[4:]:
        load.wait()
    ag_finish(g)
    opp_p, opp_m = [], []
    for lo, hi in ((0, hid // 2), (hid // 2, hid)):
        c = dot1(0, lo, hi)
        if lo == 0:
            g = ag_forward(nx)
            nx = y_gather(2)
        core_sum(0, c, lo, hi)
        cols = pl.ds(lo, hi - lo)
        opp_p.append(send(mine(0, 0, half).at[:, cols], z_in_m.at[0, :, cols], zp))
        opp_m.append(send(mine(0, half, half).at[:, cols], z_in_p.at[0, :, cols], zm))
    ag_finish(g)
    c = dot1(1)
    g = ag_forward(nx)
    nx = y_gather(3)
    core_sum(1, c)
    dir_p = send(mine(1, half, half), z_in_m.at[1], zp)
    ag_finish(g)
    c = dot1(2)
    g = ag_forward(nx)
    core_sum(2, c)
    dir_m = send(mine(2, 0, half), z_in_p.at[1], zm)
    ag_finish(g)
    c = dot1(3)
    for copy in opp_p:
        copy.wait_recv()
    add_into(part.at[1], own_row, z_in_m.at[0], 0, half)
    acc_p = [send(mine(1, j * quarter, quarter), z_in_m.at[2, pl.ds(j * quarter, quarter)], zp) for j in range(2)]
    for copy in opp_m:
        copy.wait_recv()
    add_into(part.at[2], own_row + half, z_in_p.at[0], 0, half)
    acc_m = [send(mine(2, half + j * quarter, quarter), z_in_p.at[2, pl.ds(j * quarter, quarter)], zm) for j in range(2)]
    core_sum(3, c)
    load_og.wait()

    tokens_of = [
        (z, 0), (z, 1), (nxt(z, 3), 0), (nxt(z, 1), 0),
        (nxt(z, 3), 1), (nxt(z, 1), 1), (nxt(z, 2), 0), (nxt(z, 2), 1),
    ]

    def turn(n, carry):
        cols = pl.ds(pl.multiple_of(n * tm, tm), tm)
        for t, (g, j) in enumerate(tokens_of):
            rows = [at(acts, g * grp + b * tb + j * hb, hb)[:, cols] for b in range(4)]
            acts_t[cols, t * 4 * hb:(t + 1) * 4 * hb] = jnp.concatenate(rows, axis=0).T
        return carry

    lax.fori_loop(0, feats // tm, turn, 0)
    for m in range(4, feats // tm):
        turn_w(m, True)

    dir_p.wait_recv()
    dir_m.wait_recv()
    piece = lambda zz, kk, q: hidden.at[zz, 2 * kk + q // 2, q % 2]

    def slope_piece(q, from_m, from_p):
        start = q * quarter

        def tile(n, carry):
            cols = pl.ds(pl.multiple_of(n * tv, tv), tv)
            own = part[3, pl.ds(pl.multiple_of(own_row + start, quarter), quarter), cols]
            pre = own.astype(F32) + from_m[:, cols].astype(F32) + from_p[:, cols].astype(F32)
            grad = og[start:start + quarter, cols].astype(F32) * gelu_slope(pre)
            hidden[z, 2 * k + q // 2, q % 2, :, cols] = grad.astype(BF16)
            return carry

        lax.fori_loop(0, hid // tv, tile, 0)
        here = piece(z, k, q)
        return send(here, here, sib), send(here, here, zp), send(here, here, zm)

    arrivals = (0, 2, 1, 3)
    own_sends = {}
    for j in range(2):
        rows = pl.ds(j * quarter, quarter)
        acc_p[j].wait_recv()
        own_sends[j] = slope_piece(j, z_in_m.at[2, rows], z_in_p.at[1, rows])
        acc_m[j].wait_recv()
        own_sends[2 + j] = slope_piece(2 + j, z_in_m.at[1, rows], z_in_p.at[2, rows])

    low, high, opp = nxt(z, 3), nxt(z, 1), nxt(z, 2)

    def dot2(units):
        def tile(n, carry):
            cols = pl.ds(pl.multiple_of(n * tf, tf), tf)
            rows = [hidden[g, :, j].reshape(4 * hb, hid) for _, g, js in units for j in js]
            rows = rows[0] if len(rows) == 1 else jnp.concatenate(rows, axis=0)
            share = jnp.dot(rows, w_t[:, cols], preferred_element_type=F32).astype(BF16)
            at_row = 0
            for s, _, js in units:
                for j in js:
                    ig[s, j, :, :, cols] = share[at_row:at_row + 4 * hb].reshape(4, hb, tf)
                    at_row += 4 * hb
            return carry

        lax.fori_loop(0, feats // tf, tile, 0)

    def sum_into(out, terms):
        def tile(n, carry):
            cols = pl.ds(pl.multiple_of(n * tv, tv), tv)
            for p in range(out.shape[0]):
                for q in range(out.shape[1]):
                    total = terms[0][p, q, :, cols].astype(F32)
                    for term in terms[1:]:
                        total = total + term[p, q, :, cols].astype(F32)
                    out[p, q, :, cols] = total.astype(BF16)
            return carry

        lax.fori_loop(0, feats // tv, tile, 0)

    ha, hz = pl.ds(0, hb // 2), pl.ds(hb // 2, hb // 2)

    def y_start(s0, ns, j0, nj):
        ss, js = pl.ds(s0, ns), pl.ds(j0, nj)
        blk = lambda by, rows: ig.at[ss, js, nxt(y, by), rows]
        im = lambda n: y_in_m.at[n, ss, js]
        ip = lambda n: y_in_p.at[n, ss, js]
        op = send(blk(2, ha), im(0), yp)
        om = send(blk(2, hz), ip(0), ym)
        dp = send(blk(1, hz), im(1), yp)
        dm = send(blk(3, ha), ip(1), ym)
        return ss, js, blk, im, ip, op, om, dp, dm

    def y_middle(state):
        ss, js, blk, im, ip, op, om, dp, dm = state
        op.wait_recv()
        sum_into(blk(1, ha), [blk(1, ha), im(0)])
        ap = send(blk(1, ha), im(2), yp)
        om.wait_recv()
        sum_into(blk(3, hz), [blk(3, hz), ip(0)])
        am = send(blk(3, hz), ip(2), ym)
        return ss, js, blk, im, ip, (dp, dm, ap, am)

    def y_finish(state):
        ss, js, blk, im, ip, copies = state
        for copy in copies:
            copy.wait_recv()
        sum_into(xs.at[ss, js, ha], [blk(0, ha), im(2), ip(1)])
        sum_into(xs.at[ss, js, hz], [blk(0, hz), im(1), ip(2)])

    def x_copies(s, g, j0, nj):
        one, js = pl.ds(s, 1), pl.ds(j0, nj)
        mine_x = lambda rows: xs.at[one, js, rows]
        slot = lambda n: x_in.at[n, one, js]
        make = lambda rows, n, to: ready(mine_x(rows), slot(n), to)
        copies = (
            make(ha, 0, xp), make(hz, 0, xm), make(hz, 0, xp), make(ha, 1, xp), make(ha, 2, xm), make(hz, 3, xm)
        )
        return nxt(x, 4 - g), mine_x, slot, copies, (j0, nj)

    def x_start(s, g, j0, nj):
        state = x_copies(s, g, j0, nj)
        away, _, _, copies, _ = state

        @pl.when(away == 2)
        def _():
            copies[0].start()
            copies[1].start()

        @pl.when(away == 3)
        def _():
            copies[2].start()

        @pl.when(away == 1)
        def _():
            copies[4].start()

        return state

    def x_middle(state):
        away, mine_x, slot, copies, _ = state

        @pl.when(away == 3)
        def _():
            copies[0].wait_recv()
            sum_into(mine_x(ha), [mine_x(ha), slot(0)])
            copies[3].start()

        @pl.when(away == 1)
        def _():
            copies[1].wait_recv()
            sum_into(mine_x(hz), [mine_x(hz), slot(0)])
            copies[5].start()

    def x_finish(state):
        away, mine_x, slot, copies, (j0, nj) = state
        result = lambda rows: ig_ref.at[pl.ds(0, 1), pl.ds(j0, nj), rows]

        @pl.when(away == 0)
        def _():
            for n in (2, 3, 4, 5):
                copies[n].wait_recv()
            sum_into(result(ha), [mine_x(ha), slot(1), slot(2)])
            sum_into(result(hz), [mine_x(hz), slot(0), slot(3)])

        for role, used in ((2, (0, 1)), (3, (2, 3)), (1, (4, 5))):
            @pl.when(away == role)
            def _(used=used):
                for n in used:
                    copies[n].wait_send()

    def dot3(m, rows_of, first, later):
        rows = pl.ds(m * tm, tm)
        span = 8 * hb * 2

        def tile(n, carry):
            cols = pl.ds(pl.multiple_of(n * t3, t3), t3)
            units = jnp.concatenate([hidden[g, :, j, :, cols].reshape(4 * hb, t3) for g, j in rows_of], axis=0)
            total = jnp.dot(acts_t[rows, first:first + span], units, preferred_element_type=F32)
            if later:
                total = total + wg_ref[rows, cols].astype(F32)
            wg_ref[rows, cols] = total.astype(BF16)
            return carry

        lax.fori_loop(0, hid // t3, tile, 0)

    blocks = feats // tm

    def early(lo, hi):
        for m in range(lo, hi):
            dot3(m, tokens_of[:4], 0, False)

    def late(lo, hi):
        for m in range(lo, hi):
            dot3(m, tokens_of[4:], 8 * hb * 2, True)

    def neighbours(qs):
        copies = []
        for q in qs:
            own_sends[q][1].wait_recv()
            here = piece(low, k, q)
            if q < 2:
                fwd[q] = send(here, here, zp)
            copies.append(send(here, here, sib))
            own_sends[q][2].wait_recv()
            here = piece(high, k, q)
            if q >= 2:
                fwd[q] = send(here, here, zm)
            copies.append(send(here, here, sib))
        return copies

    def opposite(qs):
        copies = []
        for q in qs:
            fwd[q].wait_recv()
            here = piece(opp, k, q)
            copies.append(send(here, here, sib))
        return copies

    def arrived(copies):
        for copy in copies:
            copy.wait_recv()

    fwd = {}
    arrived([own_sends[q][0] for q in arrivals])
    dot2([(0, z, (0, 1))])
    y0 = y_start(0, 1, 0, 2)
    from_sib = neighbours((0, 2))
    y0 = y_middle(y0)
    arrived(from_sib)
    dot2([(1, low, (0,)), (2, high, (0,))])
    y1 = y_start(1, 2, 0, 1)
    y_finish(y0)
    x0 = x_start(0, z, 0, 2)
    early(0, 2)
    y1 = y_middle(y1)
    x_middle(x0)
    early(2, blocks)
    y_finish(y1)
    from_sib = neighbours((1, 3))
    x_finish(x0)
    arrived(from_sib)
    dot2([(1, low, (1,)), (2, high, (1,))])
    y2 = y_start(1, 2, 1, 1)
    from_sib = opposite((0, 2))
    y2 = y_middle(y2)
    arrived(from_sib)
    dot2([(3, opp, (0,))])
    y3 = y_start(3, 1, 0, 1)
    y_finish(y2)
    x1 = x_start(1, low, 0, 2)
    x2 = x_start(2, high, 0, 2)
    from_sib = opposite((1, 3))
    y3 = y_middle(y3)
    arrived(from_sib)
    dot2([(3, opp, (1,))])
    y4 = y_start(3, 1, 1, 1)
    x_middle(x1)
    x_middle(x2)
    y_finish(y3)
    x3 = x_start(3, opp, 0, 1)
    late(0, 1)
    y4 = y_middle(y4)
    x_middle(x3)
    late(1, 2)
    y_finish(y4)
    x4 = x_start(3, opp, 1, 1)
    late(2, 3)
    x_middle(x4)
    x_finish(x1)
    x_finish(x2)
    x_finish(x3)
    late(3, blocks)
    x_finish(x4)

    for copy in sent:
        if copy is not None:
            copy.wait_send()


def write_out(ig_ref, wg_ref, ig_out, wg_out, sem):
    rows = wg_ref.shape[0] // 4
    copies = [pltpu.make_async_copy(ig_ref, ig_out, sem.at[4])]
    for n in range(4):
        part = pl.ds(n * rows, rows)
        copies.append(pltpu.make_async_copy(wg_ref.at[part], wg_out.at[part], sem.at[n]))
    for copy in copies:
        copy.start()
    for copy in copies:
        copy.wait()


def per_device(acts, up_weight, out_grad):
    tb, feats = acts.shape
    ob, hid = out_grad.shape
    tokens = 16 * tb
    hb, half = tb // 2, ob // 2
    vmem = lambda *shape: pltpu.VMEM(shape, BF16)
    in_hbm = pl.BlockSpec(memory_space=pltpu.HBM)
    in_vmem = pl.BlockSpec(memory_space=pltpu.VMEM)
    flops = 3 * 2 * tokens * feats * hid
    acts, up_weight, out_grad = (
        pltpu.with_memory_space_constraint(a, pltpu.HBM) for a in (acts, up_weight, out_grad)
    )
    input_grad, weight_grad = pl.pallas_call(
        kernel,
        out_shape=(
            vmem(1, 2, hb, feats),
            vmem(feats, hid),
        ),
        in_specs=[in_hbm] * 3,
        out_specs=(in_vmem, in_vmem),
        scratch_shapes=[
            vmem(tokens, feats),
            vmem(hid, feats),
            vmem(ob, hid),
            vmem(feats, tokens),
            vmem(4, 2 * ob, hid),
            vmem(4, ob, hid),
            vmem(3, half, hid),
            vmem(3, half, hid),
            vmem(4, 4, 2, hb, hid),
            vmem(4, 2, 4, hb, feats),
            vmem(3, 4, 2, hb // 2, feats),
            vmem(3, 4, 2, hb // 2, feats),
            vmem(4, 2, hb, feats),
            vmem(4, 4, 2, hb // 2, feats),
            pltpu.SemaphoreType.DMA((8,)),
            pltpu.SemaphoreType.DMA((N_SEMS,)),
            pltpu.SemaphoreType.DMA((N_SEMS,)),
        ],
        compiler_params=pltpu.CompilerParams(
            collective_id=0, has_side_effects=True, vmem_limit_bytes=50 * 2**20
        ),
        cost_estimate=pl.CostEstimate(flops=flops, bytes_accessed=4 * feats * hid, transcendentals=2 * ob * hid),
    )(acts, up_weight, out_grad)
    return pl.pallas_call(
        write_out,
        out_shape=(
            jax.ShapeDtypeStruct((tb, feats), BF16),
            jax.ShapeDtypeStruct((feats, hid), BF16),
        ),
        in_specs=[in_vmem] * 2,
        out_specs=(in_hbm, in_hbm),
        scratch_shapes=[pltpu.SemaphoreType.DMA((5,))],
        compiler_params=pltpu.CompilerParams(vmem_limit_bytes=2 * 2**20),
        cost_estimate=pl.CostEstimate(flops=0, bytes_accessed=2 * feats * hid, transcendentals=0),
    )(input_grad.reshape(tb, feats), weight_grad)


def solution(mesh):
    in_specs = (P("col", "row"), P("row", "col"), P("row", "col"))
    out_specs = (P("col", "row"), P("row", "col"))
    return jax.shard_map(
        per_device, mesh=mesh, in_specs=in_specs, out_specs=out_specs, check_vma=False
    )
```

```python
import functools

import jax
import jax.numpy as jnp
from jax import lax
from jax.experimental import pallas as pl
from jax.experimental.pallas import tpu as pltpu
from jax.sharding import PartitionSpec as P

F32, BF16 = jnp.float32, jnp.bfloat16
MESH = pl.DeviceIdType.MESH
N_SEMS = 160


def gelu_slope(pre):
    cdf = 0.5 * (1.0 + lax.erf(pre * 0.7071067811865476))
    dens = jnp.exp(-0.5 * pre * pre) * 0.3989422804014327
    return cdf + pre * dens


def tile_of(size, want):
    return want if size % want == 0 else size


def kernel(
    acts_ref, w_ref, og_ref, ig_ref, wg_ref,
    acts, w_t, og, acts_t, part, sib_in, z_in_m, z_in_p, hidden, ig, y_in_m, y_in_p, xs, x_in,
    local_sem, send_sem, recv_sem,
):
    tb, feats = acts_ref.shape
    ob, hid = og_ref.shape
    quarter = ob // 4
    tv, tn, t3 = tile_of(hid // 2, 512), tile_of(hid // 2, 768), tile_of(hid, 1536)
    tf, tm = tile_of(feats, 768), tile_of(feats, 256)
    w = wg_ref

    row, col = lax.axis_index("row"), lax.axis_index("col")
    z, k = lax.div(row, 2), lax.rem(row, 2)
    x, y = lax.div(col, 4), lax.rem(col, 4)
    nxt = lambda v, by: lax.rem(v + by, 4)
    sib = {"row": z * 2 + (1 - k)}
    zp, zm = {"row": nxt(z, 1) * 2 + k}, {"row": nxt(z, 3) * 2 + k}
    xp, xm = {"col": nxt(x, 1) * 4 + y}, {"col": nxt(x, 3) * 4 + y}
    yp, ym = {"col": x * 4 + nxt(y, 1)}, {"col": x * 4 + nxt(y, 3)}

    sent = []

    def ready(src, dst, to):
        i = len(sent)
        sent.append(None)
        return pltpu.make_async_remote_copy(
            src_ref=src, dst_ref=dst, send_sem=send_sem.at[i], recv_sem=recv_sem.at[i],
            device_id=to, device_id_type=MESH,
        )

    def send(src, dst, to):
        copy = ready(src, dst, to)
        copy.start()
        sent[-1] = copy
        return copy

    hb = tb // 2

    def step_of(group):
        away = nxt(group, 4 - z)
        odd, far = lax.rem(away, 2), lax.div(away, 2)
        return odd * (2 - lax.rem(far + y, 2)) + (1 - odd) * (3 - 3 * far)

    barrier = pltpu.get_barrier_semaphore()
    for to in (sib, zp, zm, xp, xm, yp, ym):
        pl.semaphore_signal(barrier, inc=1, device_id=to, device_id_type=MESH)
    load_acts = [
        pltpu.make_async_copy(acts_ref.at[pl.ds(j * hb, hb)], acts.at[step_of(x), y, j], local_sem.at[j])
        for j in range(2)
    ]
    load_og = pltpu.make_async_copy(og_ref, og, local_sem.at[2])
    load_w = [
        pltpu.make_async_copy(w_ref.at[pl.ds(m * tm, tm)], w.at[pl.ds(m * tm, tm)], local_sem.at[3 + m])
        for m in range(feats // tm)
    ]
    for load in (*load_acts, *load_w, load_og):
        load.start()
    for load in load_acts:
        load.wait()
    pl.semaphore_wait(barrier, 7)

    low16, high16 = pl.ds(0, hb // 2), pl.ds(hb // 2, hb // 2)

    def ag_start(block, to_p, to_m):
        a = lambda by: block(by, low16)
        b = lambda by: block(by, high16)
        pa = send(a(0), a(0), to_p)
        mb = send(b(0), b(0), to_m)
        pb = send(b(0), b(0), to_p)
        ma = send(a(0), a(0), to_m)
        return a, b, pa, mb, pb, ma, to_p, to_m

    def ag_forward(state):
        a, b, pa, mb, pb, ma, to_p, to_m = state
        pa.wait_recv()
        fa = send(a(3), a(3), to_p)
        mb.wait_recv()
        fb = send(b(1), b(1), to_m)
        return pb, ma, fa, fb

    def ag_finish(copies):
        for copy in copies:
            copy.wait_recv()

    def x_gather(j):
        return ag_start(lambda by, rows: acts.at[step_of(nxt(x, by)), y, j, rows], xp, xm)

    def y_gather(s, j0, nj):
        return ag_start(lambda by, rows: acts.at[s, nxt(y, by), pl.ds(j0, nj), rows], yp, ym)

    def turn_w(m, loaded=False):
        if not loaded:
            load_w[m].wait()

        def tile(n, carry):
            cols = pl.ds(pl.multiple_of(n * tm, tm), tm)
            w_t[cols, m * tm:(m + 1) * tm] = w[m * tm:(m + 1) * tm, cols].T
            return carry

        lax.fori_loop(0, hid // tm, tile, 0)

    def dot1(s, j0, nj):
        js = pl.ds(j0, nj)
        sem = len(sent)

        def to_sib(cols):
            return pltpu.make_async_remote_copy(
                src_ref=part.at[s, pl.ds(2 * (1 - k), 2), js, :, cols], dst_ref=sib_in.at[s, :, js, :, cols],
                send_sem=send_sem.at[sem], recv_sem=recv_sem.at[sem], device_id=sib, device_id_type=MESH,
            )

        def tile(n, carry):
            cols = pl.ds(pl.multiple_of(n * tn, tn), tn)
            share = jnp.dot(
                acts[s, :, js].reshape(4 * nj * hb, feats), w[:, cols], preferred_element_type=F32
            )
            part[s, :, js, :, cols] = share.astype(BF16).reshape(4, nj, hb, tn)
            to_sib(cols).start()
            return carry

        lax.fori_loop(0, hid // tn, tile, 0)
        sent.append(to_sib(pl.ds(0, hid)))
        return sent[-1]

    def add_into(dst, src):
        def tile(n, carry):
            cols = pl.ds(pl.multiple_of(n * tv, tv), tv)
            for j in range(dst.shape[0]):
                total = dst[j, :, cols].astype(F32) + src[j, :, cols].astype(F32)
                dst[j, :, cols] = total.astype(BF16)
            return carry

        lax.fori_loop(0, hid // tv, tile, 0)

    def core_sum(s, copy, j0, nj):
        copy.wait_recv()
        js = pl.ds(j0, nj)
        for way in range(2):
            add_into(part.at[s, 2 * k + way, js], sib_in.at[s, way, js])

    mine = lambda s, way: part.at[s, 2 * k + way]
    gx = x_gather(0)
    turn_w(0)
    gx0 = ag_forward(gx)
    gx = x_gather(1)
    ag_finish(gx0)
    g = y_gather(0, 0, 1)
    turn_w(1)
    gx1 = ag_forward(gx)
    g0 = ag_forward(g)
    ag_finish(gx1)
    g = y_gather(0, 1, 1)
    for load in load_w[2:]:
        load.wait()
    ag_finish(g0)
    opp_p, opp_m = [], []
    c = dot1(0, 0, 1)
    g0 = ag_forward(g)
    g = y_gather(1, 0, 2)
    core_sum(0, c, 0, 1)
    opp_p.append(send(mine(0, 0).at[0], z_in_m.at[0, 0], zp))
    opp_m.append(send(mine(0, 1).at[0], z_in_p.at[0, 0], zm))
    ag_finish(g0)
    c = dot1(0, 1, 1)
    g0 = ag_forward(g)
    g = y_gather(2, 0, 2)
    core_sum(0, c, 1, 1)
    opp_p.append(send(mine(0, 0).at[1], z_in_m.at[0, 1], zp))
    opp_m.append(send(mine(0, 1).at[1], z_in_p.at[0, 1], zm))
    turn_w(2, True)
    ag_finish(g0)
    c = dot1(1, 0, 2)
    g0 = ag_forward(g)
    g = y_gather(3, 0, 2)
    core_sum(1, c, 0, 2)
    dir_p = send(mine(1, 1), z_in_m.at[1], zp)
    dir_m = send(mine(1, 0), z_in_p.at[1], zm)
    turn_w(3, True)
    ag_finish(g0)
    c = dot1(2, 0, 2)
    g0 = ag_forward(g)
    core_sum(2, c, 0, 2)
    acc_p, acc_m = [], []
    for j in range(2):
        one = pl.ds(j, 1)
        opp_p[j].wait_recv()
        add_into(mine(2, 0).at[one], z_in_m.at[0, one])
        acc_p.append(send(mine(2, 0).at[j], z_in_m.at[2, j], zp))
        opp_m[j].wait_recv()
        add_into(mine(2, 1).at[one], z_in_p.at[0, one])
        acc_m.append(send(mine(2, 1).at[j], z_in_p.at[2, j], zm))
    ag_finish(g0)
    c = dot1(3, 0, 2)
    core_sum(3, c, 0, 2)
    load_og.wait()

    low, high, opp = nxt(z, 3), nxt(z, 1), nxt(z, 2)
    tokens_of = [(z, 0), (z, 1), (low, 0), (high, 0), (low, 1), (high, 1), (opp, 0), (opp, 1)]
    held_in = [(3, 3), (3, 3), (1, 2), (2, 1), (1, 2), (2, 1), (0, 0), (0, 0)]

    def turn(n, carry):
        cols = pl.ds(pl.multiple_of(n * tm, tm), tm)
        for t, steps in enumerate(held_in):
            rows = [acts[steps[b % 2], b, tokens_of[t][1], :, cols] for b in range(4)]
            acts_t[cols, t * 4 * hb:(t + 1) * 4 * hb] = jnp.concatenate(rows, axis=0).T
        return carry

    lax.fori_loop(0, feats // tm, turn, 0)
    for m in range(4, feats // tm):
        turn_w(m, True)

    dir_p.wait_recv()
    dir_m.wait_recv()
    piece = lambda zz, kk, q: hidden.at[zz, 2 * kk + q // 2, q % 2]

    def slope_piece(q, from_m, from_p):
        start = q * quarter

        def tile(n, carry):
            cols = pl.ds(pl.multiple_of(n * tv, tv), tv)
            own = part[3, 2 * k + q // 2, q % 2, :, cols]
            pre = own.astype(F32) + from_m[:, cols].astype(F32) + from_p[:, cols].astype(F32)
            grad = og[start:start + quarter, cols].astype(F32) * gelu_slope(pre)
            hidden[z, 2 * k + q // 2, q % 2, :, cols] = grad.astype(BF16)
            return carry

        lax.fori_loop(0, hid // tv, tile, 0)
        here = piece(z, k, q)
        return send(here, here, sib), send(here, here, zp), send(here, here, zm)

    arrivals = (0, 2, 1, 3)
    own_sends = {}
    for j in range(2):
        acc_p[j].wait_recv()
        own_sends[j] = slope_piece(j, z_in_m.at[2, j], z_in_p.at[1, j])
        acc_m[j].wait_recv()
        own_sends[2 + j] = slope_piece(2 + j, z_in_m.at[1, j], z_in_p.at[2, j])

    def dot2(units):
        def tile(n, carry):
            cols = pl.ds(pl.multiple_of(n * tf, tf), tf)
            rows = [hidden[g, :, j].reshape(4 * hb, hid) for _, g, js in units for j in js]
            rows = rows[0] if len(rows) == 1 else jnp.concatenate(rows, axis=0)
            share = jnp.dot(rows, w_t[:, cols], preferred_element_type=F32).astype(BF16)
            at_row = 0
            for s, _, js in units:
                for j in js:
                    ig[s, j, :, :, cols] = share[at_row:at_row + 4 * hb].reshape(4, hb, tf)
                    at_row += 4 * hb
            return carry

        lax.fori_loop(0, feats // tf, tile, 0)

    def sum_into(out, terms):
        def tile(n, carry):
            cols = pl.ds(pl.multiple_of(n * tv, tv), tv)
            for p in range(out.shape[0]):
                for q in range(out.shape[1]):
                    total = terms[0][p, q, :, cols].astype(F32)
                    for term in terms[1:]:
                        total = total + term[p, q, :, cols].astype(F32)
                    out[p, q, :, cols] = total.astype(BF16)
            return carry

        lax.fori_loop(0, feats // tv, tile, 0)

    ha, hz = pl.ds(0, hb // 2), pl.ds(hb // 2, hb // 2)

    def y_start(s0, ns, j0, nj):
        ss, js = pl.ds(s0, ns), pl.ds(j0, nj)
        blk = lambda by, rows: ig.at[ss, js, nxt(y, by), rows]
        im = lambda n: y_in_m.at[n, ss, js]
        ip = lambda n: y_in_p.at[n, ss, js]
        op = send(blk(2, ha), im(0), yp)
        om = send(blk(2, hz), ip(0), ym)
        dp = send(blk(1, hz), im(1), yp)
        dm = send(blk(3, ha), ip(1), ym)
        return ss, js, blk, im, ip, op, om, dp, dm

    def y_middle(state):
        ss, js, blk, im, ip, op, om, dp, dm = state
        op.wait_recv()
        sum_into(blk(1, ha), [blk(1, ha), im(0)])
        ap = send(blk(1, ha), im(2), yp)
        om.wait_recv()
        sum_into(blk(3, hz), [blk(3, hz), ip(0)])
        am = send(blk(3, hz), ip(2), ym)
        return ss, js, blk, im, ip, (dp, dm, ap, am)

    def y_finish(state):
        ss, js, blk, im, ip, copies = state
        for copy in copies:
            copy.wait_recv()
        sum_into(xs.at[ss, js, ha], [blk(0, ha), im(2), ip(1)])
        sum_into(xs.at[ss, js, hz], [blk(0, hz), im(1), ip(2)])

    def x_copies(s, g, j0, nj):
        one, js = pl.ds(s, 1), pl.ds(j0, nj)
        mine_x = lambda rows: xs.at[one, js, rows]
        slot = lambda n: x_in.at[n, one, js]
        make = lambda rows, n, to: ready(mine_x(rows), slot(n), to)
        copies = (
            make(ha, 0, xp), make(hz, 0, xm), make(hz, 0, xp), make(ha, 1, xp), make(ha, 2, xm), make(hz, 3, xm)
        )
        return nxt(x, 4 - g), mine_x, slot, copies, (j0, nj)

    def x_start(s, g, j0, nj):
        state = x_copies(s, g, j0, nj)
        away, _, _, copies, _ = state

        @pl.when(away == 2)
        def _():
            copies[0].start()
            copies[1].start()

        @pl.when(away == 3)
        def _():
            copies[2].start()

        @pl.when(away == 1)
        def _():
            copies[4].start()

        return state

    def x_middle(state):
        away, mine_x, slot, copies, _ = state

        @pl.when(away == 3)
        def _():
            copies[0].wait_recv()
            sum_into(mine_x(ha), [mine_x(ha), slot(0)])
            copies[3].start()

        @pl.when(away == 1)
        def _():
            copies[1].wait_recv()
            sum_into(mine_x(hz), [mine_x(hz), slot(0)])
            copies[5].start()

    def x_finish(state):
        away, mine_x, slot, copies, (j0, nj) = state
        result = lambda rows: ig_ref.at[pl.ds(0, 1), pl.ds(j0, nj), rows]

        @pl.when(away == 0)
        def _():
            for n in (2, 3, 4, 5):
                copies[n].wait_recv()
            sum_into(result(ha), [mine_x(ha), slot(1), slot(2)])
            sum_into(result(hz), [mine_x(hz), slot(0), slot(3)])

        for role, used in ((2, (0, 1)), (3, (2, 3)), (1, (4, 5))):
            @pl.when(away == role)
            def _(used=used):
                for n in used:
                    copies[n].wait_send()

    def dot3(m, rows_of, first, later):
        rows = pl.ds(m * tm, tm)
        span = 8 * hb * 2

        def tile(n, carry):
            cols = pl.ds(pl.multiple_of(n * t3, t3), t3)
            units = jnp.concatenate([hidden[g, :, j, :, cols].reshape(4 * hb, t3) for g, j in rows_of], axis=0)
            total = jnp.dot(acts_t[rows, first:first + span], units, preferred_element_type=F32)
            if later:
                total = total + wg_ref[rows, cols].astype(F32)
            wg_ref[rows, cols] = total.astype(BF16)
            return carry

        lax.fori_loop(0, hid // t3, tile, 0)

    blocks = feats // tm

    def early(lo, hi):
        for m in range(lo, hi):
            dot3(m, tokens_of[:4], 0, False)

    def late(lo, hi):
        for m in range(lo, hi):
            dot3(m, tokens_of[4:], 8 * hb * 2, True)

    def neighbours(qs):
        copies = []
        for q in qs:
            own_sends[q][1].wait_recv()
            here = piece(low, k, q)
            if q < 2:
                fwd[q] = send(here, here, zp)
            copies.append(send(here, here, sib))
            own_sends[q][2].wait_recv()
            here = piece(high, k, q)
            if q >= 2:
                fwd[q] = send(here, here, zm)
            copies.append(send(here, here, sib))
        return copies

    def opposite(qs):
        copies = []
        for q in qs:
            fwd[q].wait_recv()
            here = piece(opp, k, q)
            copies.append(send(here, here, sib))
        return copies

    def arrived(copies):
        for copy in copies:
            copy.wait_recv()

    fwd = {}
    arrived([own_sends[q][0] for q in arrivals])
    dot2([(0, z, (0, 1))])
    y0 = y_start(0, 1, 0, 2)
    from_sib = neighbours((0, 2))
    y0 = y_middle(y0)
    arrived(from_sib)
    dot2([(1, low, (0,)), (2, high, (0,))])
    y1 = y_start(1, 2, 0, 1)
    y_finish(y0)
    x0 = x_start(0, z, 0, 2)
    early(0, 2)
    y1 = y_middle(y1)
    x_middle(x0)
    early(2, blocks)
    y_finish(y1)
    from_sib = neighbours((1, 3))
    x_finish(x0)
    arrived(from_sib)
    dot2([(1, low, (1,)), (2, high, (1,))])
    y2 = y_start(1, 2, 1, 1)
    from_sib = opposite((0, 2))
    y2 = y_middle(y2)
    arrived(from_sib)
    dot2([(3, opp, (0,))])
    y3 = y_start(3, 1, 0, 1)
    y_finish(y2)
    x1 = x_start(1, low, 0, 2)
    x2 = x_start(2, high, 0, 2)
    from_sib = opposite((1, 3))
    y3 = y_middle(y3)
    arrived(from_sib)
    dot2([(3, opp, (1,))])
    y4 = y_start(3, 1, 1, 1)
    x_middle(x1)
    x_middle(x2)
    y_finish(y3)
    x3 = x_start(3, opp, 0, 1)
    late(0, 1)
    y4 = y_middle(y4)
    x_middle(x3)
    late(1, 2)
    y_finish(y4)
    x4 = x_start(3, opp, 1, 1)
    late(2, 3)
    x_middle(x4)
    x_finish(x1)
    x_finish(x2)
    x_finish(x3)
    late(3, blocks)
    x_finish(x4)

    for copy in sent:
        if copy is not None:
            copy.wait_send()


def write_out(ig_ref, wg_ref, ig_out, wg_out, sem):
    rows = wg_ref.shape[0] // 4
    copies = [pltpu.make_async_copy(ig_ref, ig_out, sem.at[4])]
    for n in range(4):
        part = pl.ds(n * rows, rows)
        copies.append(pltpu.make_async_copy(wg_ref.at[part], wg_out.at[part], sem.at[n]))
    for copy in copies:
        copy.start()
    for copy in copies:
        copy.wait()


def per_device(acts, up_weight, out_grad):
    tb, feats = acts.shape
    ob, hid = out_grad.shape
    tokens = 16 * tb
    hb = tb // 2
    vmem = lambda *shape: pltpu.VMEM(shape, BF16)
    in_hbm = pl.BlockSpec(memory_space=pltpu.HBM)
    in_vmem = pl.BlockSpec(memory_space=pltpu.VMEM)
    flops = 3 * 2 * tokens * feats * hid
    acts, up_weight, out_grad = (
        pltpu.with_memory_space_constraint(a, pltpu.HBM) for a in (acts, up_weight, out_grad)
    )
    input_grad, weight_grad = pl.pallas_call(
        kernel,
        out_shape=(
            vmem(1, 2, hb, feats),
            vmem(feats, hid),
        ),
        in_specs=[in_hbm] * 3,
        out_specs=(in_vmem, in_vmem),
        scratch_shapes=[
            vmem(4, 4, 2, hb, feats),
            vmem(hid, feats),
            vmem(ob, hid),
            vmem(feats, tokens),
            vmem(4, 4, 2, hb, hid),
            vmem(4, 2, 2, hb, hid),
            vmem(3, 2, hb, hid),
            vmem(3, 2, hb, hid),
            vmem(4, 4, 2, hb, hid),
            vmem(4, 2, 4, hb, feats),
            vmem(3, 4, 2, hb // 2, feats),
            vmem(3, 4, 2, hb // 2, feats),
            vmem(4, 2, hb, feats),
            vmem(4, 4, 2, hb // 2, feats),
            pltpu.SemaphoreType.DMA((9,)),
            pltpu.SemaphoreType.DMA((N_SEMS,)),
            pltpu.SemaphoreType.DMA((N_SEMS,)),
        ],
        compiler_params=pltpu.CompilerParams(
            collective_id=0, has_side_effects=True, vmem_limit_bytes=50 * 2**20
        ),
        cost_estimate=pl.CostEstimate(flops=flops, bytes_accessed=4 * feats * hid, transcendentals=2 * ob * hid),
    )(acts, up_weight, out_grad)
    return pl.pallas_call(
        write_out,
        out_shape=(
            jax.ShapeDtypeStruct((tb, feats), BF16),
            jax.ShapeDtypeStruct((feats, hid), BF16),
        ),
        in_specs=[in_vmem] * 2,
        out_specs=(in_hbm, in_hbm),
        scratch_shapes=[pltpu.SemaphoreType.DMA((5,))],
        compiler_params=pltpu.CompilerParams(vmem_limit_bytes=2 * 2**20),
        cost_estimate=pl.CostEstimate(flops=0, bytes_accessed=2 * feats * hid, transcendentals=0),
    )(input_grad.reshape(tb, feats), weight_grad)


def solution(mesh):
    in_specs = (P("col", "row"), P("row", "col"), P("row", "col"))
    out_specs = (P("col", "row"), P("row", "col"))
    return jax.shard_map(
        per_device, mesh=mesh, in_specs=in_specs, out_specs=out_specs, check_vma=False
    )
```

```python
import functools

import jax
import jax.numpy as jnp
from jax import lax
from jax.experimental import pallas as pl
from jax.experimental.pallas import tpu as pltpu
from jax.sharding import PartitionSpec as P

F32, BF16 = jnp.float32, jnp.bfloat16
MESH = pl.DeviceIdType.MESH
N_SEMS = 160


def gelu_slope(pre):
    cdf = 0.5 * (1.0 + lax.erf(pre * 0.7071067811865476))
    dens = jnp.exp(-0.5 * pre * pre) * 0.3989422804014327
    return cdf + pre * dens


def tile_of(size, want):
    return want if size % want == 0 else size


def kernel(
    acts_ref, w_ref, og_ref, ig_ref, wg_ref,
    acts, w_t, og, acts_t, part, sib_in, z_in_m, z_in_p, hidden, ig, y_in_m, y_in_p, xs, x_in,
    local_sem, send_sem, recv_sem,
):
    tb, feats = acts_ref.shape
    ob, hid = og_ref.shape
    quarter = ob // 4
    tv, tn, t3 = tile_of(hid // 2, 512), tile_of(hid // 2, 768), tile_of(hid, 256)
    tf, tm = tile_of(feats, 768), tile_of(feats, 256)
    w = wg_ref

    row, col = lax.axis_index("row"), lax.axis_index("col")
    z, k = lax.div(row, 2), lax.rem(row, 2)
    x, y = lax.div(col, 4), lax.rem(col, 4)
    nxt = lambda v, by: lax.rem(v + by, 4)
    sib = {"row": z * 2 + (1 - k)}
    zp, zm = {"row": nxt(z, 1) * 2 + k}, {"row": nxt(z, 3) * 2 + k}
    xp, xm = {"col": nxt(x, 1) * 4 + y}, {"col": nxt(x, 3) * 4 + y}
    yp, ym = {"col": x * 4 + nxt(y, 1)}, {"col": x * 4 + nxt(y, 3)}

    sent = []

    def ready(src, dst, to):
        i = len(sent)
        sent.append(None)
        return pltpu.make_async_remote_copy(
            src_ref=src, dst_ref=dst, send_sem=send_sem.at[i], recv_sem=recv_sem.at[i],
            device_id=to, device_id_type=MESH,
        )

    def send(src, dst, to):
        copy = ready(src, dst, to)
        copy.start()
        sent[-1] = copy
        return copy

    hb = tb // 2

    def step_of(group):
        away = nxt(group, 4 - z)
        odd, far = lax.rem(away, 2), lax.div(away, 2)
        return odd * (2 - lax.rem(far + y, 2)) + (1 - odd) * (3 - 3 * far)

    barrier = pltpu.get_barrier_semaphore()
    for to in (sib, zp, zm, xp, xm, yp, ym):
        pl.semaphore_signal(barrier, inc=1, device_id=to, device_id_type=MESH)
    load_acts = [
        pltpu.make_async_copy(acts_ref.at[pl.ds(j * hb, hb)], acts.at[step_of(x), y, j], local_sem.at[j])
        for j in range(2)
    ]
    load_og = pltpu.make_async_copy(og_ref, og, local_sem.at[2])
    load_w = [
        pltpu.make_async_copy(w_ref.at[pl.ds(m * tm, tm)], w.at[pl.ds(m * tm, tm)], local_sem.at[3 + m])
        for m in range(feats // tm)
    ]
    for load in (*load_acts, *load_w, load_og):
        load.start()
    for load in load_acts:
        load.wait()
    pl.semaphore_wait(barrier, 7)

    low16, high16 = pl.ds(0, hb // 2), pl.ds(hb // 2, hb // 2)

    def ag_start(block, to_p, to_m):
        a = lambda by: block(by, low16)
        b = lambda by: block(by, high16)
        pa = send(a(0), a(0), to_p)
        mb = send(b(0), b(0), to_m)
        pb = send(b(0), b(0), to_p)
        ma = send(a(0), a(0), to_m)
        return a, b, pa, mb, pb, ma, to_p, to_m

    def ag_forward(state):
        a, b, pa, mb, pb, ma, to_p, to_m = state
        pa.wait_recv()
        fa = send(a(3), a(3), to_p)
        mb.wait_recv()
        fb = send(b(1), b(1), to_m)
        return pb, ma, fa, fb

    def ag_finish(copies):
        for copy in copies:
            copy.wait_recv()

    def x_gather(j):
        return ag_start(lambda by, rows: acts.at[step_of(nxt(x, by)), y, j, rows], xp, xm)

    def y_gather(s, j0, nj):
        return ag_start(lambda by, rows: acts.at[s, nxt(y, by), pl.ds(j0, nj), rows], yp, ym)

    def turn_w(m, loaded=False):
        if not loaded:
            load_w[m].wait()

        def tile(n, carry):
            cols = pl.ds(pl.multiple_of(n * tm, tm), tm)
            w_t[cols, m * tm:(m + 1) * tm] = w[m * tm:(m + 1) * tm, cols].T
            return carry

        lax.fori_loop(0, hid // tm, tile, 0)

    def dot1(s, j0, nj):
        js = pl.ds(j0, nj)
        sem = len(sent)

        def to_sib(cols):
            return pltpu.make_async_remote_copy(
                src_ref=part.at[s, pl.ds(2 * (1 - k), 2), js, :, cols], dst_ref=sib_in.at[s, :, js, :, cols],
                send_sem=send_sem.at[sem], recv_sem=recv_sem.at[sem], device_id=sib, device_id_type=MESH,
            )

        def tile(n, carry):
            cols = pl.ds(pl.multiple_of(n * tn, tn), tn)
            share = jnp.dot(
                acts[s, :, js].reshape(4 * nj * hb, feats), w[:, cols], preferred_element_type=F32
            )
            part[s, :, js, :, cols] = share.astype(BF16).reshape(4, nj, hb, tn)
            to_sib(cols).start()
            return carry

        lax.fori_loop(0, hid // tn, tile, 0)
        sent.append(to_sib(pl.ds(0, hid)))
        return sent[-1]

    def add_into(dst, src):
        def tile(n, carry):
            cols = pl.ds(pl.multiple_of(n * tv, tv), tv)
            for j in range(dst.shape[0]):
                total = dst[j, :, cols].astype(F32) + src[j, :, cols].astype(F32)
                dst[j, :, cols] = total.astype(BF16)
            return carry

        lax.fori_loop(0, hid // tv, tile, 0)

    def core_sum(s, copy, j0, nj):
        copy.wait_recv()
        js = pl.ds(j0, nj)
        for way in range(2):
            add_into(part.at[s, 2 * k + way, js], sib_in.at[s, way, js])

    mine = lambda s, way: part.at[s, 2 * k + way]
    gx = x_gather(0)
    turn_w(0)
    gx0 = ag_forward(gx)
    gx = x_gather(1)
    turn_w(1)
    ag_finish(gx0)
    g = y_gather(0, 0, 1)
    turn_w(2)
    gx1 = ag_forward(gx)
    g0 = ag_forward(g)
    turn_w(3)
    ag_finish(gx1)
    g = y_gather(0, 1, 1)
    for load in load_w[4:]:
        load.wait()
    ag_finish(g0)
    opp_p, opp_m = [], []
    c = dot1(0, 0, 1)
    g0 = ag_forward(g)
    g = y_gather(1, 0, 2)
    core_sum(0, c, 0, 1)
    opp_p.append(send(mine(0, 0).at[0], z_in_m.at[0, 0], zp))
    opp_m.append(send(mine(0, 1).at[0], z_in_p.at[0, 0], zm))
    ag_finish(g0)
    c = dot1(0, 1, 1)
    g0 = ag_forward(g)
    g = y_gather(2, 0, 2)
    core_sum(0, c, 1, 1)
    opp_p.append(send(mine(0, 0).at[1], z_in_m.at[0, 1], zp))
    opp_m.append(send(mine(0, 1).at[1], z_in_p.at[0, 1], zm))
    ag_finish(g0)
    c = dot1(1, 0, 2)
    g0 = ag_forward(g)
    g = y_gather(3, 0, 2)
    core_sum(1, c, 0, 2)
    dir_p = send(mine(1, 1), z_in_m.at[1], zp)
    dir_m = send(mine(1, 0), z_in_p.at[1], zm)
    ag_finish(g0)
    c = dot1(2, 0, 2)
    g0 = ag_forward(g)
    core_sum(2, c, 0, 2)
    acc_p, acc_m = [], []
    for j in range(2):
        one = pl.ds(j, 1)
        opp_p[j].wait_recv()
        add_into(mine(2, 0).at[one], z_in_m.at[0, one])
        acc_p.append(send(mine(2, 0).at[j], z_in_m.at[2, j], zp))
        opp_m[j].wait_recv()
        add_into(mine(2, 1).at[one], z_in_p.at[0, one])
        acc_m.append(send(mine(2, 1).at[j], z_in_p.at[2, j], zm))
    ag_finish(g0)
    c = dot1(3, 0, 2)
    core_sum(3, c, 0, 2)
    load_og.wait()

    low, high, opp = nxt(z, 3), nxt(z, 1), nxt(z, 2)
    tokens_of = [(z, 0), (z, 1), (low, 0), (high, 0), (low, 1), (high, 1), (opp, 0), (opp, 1)]
    held_in = [(3, 3), (3, 3), (1, 2), (2, 1), (1, 2), (2, 1), (0, 0), (0, 0)]

    def turn(n, carry):
        cols = pl.ds(pl.multiple_of(n * tm, tm), tm)
        for t, steps in enumerate(held_in):
            rows = [acts[steps[b % 2], b, tokens_of[t][1], :, cols] for b in range(4)]
            acts_t[cols, t * 4 * hb:(t + 1) * 4 * hb] = jnp.concatenate(rows, axis=0).T
        return carry

    lax.fori_loop(0, feats // tm, turn, 0)
    for m in range(4, feats // tm):
        turn_w(m, True)

    dir_p.wait_recv()
    dir_m.wait_recv()
    piece = lambda zz, kk, q: hidden.at[zz, 2 * kk + q // 2, q % 2]

    def slope_piece(q, from_m, from_p):
        start = q * quarter

        def tile(n, carry):
            cols = pl.ds(pl.multiple_of(n * tv, tv), tv)
            own = part[3, 2 * k + q // 2, q % 2, :, cols]
            pre = own.astype(F32) + from_m[:, cols].astype(F32) + from_p[:, cols].astype(F32)
            grad = og[start:start + quarter, cols].astype(F32) * gelu_slope(pre)
            hidden[z, 2 * k + q // 2, q % 2, :, cols] = grad.astype(BF16)
            return carry

        lax.fori_loop(0, hid // tv, tile, 0)
        here = piece(z, k, q)
        return send(here, here, sib), send(here, here, zp), send(here, here, zm)

    arrivals = (0, 2, 1, 3)
    own_sends = {}
    for j in range(2):
        acc_p[j].wait_recv()
        own_sends[j] = slope_piece(j, z_in_m.at[2, j], z_in_p.at[1, j])
        acc_m[j].wait_recv()
        own_sends[2 + j] = slope_piece(2 + j, z_in_m.at[1, j], z_in_p.at[2, j])

    def dot2(units):
        def tile(n, carry):
            cols = pl.ds(pl.multiple_of(n * tf, tf), tf)
            rows = [hidden[g, :, j].reshape(4 * hb, hid) for _, g, js in units for j in js]
            rows = rows[0] if len(rows) == 1 else jnp.concatenate(rows, axis=0)
            share = jnp.dot(rows, w_t[:, cols], preferred_element_type=F32).astype(BF16)
            at_row = 0
            for s, _, js in units:
                for j in js:
                    ig[s, j, :, :, cols] = share[at_row:at_row + 4 * hb].reshape(4, hb, tf)
                    at_row += 4 * hb
            return carry

        lax.fori_loop(0, feats // tf, tile, 0)

    def sum_into(out, terms):
        def tile(n, carry):
            cols = pl.ds(pl.multiple_of(n * tv, tv), tv)
            for p in range(out.shape[0]):
                for q in range(out.shape[1]):
                    total = terms[0][p, q, :, cols].astype(F32)
                    for term in terms[1:]:
                        total = total + term[p, q, :, cols].astype(F32)
                    out[p, q, :, cols] = total.astype(BF16)
            return carry

        lax.fori_loop(0, feats // tv, tile, 0)

    ha, hz = pl.ds(0, hb // 2), pl.ds(hb // 2, hb // 2)

    def y_start(s0, ns, j0, nj):
        ss, js = pl.ds(s0, ns), pl.ds(j0, nj)
        blk = lambda by, rows: ig.at[ss, js, nxt(y, by), rows]
        im = lambda n: y_in_m.at[n, ss, js]
        ip = lambda n: y_in_p.at[n, ss, js]
        op = send(blk(2, ha), im(0), yp)
        om = send(blk(2, hz), ip(0), ym)
        dp = send(blk(1, hz), im(1), yp)
        dm = send(blk(3, ha), ip(1), ym)
        return ss, js, blk, im, ip, op, om, dp, dm

    def y_middle(state):
        ss, js, blk, im, ip, op, om, dp, dm = state
        op.wait_recv()
        sum_into(blk(1, ha), [blk(1, ha), im(0)])
        ap = send(blk(1, ha), im(2), yp)
        om.wait_recv()
        sum_into(blk(3, hz), [blk(3, hz), ip(0)])
        am = send(blk(3, hz), ip(2), ym)
        return ss, js, blk, im, ip, (dp, dm, ap, am)

    def y_finish(state):
        ss, js, blk, im, ip, copies = state
        for copy in copies:
            copy.wait_recv()
        sum_into(xs.at[ss, js, ha], [blk(0, ha), im(2), ip(1)])
        sum_into(xs.at[ss, js, hz], [blk(0, hz), im(1), ip(2)])

    def x_copies(s, g, j0, nj):
        one, js = pl.ds(s, 1), pl.ds(j0, nj)
        mine_x = lambda rows: xs.at[one, js, rows]
        slot = lambda n: x_in.at[n, one, js]
        make = lambda rows, n, to: ready(mine_x(rows), slot(n), to)
        copies = (
            make(ha, 0, xp), make(hz, 0, xm), make(hz, 0, xp), make(ha, 1, xp), make(ha, 2, xm), make(hz, 3, xm)
        )
        return nxt(x, 4 - g), mine_x, slot, copies, (j0, nj)

    def x_start(s, g, j0, nj):
        state = x_copies(s, g, j0, nj)
        away, _, _, copies, _ = state

        @pl.when(away == 2)
        def _():
            copies[0].start()
            copies[1].start()

        @pl.when(away == 3)
        def _():
            copies[2].start()

        @pl.when(away == 1)
        def _():
            copies[4].start()

        return state

    def x_middle(state):
        away, mine_x, slot, copies, _ = state

        @pl.when(away == 3)
        def _():
            copies[0].wait_recv()
            sum_into(mine_x(ha), [mine_x(ha), slot(0)])
            copies[3].start()

        @pl.when(away == 1)
        def _():
            copies[1].wait_recv()
            sum_into(mine_x(hz), [mine_x(hz), slot(0)])
            copies[5].start()

    def x_finish(state):
        away, mine_x, slot, copies, (j0, nj) = state
        result = lambda rows: ig_ref.at[pl.ds(0, 1), pl.ds(j0, nj), rows]

        @pl.when(away == 0)
        def _():
            for n in (2, 3, 4, 5):
                copies[n].wait_recv()
            sum_into(result(ha), [mine_x(ha), slot(1), slot(2)])
            sum_into(result(hz), [mine_x(hz), slot(0), slot(3)])

        for role, used in ((2, (0, 1)), (3, (2, 3)), (1, (4, 5))):
            @pl.when(away == role)
            def _(used=used):
                for n in used:
                    copies[n].wait_send()

    def dot3(lo, hi, rows_of, first, later):
        span = 16 * hb

        def tile(n, carry):
            cols = pl.ds(pl.multiple_of(n * t3, t3), t3)
            units = jnp.concatenate([hidden[g, :, j, :, cols].reshape(4 * hb, t3) for g, j in rows_of], axis=0)
            total = jnp.dot(acts_t[:, first:first + span], units, preferred_element_type=F32)
            if later:
                total = total + wg_ref[:, cols].astype(F32)
            wg_ref[:, cols] = total.astype(BF16)
            return carry

        lax.fori_loop(lo, hi, tile, 0)

    blocks = hid // t3

    def early(lo, hi):
        dot3(lo * blocks // 6, hi * blocks // 6, tokens_of[:4], 0, False)

    def late(lo, hi):
        dot3(lo * blocks // 6, hi * blocks // 6, tokens_of[4:], 16 * hb, True)

    def neighbours(qs):
        copies = []
        for q in qs:
            own_sends[q][1].wait_recv()
            here = piece(low, k, q)
            if q < 2:
                fwd[q] = send(here, here, zp)
            copies.append(send(here, here, sib))
            own_sends[q][2].wait_recv()
            here = piece(high, k, q)
            if q >= 2:
                fwd[q] = send(here, here, zm)
            copies.append(send(here, here, sib))
        return copies

    def opposite(qs):
        copies = []
        for q in qs:
            fwd[q].wait_recv()
            here = piece(opp, k, q)
            copies.append(send(here, here, sib))
        return copies

    def arrived(copies):
        for copy in copies:
            copy.wait_recv()

    fwd = {}
    arrived([own_sends[q][0] for q in arrivals])
    dot2([(0, z, (0, 1))])
    y0 = y_start(0, 1, 0, 2)
    from_sib = neighbours((0, 2))
    y0 = y_middle(y0)
    arrived(from_sib)
    dot2([(1, low, (0,)), (2, high, (0,))])
    y1 = y_start(1, 2, 0, 1)
    y_finish(y0)
    x0 = x_start(0, z, 0, 2)
    early(0, 2)
    y1 = y_middle(y1)
    x_middle(x0)
    early(2, 6)
    y_finish(y1)
    from_sib = neighbours((1, 3))
    x_finish(x0)
    arrived(from_sib)
    dot2([(1, low, (1,)), (2, high, (1,))])
    y2 = y_start(1, 2, 1, 1)
    from_sib = opposite((0, 2))
    y2 = y_middle(y2)
    arrived(from_sib)
    dot2([(3, opp, (0,))])
    y3 = y_start(3, 1, 0, 1)
    y_finish(y2)
    x1 = x_start(1, low, 0, 2)
    x2 = x_start(2, high, 0, 2)
    from_sib = opposite((1, 3))
    y3 = y_middle(y3)
    arrived(from_sib)
    dot2([(3, opp, (1,))])
    y4 = y_start(3, 1, 1, 1)
    x_middle(x1)
    x_middle(x2)
    y_finish(y3)
    x3 = x_start(3, opp, 0, 1)
    late(0, 1)
    y4 = y_middle(y4)
    x_middle(x3)
    late(1, 2)
    y_finish(y4)
    x4 = x_start(3, opp, 1, 1)
    late(2, 3)
    x_middle(x4)
    x_finish(x1)
    x_finish(x2)
    x_finish(x3)
    late(3, 6)
    x_finish(x4)

    for copy in sent:
        if copy is not None:
            copy.wait_send()


def write_out(ig_ref, wg_ref, ig_out, wg_out, sem):
    rows = wg_ref.shape[0] // 4
    copies = [pltpu.make_async_copy(ig_ref, ig_out, sem.at[4])]
    for n in range(4):
        part = pl.ds(n * rows, rows)
        copies.append(pltpu.make_async_copy(wg_ref.at[part], wg_out.at[part], sem.at[n]))
    for copy in copies:
        copy.start()
    for copy in copies:
        copy.wait()


def per_device(acts, up_weight, out_grad):
    tb, feats = acts.shape
    ob, hid = out_grad.shape
    tokens = 16 * tb
    hb = tb // 2
    vmem = lambda *shape: pltpu.VMEM(shape, BF16)
    in_hbm = pl.BlockSpec(memory_space=pltpu.HBM)
    in_vmem = pl.BlockSpec(memory_space=pltpu.VMEM)
    flops = 3 * 2 * tokens * feats * hid
    acts, up_weight, out_grad = (
        pltpu.with_memory_space_constraint(a, pltpu.HBM) for a in (acts, up_weight, out_grad)
    )
    input_grad, weight_grad = pl.pallas_call(
        kernel,
        out_shape=(
            vmem(1, 2, hb, feats),
            vmem(feats, hid),
        ),
        in_specs=[in_hbm] * 3,
        out_specs=(in_vmem, in_vmem),
        scratch_shapes=[
            vmem(4, 4, 2, hb, feats),
            vmem(hid, feats),
            vmem(ob, hid),
            vmem(feats, tokens),
            vmem(4, 4, 2, hb, hid),
            vmem(4, 2, 2, hb, hid),
            vmem(3, 2, hb, hid),
            vmem(3, 2, hb, hid),
            vmem(4, 4, 2, hb, hid),
            vmem(4, 2, 4, hb, feats),
            vmem(3, 4, 2, hb // 2, feats),
            vmem(3, 4, 2, hb // 2, feats),
            vmem(4, 2, hb, feats),
            vmem(4, 4, 2, hb // 2, feats),
            pltpu.SemaphoreType.DMA((9,)),
            pltpu.SemaphoreType.DMA((N_SEMS,)),
            pltpu.SemaphoreType.DMA((N_SEMS,)),
        ],
        compiler_params=pltpu.CompilerParams(
            collective_id=0, has_side_effects=True, vmem_limit_bytes=50 * 2**20
        ),
        cost_estimate=pl.CostEstimate(flops=flops, bytes_accessed=4 * feats * hid, transcendentals=2 * ob * hid),
    )(acts, up_weight, out_grad)
    return pl.pallas_call(
        write_out,
        out_shape=(
            jax.ShapeDtypeStruct((tb, feats), BF16),
            jax.ShapeDtypeStruct((feats, hid), BF16),
        ),
        in_specs=[in_vmem] * 2,
        out_specs=(in_hbm, in_hbm),
        scratch_shapes=[pltpu.SemaphoreType.DMA((5,))],
        compiler_params=pltpu.CompilerParams(vmem_limit_bytes=2 * 2**20),
        cost_estimate=pl.CostEstimate(flops=0, bytes_accessed=2 * feats * hid, transcendentals=0),
    )(input_grad.reshape(tb, feats), weight_grad)


def solution(mesh):
    in_specs = (P("col", "row"), P("row", "col"), P("row", "col"))
    out_specs = (P("col", "row"), P("row", "col"))
    return jax.shard_map(
        per_device, mesh=mesh, in_specs=in_specs, out_specs=out_specs, check_vma=False
    )
```

```python
import functools

import jax
import jax.numpy as jnp
from jax import lax
from jax.experimental import pallas as pl
from jax.experimental.pallas import tpu as pltpu
from jax.sharding import PartitionSpec as P

F32, BF16 = jnp.float32, jnp.bfloat16
MESH = pl.DeviceIdType.MESH
N_SEMS = 160


def gelu_slope(pre):
    cdf = 0.5 * (1.0 + lax.erf(pre * 0.7071067811865476))
    dens = jnp.exp(-0.5 * pre * pre) * 0.3989422804014327
    return cdf + pre * dens


def tile_of(size, want):
    return want if size % want == 0 else size


def kernel(
    acts_ref, w_ref, og_ref, ig_ref, wg_ref,
    acts, w_t, og, acts_t, part, sib_in, z_in_m, z_in_p, hidden, ig, y_in_m, y_in_p, xs, x_in,
    local_sem, send_sem, recv_sem,
):
    tb, feats = acts_ref.shape
    ob, hid = og_ref.shape
    quarter = ob // 4
    tv, tn, t3 = tile_of(hid // 2, 512), tile_of(hid // 2, 1536), tile_of(hid, 512)
    tf, tm = tile_of(feats, 1536), tile_of(feats, 256)
    w = wg_ref

    row, col = lax.axis_index("row"), lax.axis_index("col")
    z, k = lax.div(row, 2), lax.rem(row, 2)
    x, y = lax.div(col, 4), lax.rem(col, 4)
    nxt = lambda v, by: lax.rem(v + by, 4)
    sib = {"row": z * 2 + (1 - k)}
    zp, zm = {"row": nxt(z, 1) * 2 + k}, {"row": nxt(z, 3) * 2 + k}
    xp, xm = {"col": nxt(x, 1) * 4 + y}, {"col": nxt(x, 3) * 4 + y}
    yp, ym = {"col": x * 4 + nxt(y, 1)}, {"col": x * 4 + nxt(y, 3)}

    sent = []

    def ready(src, dst, to):
        i = len(sent)
        sent.append(None)
        return pltpu.make_async_remote_copy(
            src_ref=src, dst_ref=dst, send_sem=send_sem.at[i], recv_sem=recv_sem.at[i],
            device_id=to, device_id_type=MESH,
        )

    def send(src, dst, to):
        copy = ready(src, dst, to)
        copy.start()
        sent[-1] = copy
        return copy

    hb = tb // 2

    def step_of(group):
        away = nxt(group, 4 - z)
        odd, far = lax.rem(away, 2), lax.div(away, 2)
        return odd * (2 - lax.rem(far + y, 2)) + (1 - odd) * (3 - 3 * far)

    barrier = pltpu.get_barrier_semaphore()
    for to in (sib, zp, zm, xp, xm, yp, ym):
        pl.semaphore_signal(barrier, inc=1, device_id=to, device_id_type=MESH)
    load_acts = [
        pltpu.make_async_copy(acts_ref.at[pl.ds(j * hb, hb)], acts.at[step_of(x), y, j], local_sem.at[j])
        for j in range(2)
    ]
    load_og = pltpu.make_async_copy(og_ref, og, local_sem.at[2])
    load_w = [
        pltpu.make_async_copy(w_ref.at[pl.ds(m * tm, tm)], w.at[pl.ds(m * tm, tm)], local_sem.at[3 + m])
        for m in range(feats // tm)
    ]
    for load in (*load_acts, *load_w, load_og):
        load.start()
    for load in load_acts:
        load.wait()
    pl.semaphore_wait(barrier, 7)

    low16, high16 = pl.ds(0, hb // 2), pl.ds(hb // 2, hb // 2)

    def ag_start(block, to_p, to_m):
        a = lambda by: block(by, low16)
        b = lambda by: block(by, high16)
        pa = send(a(0), a(0), to_p)
        mb = send(b(0), b(0), to_m)
        pb = send(b(0), b(0), to_p)
        ma = send(a(0), a(0), to_m)
        return a, b, pa, mb, pb, ma, to_p, to_m

    def ag_forward(state):
        a, b, pa, mb, pb, ma, to_p, to_m = state
        pa.wait_recv()
        fa = send(a(3), a(3), to_p)
        mb.wait_recv()
        fb = send(b(1), b(1), to_m)
        return pb, ma, fa, fb

    def ag_finish(copies):
        for copy in copies:
            copy.wait_recv()

    def x_gather(j):
        return ag_start(lambda by, rows: acts.at[step_of(nxt(x, by)), y, j, rows], xp, xm)

    def y_gather(s, j0, nj):
        return ag_start(lambda by, rows: acts.at[s, nxt(y, by), pl.ds(j0, nj), rows], yp, ym)

    def turn_w(m, loaded=False):
        if not loaded:
            load_w[m].wait()

        def tile(n, carry):
            cols = pl.ds(pl.multiple_of(n * tm, tm), tm)
            w_t[cols, m * tm:(m + 1) * tm] = w[m * tm:(m + 1) * tm, cols].T
            return carry

        lax.fori_loop(0, hid // tm, tile, 0)

    def dot1(s, j0, nj):
        js = pl.ds(j0, nj)
        sem = len(sent)

        def to_sib(cols):
            return pltpu.make_async_remote_copy(
                src_ref=part.at[s, pl.ds(2 * (1 - k), 2), js, :, cols], dst_ref=sib_in.at[s, :, js, :, cols],
                send_sem=send_sem.at[sem], recv_sem=recv_sem.at[sem], device_id=sib, device_id_type=MESH,
            )

        def tile(n, carry):
            cols = pl.ds(pl.multiple_of(n * tn, tn), tn)
            share = jnp.dot(
                acts[s, :, js].reshape(4 * nj * hb, feats), w[:, cols], preferred_element_type=F32
            )
            part[s, :, js, :, cols] = share.astype(BF16).reshape(4, nj, hb, tn)
            to_sib(cols).start()
            return carry

        lax.fori_loop(0, hid // tn, tile, 0)
        sent.append(to_sib(pl.ds(0, hid)))
        return sent[-1]

    def add_into(dst, src):
        def tile(n, carry):
            cols = pl.ds(pl.multiple_of(n * tv, tv), tv)
            for j in range(dst.shape[0]):
                total = dst[j, :, cols].astype(F32) + src[j, :, cols].astype(F32)
                dst[j, :, cols] = total.astype(BF16)
            return carry

        lax.fori_loop(0, hid // tv, tile, 0)

    def core_sum(s, copy, j0, nj):
        copy.wait_recv()
        js = pl.ds(j0, nj)
        for way in range(2):
            add_into(part.at[s, 2 * k + way, js], sib_in.at[s, way, js])

    mine = lambda s, way: part.at[s, 2 * k + way]
    gx = x_gather(0)
    turn_w(0)
    gx0 = ag_forward(gx)
    gx = x_gather(1)
    turn_w(1)
    ag_finish(gx0)
    g = y_gather(0, 0, 1)
    turn_w(2)
    gx1 = ag_forward(gx)
    g0 = ag_forward(g)
    turn_w(3)
    ag_finish(gx1)
    g = y_gather(0, 1, 1)
    for load in load_w[4:]:
        load.wait()
    ag_finish(g0)
    opp_p, opp_m = [], []
    c = dot1(0, 0, 1)
    g0 = ag_forward(g)
    g = y_gather(1, 0, 1)
    core_sum(0, c, 0, 1)
    opp_p.append(send(mine(0, 0).at[0], z_in_m.at[0, 0], zp))
    opp_m.append(send(mine(0, 1).at[0], z_in_p.at[0, 0], zm))
    ag_finish(g0)
    c = dot1(0, 1, 1)
    g0 = ag_forward(g)
    g = y_gather(1, 1, 1)
    core_sum(0, c, 1, 1)
    opp_p.append(send(mine(0, 0).at[1], z_in_m.at[0, 1], zp))
    opp_m.append(send(mine(0, 1).at[1], z_in_p.at[0, 1], zm))
    dir_p, dir_m = [], []
    for j in range(2):
        ag_finish(g0)
        c = dot1(1, j, 1)
        g0 = ag_forward(g)
        g = y_gather(2 + j, 0, 2)
        core_sum(1, c, j, 1)
        dir_p.append(send(mine(1, 1).at[j], z_in_m.at[1, j], zp))
        dir_m.append(send(mine(1, 0).at[j], z_in_p.at[1, j], zm))
    ag_finish(g0)
    c = dot1(2, 0, 2)
    g0 = ag_forward(g)
    core_sum(2, c, 0, 2)
    acc_p, acc_m = [], []
    for j in range(2):
        one = pl.ds(j, 1)
        opp_p[j].wait_recv()
        add_into(mine(2, 0).at[one], z_in_m.at[0, one])
        acc_p.append(send(mine(2, 0).at[j], z_in_m.at[2, j], zp))
        opp_m[j].wait_recv()
        add_into(mine(2, 1).at[one], z_in_p.at[0, one])
        acc_m.append(send(mine(2, 1).at[j], z_in_p.at[2, j], zm))
    ag_finish(g0)
    c = dot1(3, 0, 2)
    core_sum(3, c, 0, 2)
    load_og.wait()

    low, high, opp = nxt(z, 3), nxt(z, 1), nxt(z, 2)
    tokens_of = [(z, 0), (z, 1), (low, 0), (high, 0), (low, 1), (high, 1), (opp, 0), (opp, 1)]
    held_in = [(3, 3), (3, 3), (1, 2), (2, 1), (1, 2), (2, 1), (0, 0), (0, 0)]

    def turn(n, carry):
        cols = pl.ds(pl.multiple_of(n * tm, tm), tm)
        for t, steps in enumerate(held_in):
            rows = [acts[steps[b % 2], b, tokens_of[t][1], :, cols] for b in range(4)]
            acts_t[cols, t * 4 * hb:(t + 1) * 4 * hb] = jnp.concatenate(rows, axis=0).T
        return carry

    lax.fori_loop(0, feats // tm, turn, 0)
    for m in range(4, feats // tm):
        turn_w(m, True)

    for copy in (*dir_p, *dir_m):
        copy.wait_recv()
    piece = lambda zz, kk, q: hidden.at[zz, 2 * kk + q // 2, q % 2]

    def slope_piece(q, from_m, from_p):
        start = q * quarter

        def tile(n, carry):
            cols = pl.ds(pl.multiple_of(n * tv, tv), tv)
            own = part[3, 2 * k + q // 2, q % 2, :, cols]
            pre = own.astype(F32) + from_m[:, cols].astype(F32) + from_p[:, cols].astype(F32)
            grad = og[start:start + quarter, cols].astype(F32) * gelu_slope(pre)
            hidden[z, 2 * k + q // 2, q % 2, :, cols] = grad.astype(BF16)
            return carry

        lax.fori_loop(0, hid // tv, tile, 0)
        here = piece(z, k, q)
        return send(here, here, sib), send(here, here, zp), send(here, here, zm)

    arrivals = (0, 2, 1, 3)
    own_sends = {}
    for j in range(2):
        acc_p[j].wait_recv()
        own_sends[j] = slope_piece(j, z_in_m.at[2, j], z_in_p.at[1, j])
        acc_m[j].wait_recv()
        own_sends[2 + j] = slope_piece(2 + j, z_in_m.at[1, j], z_in_p.at[2, j])

    def dot2(units):
        def tile(n, carry):
            cols = pl.ds(pl.multiple_of(n * tf, tf), tf)
            rows = [hidden[g, :, j].reshape(4 * hb, hid) for _, g, js in units for j in js]
            rows = rows[0] if len(rows) == 1 else jnp.concatenate(rows, axis=0)
            share = jnp.dot(rows, w_t[:, cols], preferred_element_type=F32).astype(BF16)
            at_row = 0
            for s, _, js in units:
                for j in js:
                    ig[s, j, :, :, cols] = share[at_row:at_row + 4 * hb].reshape(4, hb, tf)
                    at_row += 4 * hb
            return carry

        lax.fori_loop(0, feats // tf, tile, 0)

    def sum_into(out, terms):
        def tile(n, carry):
            cols = pl.ds(pl.multiple_of(n * tv, tv), tv)
            for p in range(out.shape[0]):
                for q in range(out.shape[1]):
                    total = terms[0][p, q, :, cols].astype(F32)
                    for term in terms[1:]:
                        total = total + term[p, q, :, cols].astype(F32)
                    out[p, q, :, cols] = total.astype(BF16)
            return carry

        lax.fori_loop(0, feats // tv, tile, 0)

    ha, hz = pl.ds(0, hb // 2), pl.ds(hb // 2, hb // 2)

    def y_start(s0, ns, j0, nj):
        ss, js = pl.ds(s0, ns), pl.ds(j0, nj)
        blk = lambda by, rows: ig.at[ss, js, nxt(y, by), rows]
        im = lambda n: y_in_m.at[n, ss, js]
        ip = lambda n: y_in_p.at[n, ss, js]
        op = send(blk(2, ha), im(0), yp)
        om = send(blk(2, hz), ip(0), ym)
        dp = send(blk(1, hz), im(1), yp)
        dm = send(blk(3, ha), ip(1), ym)
        return ss, js, blk, im, ip, op, om, dp, dm

    def y_middle(state):
        ss, js, blk, im, ip, op, om, dp, dm = state
        op.wait_recv()
        sum_into(blk(1, ha), [blk(1, ha), im(0)])
        ap = send(blk(1, ha), im(2), yp)
        om.wait_recv()
        sum_into(blk(3, hz), [blk(3, hz), ip(0)])
        am = send(blk(3, hz), ip(2), ym)
        return ss, js, blk, im, ip, (dp, dm, ap, am)

    def y_finish(state):
        ss, js, blk, im, ip, copies = state
        for copy in copies:
            copy.wait_recv()
        sum_into(xs.at[ss, js, ha], [blk(0, ha), im(2), ip(1)])
        sum_into(xs.at[ss, js, hz], [blk(0, hz), im(1), ip(2)])

    def x_copies(s, g, j0, nj):
        one, js = pl.ds(s, 1), pl.ds(j0, nj)
        mine_x = lambda rows: xs.at[one, js, rows]
        slot = lambda n: x_in.at[n, one, js]
        make = lambda rows, n, to: ready(mine_x(rows), slot(n), to)
        copies = (
            make(ha, 0, xp), make(hz, 0, xm), make(hz, 0, xp), make(ha, 1, xp), make(ha, 2, xm), make(hz, 3, xm)
        )
        return nxt(x, 4 - g), mine_x, slot, copies, (j0, nj)

    def x_start(s, g, j0, nj):
        state = x_copies(s, g, j0, nj)
        away, _, _, copies, _ = state

        @pl.when(away == 2)
        def _():
            copies[0].start()
            copies[1].start()

        @pl.when(away == 3)
        def _():
            copies[2].start()

        @pl.when(away == 1)
        def _():
            copies[4].start()

        return state

    def x_middle(state):
        away, mine_x, slot, copies, _ = state

        @pl.when(away == 3)
        def _():
            copies[0].wait_recv()
            sum_into(mine_x(ha), [mine_x(ha), slot(0)])
            copies[3].start()

        @pl.when(away == 1)
        def _():
            copies[1].wait_recv()
            sum_into(mine_x(hz), [mine_x(hz), slot(0)])
            copies[5].start()

    def x_finish(state):
        away, mine_x, slot, copies, (j0, nj) = state
        result = lambda rows: ig_ref.at[pl.ds(0, 1), pl.ds(j0, nj), rows]

        @pl.when(away == 0)
        def _():
            for n in (2, 3, 4, 5):
                copies[n].wait_recv()
            sum_into(result(ha), [mine_x(ha), slot(1), slot(2)])
            sum_into(result(hz), [mine_x(hz), slot(0), slot(3)])

        for role, used in ((2, (0, 1)), (3, (2, 3)), (1, (4, 5))):
            @pl.when(away == role)
            def _(used=used):
                for n in used:
                    copies[n].wait_send()

    def dot3(lo, hi, rows_of, first, later):
        span = 16 * hb

        def tile(n, carry):
            cols = pl.ds(pl.multiple_of(n * t3, t3), t3)
            units = jnp.concatenate([hidden[g, :, j, :, cols].reshape(4 * hb, t3) for g, j in rows_of], axis=0)
            total = jnp.dot(acts_t[:, first:first + span], units, preferred_element_type=F32)
            if later:
                total = total + wg_ref[:, cols].astype(F32)
            wg_ref[:, cols] = total.astype(BF16)
            return carry

        lax.fori_loop(lo, hi, tile, 0)

    blocks = hid // t3

    def early(lo, hi):
        dot3(lo * blocks // 6, hi * blocks // 6, tokens_of[:4], 0, False)

    def late(lo, hi):
        dot3(lo * blocks // 6, hi * blocks // 6, tokens_of[4:], 16 * hb, True)

    def neighbours(qs):
        copies = []
        for q in qs:
            own_sends[q][1].wait_recv()
            here = piece(low, k, q)
            if q < 2:
                fwd[q] = send(here, here, zp)
            copies.append(send(here, here, sib))
            own_sends[q][2].wait_recv()
            here = piece(high, k, q)
            if q >= 2:
                fwd[q] = send(here, here, zm)
            copies.append(send(here, here, sib))
        return copies

    def opposite(qs):
        copies = []
        for q in qs:
            fwd[q].wait_recv()
            here = piece(opp, k, q)
            copies.append(send(here, here, sib))
        return copies

    def arrived(copies):
        for copy in copies:
            copy.wait_recv()

    fwd = {}
    arrived([own_sends[q][0] for q in arrivals])
    dot2([(0, z, (0, 1))])
    y0 = y_start(0, 1, 0, 2)
    from_sib = neighbours((0, 2))
    y0 = y_middle(y0)
    arrived(from_sib)
    dot2([(1, low, (0,)), (2, high, (0,))])
    y1 = y_start(1, 2, 0, 1)
    y_finish(y0)
    x0 = x_start(0, z, 0, 2)
    early(0, 2)
    y1 = y_middle(y1)
    x_middle(x0)
    from_sib = neighbours((1,))
    early(2, 4)
    y_finish(y1)
    from_sib += neighbours((3,))
    x_finish(x0)
    early(4, 5)
    arrived(from_sib)
    dot2([(1, low, (1,)), (2, high, (1,))])
    y2 = y_start(1, 2, 1, 1)
    early(5, 6)
    from_sib = opposite((0, 2))
    y2 = y_middle(y2)
    arrived(from_sib)
    dot2([(3, opp, (0,))])
    y3 = y_start(3, 1, 0, 1)
    y_finish(y2)
    x1 = x_start(1, low, 0, 2)
    x2 = x_start(2, high, 0, 2)
    from_sib = opposite((1, 3))
    y3 = y_middle(y3)
    arrived(from_sib)
    dot2([(3, opp, (1,))])
    y4 = y_start(3, 1, 1, 1)
    x_middle(x1)
    x_middle(x2)
    y_finish(y3)
    x3 = x_start(3, opp, 0, 1)
    late(0, 1)
    y4 = y_middle(y4)
    x_middle(x3)
    late(1, 2)
    y_finish(y4)
    x4 = x_start(3, opp, 1, 1)
    late(2, 3)
    x_middle(x4)
    x_finish(x1)
    x_finish(x2)
    x_finish(x3)
    late(3, 6)
    x_finish(x4)

    for copy in sent:
        if copy is not None:
            copy.wait_send()


def write_out(ig_ref, wg_ref, ig_out, wg_out, sem):
    rows = wg_ref.shape[0] // 4
    copies = [pltpu.make_async_copy(ig_ref, ig_out, sem.at[4])]
    for n in range(4):
        part = pl.ds(n * rows, rows)
        copies.append(pltpu.make_async_copy(wg_ref.at[part], wg_out.at[part], sem.at[n]))
    for copy in copies:
        copy.start()
    for copy in copies:
        copy.wait()


def per_device(acts, up_weight, out_grad):
    tb, feats = acts.shape
    ob, hid = out_grad.shape
    tokens = 16 * tb
    hb = tb // 2
    vmem = lambda *shape: pltpu.VMEM(shape, BF16)
    in_hbm = pl.BlockSpec(memory_space=pltpu.HBM)
    in_vmem = pl.BlockSpec(memory_space=pltpu.VMEM)
    flops = 3 * 2 * tokens * feats * hid
    acts, up_weight, out_grad = (
        pltpu.with_memory_space_constraint(a, pltpu.HBM) for a in (acts, up_weight, out_grad)
    )
    input_grad, weight_grad = pl.pallas_call(
        kernel,
        out_shape=(
            vmem(1, 2, hb, feats),
            vmem(feats, hid),
        ),
        in_specs=[in_hbm] * 3,
        out_specs=(in_vmem, in_vmem),
        scratch_shapes=[
            vmem(4, 4, 2, hb, feats),
            vmem(hid, feats),
            vmem(ob, hid),
            vmem(feats, tokens),
            vmem(4, 4, 2, hb, hid),
            vmem(4, 2, 2, hb, hid),
            vmem(3, 2, hb, hid),
            vmem(3, 2, hb, hid),
            vmem(4, 4, 2, hb, hid),
            vmem(4, 2, 4, hb, feats),
            vmem(3, 4, 2, hb // 2, feats),
            vmem(3, 4, 2, hb // 2, feats),
            vmem(4, 2, hb, feats),
            vmem(4, 4, 2, hb // 2, feats),
            pltpu.SemaphoreType.DMA((9,)),
            pltpu.SemaphoreType.DMA((N_SEMS,)),
            pltpu.SemaphoreType.DMA((N_SEMS,)),
        ],
        compiler_params=pltpu.CompilerParams(
            collective_id=0, has_side_effects=True, vmem_limit_bytes=50 * 2**20
        ),
        cost_estimate=pl.CostEstimate(flops=flops, bytes_accessed=4 * feats * hid, transcendentals=2 * ob * hid),
    )(acts, up_weight, out_grad)
    return pl.pallas_call(
        write_out,
        out_shape=(
            jax.ShapeDtypeStruct((tb, feats), BF16),
            jax.ShapeDtypeStruct((feats, hid), BF16),
        ),
        in_specs=[in_vmem] * 2,
        out_specs=(in_hbm, in_hbm),
        scratch_shapes=[pltpu.SemaphoreType.DMA((5,))],
        compiler_params=pltpu.CompilerParams(vmem_limit_bytes=2 * 2**20),
        cost_estimate=pl.CostEstimate(flops=0, bytes_accessed=2 * feats * hid, transcendentals=0),
    )(input_grad.reshape(tb, feats), weight_grad)


def solution(mesh):
    in_specs = (P("col", "row"), P("row", "col"), P("row", "col"))
    out_specs = (P("col", "row"), P("row", "col"))
    return jax.shard_map(
        per_device, mesh=mesh, in_specs=in_specs, out_specs=out_specs, check_vma=False
    )
```

```python
import functools

import jax
import jax.numpy as jnp
from jax import lax
from jax.experimental import pallas as pl
from jax.experimental.pallas import tpu as pltpu
from jax.sharding import PartitionSpec as P

F32, BF16 = jnp.float32, jnp.bfloat16
MESH = pl.DeviceIdType.MESH
N_SEMS = 160


def gelu_slope(pre):
    cdf = 0.5 * (1.0 + lax.erf(pre * 0.7071067811865476))
    dens = jnp.exp(-0.5 * pre * pre) * 0.3989422804014327
    return cdf + pre * dens


def tile_of(size, want):
    return want if size % want == 0 else size


def kernel(
    acts_ref, w_ref, og_ref, ig_ref, wg_ref,
    acts, w_t, og, acts_t, part, sib_in, z_in, hidden, ig, y_in_m, y_in_p, xs, x_in,
    local_sem, send_sem, recv_sem,
):
    tb, feats = acts_ref.shape
    ob, hid = og_ref.shape
    quarter = ob // 4
    tv, tn, t3 = tile_of(hid // 2, 512), tile_of(hid // 2, 768), tile_of(hid, 256)
    tf, tm = tile_of(feats, 768), tile_of(feats, 256)
    w = wg_ref

    row, col = lax.axis_index("row"), lax.axis_index("col")
    z, k = lax.div(row, 2), lax.rem(row, 2)
    x, y = lax.div(col, 4), lax.rem(col, 4)
    nxt = lambda v, by: lax.rem(v + by, 4)
    sib = {"row": z * 2 + (1 - k)}
    zp, zm = {"row": nxt(z, 1) * 2 + k}, {"row": nxt(z, 3) * 2 + k}
    xp, xm = {"col": nxt(x, 1) * 4 + y}, {"col": nxt(x, 3) * 4 + y}
    yp, ym = {"col": x * 4 + nxt(y, 1)}, {"col": x * 4 + nxt(y, 3)}

    made = []

    def link(src, dst, to, always=True):
        i = len(made)
        copy = pltpu.make_async_remote_copy(
            src_ref=src, dst_ref=dst, send_sem=send_sem.at[i], recv_sem=recv_sem.at[i],
            device_id=to, device_id_type=MESH,
        )
        made.append(copy if always else None)
        return copy

    def at_turn(n, turn, *work):
        @pl.when(n == turn)
        def _():
            for do in work:
                do()

    def arrived(copies):
        for copy in copies:
            copy.wait_recv()

    hb = tb // 2

    def step_of(group):
        away = nxt(group, 4 - z)
        odd, far = lax.rem(away, 2), lax.div(away, 2)
        return odd * (2 - lax.rem(far + y, 2)) + (1 - odd) * (3 - 3 * far)

    barrier = pltpu.get_barrier_semaphore()
    for to in (sib, zp, zm, xp, xm, yp, ym):
        pl.semaphore_signal(barrier, inc=1, device_id=to, device_id_type=MESH)
    load_acts = [
        pltpu.make_async_copy(acts_ref.at[pl.ds(j * hb, hb)], acts.at[step_of(x), y, j], local_sem.at[j])
        for j in range(2)
    ]
    load_og = pltpu.make_async_copy(og_ref, og, local_sem.at[2])
    load_w = [
        pltpu.make_async_copy(w_ref.at[pl.ds(m * tm, tm)], w.at[pl.ds(m * tm, tm)], local_sem.at[3 + m])
        for m in range(feats // tm)
    ]
    for load in (*load_acts, *load_w, load_og):
        load.start()
    for load in load_acts:
        load.wait()
    pl.semaphore_wait(barrier, 7)

    ha, hz = pl.ds(0, hb // 2), pl.ds(hb // 2, hb // 2)

    class Gather:
        def __init__(self, block, to_p, to_m):
            a, b = (lambda by: block(by, ha)), (lambda by: block(by, hz))
            self.pa, self.mb = link(a(0), a(0), to_p), link(b(0), b(0), to_m)
            self.pb, self.ma = link(b(0), b(0), to_p), link(a(0), a(0), to_m)
            self.fa, self.fb = link(a(3), a(3), to_p), link(b(1), b(1), to_m)

        def start(self):
            for copy in (self.pa, self.mb, self.pb, self.ma):
                copy.start()

        def forward(self):
            self.pa.wait_recv()
            self.fa.start()
            self.mb.wait_recv()
            self.fb.start()

        def finish(self):
            arrived((self.pb, self.ma, self.fa, self.fb))

    def x_gather(j):
        return Gather(lambda by, rows: acts.at[step_of(nxt(x, by)), y, j, rows], xp, xm)

    def y_gather(s, j0, nj):
        return Gather(lambda by, rows: acts.at[s, nxt(y, by), pl.ds(j0, nj), rows], yp, ym)

    gx = [x_gather(0), x_gather(1)]
    gy = [y_gather(0, 0, 1), y_gather(0, 1, 1), y_gather(1, 0, 2), y_gather(2, 0, 2), y_gather(3, 0, 2)]

    def turn_w(m):
        to = pl.ds(pl.multiple_of(m * tm, tm), tm)

        def tile(n, carry):
            cols = pl.ds(pl.multiple_of(n * tm, tm), tm)
            w_t[cols, to] = w[to, cols].T
            return carry

        lax.fori_loop(0, hid // tm, tile, 0)

    theirs = lambda s, js, cols: part.at[s, pl.ds(2 * (1 - k), 2), js, :, cols]
    every = pl.ds(0, hid)
    sib_first = len(made)
    for s, j0, nj in ((0, 0, 1), (0, 1, 1), (1, 0, 2), (2, 0, 2), (3, 0, 2)):
        js = pl.ds(j0, nj)
        link(theirs(s, js, every), sib_in.at[s, :, js, :, every], sib)

    def add_into(dst, src):
        def tile(n, carry):
            cols = pl.ds(pl.multiple_of(n * tv, tv), tv)
            for j in range(dst.shape[0]):
                total = dst[j, :, cols].astype(F32) + src[j, :, cols].astype(F32)
                dst[j, :, cols] = total.astype(BF16)
            return carry

        lax.fori_loop(0, hid // tv, tile, 0)

    def dot1(s, j0, nj, sem, between):
        js = pl.ds(j0, nj)

        def to_sib(cols):
            return pltpu.make_async_remote_copy(
                src_ref=theirs(s, js, cols), dst_ref=sib_in.at[s, :, js, :, cols],
                send_sem=send_sem.at[sem], recv_sem=recv_sem.at[sem], device_id=sib, device_id_type=MESH,
            )

        def tile(n, carry):
            cols = pl.ds(pl.multiple_of(n * tn, tn), tn)
            share = jnp.dot(
                acts[s, :, js].reshape(4 * nj * hb, feats), w[:, cols], preferred_element_type=F32
            )
            part[s, :, js, :, cols] = share.astype(BF16).reshape(4, nj, hb, tn)
            to_sib(cols).start()
            return carry

        lax.fori_loop(0, hid // tn, tile, 0)
        between()
        to_sib(every).wait_recv()

        def own(way, carry):
            add_into(part.at[s, 2 * k + way, js], sib_in.at[s, way, js])
            return carry

        lax.fori_loop(0, 2, own, 0)

    mine = lambda s, way, j: part.at[s, 2 * k + way, j]
    to_z, back_z = (zp, zm), (zm, zp)
    hop = [[link(mine(0, way, j), z_in.at[way, 0, j], to_z[way]) for j in range(2)] for way in range(2)]
    both = pl.ds(0, 2)
    direct = [link(mine(1, way, both), z_in.at[1 - way, 1], back_z[way]) for way in range(2)]
    acc = [[link(mine(2, way, j), z_in.at[way, 2, j], to_z[way]) for j in range(2)] for way in range(2)]

    gx[0].start()
    load_w[0].wait()
    turn_w(0)
    gx[0].forward()
    gx[1].start()
    load_w[1].wait()
    turn_w(1)
    gx[0].finish()
    gy[0].start()
    load_w[2].wait()
    turn_w(2)
    gx[1].forward()
    gy[0].forward()
    load_w[3].wait()
    turn_w(3)
    gx[1].finish()
    gy[1].start()
    for load in load_w[4:]:
        load.wait()

    def half_step(u, carry):
        at_turn(u, 0, gy[0].finish)
        at_turn(u, 1, gy[1].finish)

        def between():
            at_turn(u, 0, gy[1].forward, gy[2].start)
            at_turn(u, 1, gy[2].forward, gy[3].start)

        dot1(0, u, 1, sib_first + u, between)
        for j in range(2):
            at_turn(u, j, hop[0][j].start, hop[1][j].start)
        return carry

    lax.fori_loop(0, 2, half_step, 0)

    def accumulate():
        def one(n, carry):
            j, way = lax.div(n, 2), lax.rem(n, 2)
            for i in range(4):
                at_turn(n, i, hop[i % 2][i // 2].wait_recv)
            add_into(part.at[2, 2 * k + way, pl.ds(j, 1)], z_in.at[way, 0, pl.ds(j, 1)])
            for i in range(4):
                at_turn(n, i, acc[i % 2][i // 2].start)
            return carry

        lax.fori_loop(0, 4, one, 0)

    def full_step(s, carry):
        for i in (1, 2, 3):
            at_turn(s, i, gy[1 + i].finish)

        def between():
            at_turn(s, 1, gy[3].forward, gy[4].start)
            at_turn(s, 2, gy[4].forward)

        dot1(s, 0, 2, sib_first + 1 + s, between)
        at_turn(s, 1, direct[0].start, direct[1].start)
        at_turn(s, 2, accumulate)
        return carry

    lax.fori_loop(1, 4, full_step, 0)
    load_og.wait()

    low, high, opp = nxt(z, 3), nxt(z, 1), nxt(z, 2)
    tokens_of = [(z, 0), (z, 1), (low, 0), (high, 0), (low, 1), (high, 1), (opp, 0), (opp, 1)]
    held_in = [(3, 3), (3, 3), (1, 2), (2, 1), (1, 2), (2, 1), (0, 0), (0, 0)]

    def turn(n, carry):
        cols = pl.ds(pl.multiple_of(n * tm, tm), tm)
        for t, steps in enumerate(held_in):
            rows = [acts[steps[b % 2], b, tokens_of[t][1], :, cols] for b in range(4)]
            acts_t[cols, t * 4 * hb:(t + 1) * 4 * hb] = jnp.concatenate(rows, axis=0).T
        return carry

    lax.fori_loop(0, feats // tm, turn, 0)

    def turn_rest(m, carry):
        turn_w(m)
        return carry

    lax.fori_loop(4, feats // tm, turn_rest, 0)

    piece = lambda zz, q: hidden.at[zz, 2 * k + q // 2, q % 2]
    own = [[link(piece(z, q), piece(z, q), to) for to in (sib, zp, zm)] for q in range(4)]
    fwd = [link(piece((low, high)[q // 2], q), piece((low, high)[q // 2], q), to_z[q // 2]) for q in range(4)]
    low_sib = [link(piece(low, q), piece(low, q), sib) for q in range(4)]
    high_sib = [link(piece(high, q), piece(high, q), sib) for q in range(4)]
    opp_sib = [link(piece(opp, q), piece(opp, q), sib) for q in range(4)]
    arrived(direct)

    def slope_piece(n, carry):
        j, way = lax.div(n, 2), lax.rem(n, 2)
        for i in range(4):
            at_turn(n, i, acc[i % 2][i // 2].wait_recv)
        start = pl.multiple_of((2 * way + j) * quarter, quarter)

        def tile(m, carry):
            cols = pl.ds(pl.multiple_of(m * tv, tv), tv)
            pre = part[3, 2 * k + way, j, :, cols].astype(F32)
            pre = pre + z_in[way, 2, j, :, cols].astype(F32) + z_in[1 - way, 1, j, :, cols].astype(F32)
            grad = og[pl.ds(start, quarter), cols].astype(F32) * gelu_slope(pre)
            hidden[z, 2 * k + way, j, :, cols] = grad.astype(BF16)
            return carry

        lax.fori_loop(0, hid // tv, tile, 0)
        for i in range(4):
            at_turn(n, i, *(copy.start for copy in own[2 * (i % 2) + i // 2]))
        return carry

    lax.fori_loop(0, 4, slope_piece, 0)

    def dot2(units):
        def tile(n, carry):
            cols = pl.ds(pl.multiple_of(n * tf, tf), tf)
            rows = [hidden[g, :, j].reshape(4 * hb, hid) for _, g, j in units]
            rows = rows[0] if len(rows) == 1 else jnp.concatenate(rows, axis=0)
            share = jnp.dot(rows, w_t[:, cols], preferred_element_type=F32).astype(BF16)
            for i, (s, _, j) in enumerate(units):
                ig[s, j, :, :, cols] = share[i * 4 * hb:(i + 1) * 4 * hb].reshape(4, hb, tf)
            return carry

        lax.fori_loop(0, feats // tf, tile, 0)

    def sum_into(out, terms):
        def tile(n, carry):
            cols = pl.ds(pl.multiple_of(n * tv, tv), tv)
            for p in range(out.shape[0]):
                for q in range(out.shape[1]):
                    total = terms[0][p, q, :, cols].astype(F32)
                    for term in terms[1:]:
                        total = total + term[p, q, :, cols].astype(F32)
                    out[p, q, :, cols] = total.astype(BF16)
            return carry

        lax.fori_loop(0, feats // tv, tile, 0)

    class ScatterY:
        def __init__(self, s0, ns, j0, nj):
            ss, js = pl.ds(s0, ns), pl.ds(j0, nj)
            self.blk = lambda by, rows: ig.at[ss, js, nxt(y, by), rows]
            self.im, self.ip = (lambda n: y_in_m.at[n, ss, js]), (lambda n: y_in_p.at[n, ss, js])
            self.out = lambda rows: xs.at[ss, js, rows]
            blk, im, ip = self.blk, self.im, self.ip
            self.op, self.om = link(blk(2, ha), im(0), yp), link(blk(2, hz), ip(0), ym)
            self.dp, self.dm = link(blk(1, hz), im(1), yp), link(blk(3, ha), ip(1), ym)
            self.ap, self.am = link(blk(1, ha), im(2), yp), link(blk(3, hz), ip(2), ym)

        def start(self):
            for copy in (self.op, self.om, self.dp, self.dm):
                copy.start()

        def middle(self):
            self.op.wait_recv()
            sum_into(self.blk(1, ha), [self.blk(1, ha), self.im(0)])
            self.ap.start()
            self.om.wait_recv()
            sum_into(self.blk(3, hz), [self.blk(3, hz), self.ip(0)])
            self.am.start()

        def finish(self):
            arrived((self.dp, self.dm, self.ap, self.am))
            sum_into(self.out(ha), [self.blk(0, ha), self.im(2), self.ip(1)])
            sum_into(self.out(hz), [self.blk(0, hz), self.im(1), self.ip(2)])

    class ReduceX:
        def __init__(self, s, g, j0, nj):
            one, js = pl.ds(s, 1), pl.ds(j0, nj)
            self.away = nxt(x, 4 - g)
            self.src = lambda rows: xs.at[one, js, rows]
            self.slot = lambda n: x_in.at[n, one, js]
            self.out = lambda rows: ig_ref.at[pl.ds(0, 1), js, rows]
            make = lambda rows, n, to: link(self.src(rows), self.slot(n), to, False)
            self.copies = (
                make(ha, 0, xp), make(hz, 0, xm), make(hz, 0, xp), make(ha, 1, xp), make(ha, 2, xm), make(hz, 3, xm)
            )

        def start(self):
            c = self.copies
            at_turn(self.away, 2, c[0].start, c[1].start)
            at_turn(self.away, 3, c[2].start)
            at_turn(self.away, 1, c[4].start)

        def middle(self):
            c, src, slot = self.copies, self.src, self.slot
            add = lambda rows: sum_into(src(rows), [src(rows), slot(0)])
            at_turn(self.away, 3, c[0].wait_recv, lambda: add(ha), c[3].start)
            at_turn(self.away, 1, c[1].wait_recv, lambda: add(hz), c[5].start)

        def finish(self):
            c, src, slot, out = self.copies, self.src, self.slot, self.out

            def total():
                arrived(c[2:])
                sum_into(out(ha), [src(ha), slot(1), slot(2)])
                sum_into(out(hz), [src(hz), slot(0), slot(3)])

            at_turn(self.away, 0, total)
            at_turn(self.away, 2, c[0].wait_send, c[1].wait_send)
            at_turn(self.away, 3, c[2].wait_send, c[3].wait_send)
            at_turn(self.away, 1, c[4].wait_send, c[5].wait_send)

    def dot3(rows_of, first, later, before):
        span = 16 * hb

        def tile(n, carry):
            before(n)
            cols = pl.ds(pl.multiple_of(n * t3, t3), t3)
            units = jnp.concatenate([hidden[g, :, j, :, cols].reshape(4 * hb, t3) for g, j in rows_of], axis=0)
            total = jnp.dot(acts_t[:, first:first + span], units, preferred_element_type=F32)
            if later:
                total = total + wg_ref[:, cols].astype(F32)
            wg_ref[:, cols] = total.astype(BF16)
            return carry

        lax.fori_loop(0, hid // t3, tile, 0)

    def neighbours(*qs):
        def work():
            for q in qs:
                own[q][1].wait_recv()
                if q < 2:
                    fwd[q].start()
                low_sib[q].start()
                own[q][2].wait_recv()
                if q >= 2:
                    fwd[q].start()
                high_sib[q].start()
        return work

    def opposite(*qs):
        def work():
            for q in qs:
                fwd[q].wait_recv()
                opp_sib[q].start()
        return work

    def from_sib(*copies):
        return lambda: arrived(copies)

    ys = [ScatterY(0, 1, 0, 2), ScatterY(1, 2, 0, 1), ScatterY(1, 2, 1, 1), ScatterY(3, 1, 0, 1), ScatterY(3, 1, 1, 1)]
    xr = [
        ReduceX(0, z, 0, 2), ReduceX(1, low, 0, 2), ReduceX(2, high, 0, 2), ReduceX(3, opp, 0, 1), ReduceX(3, opp, 1, 1)
    ]

    def early():
        def before(n):
            at_turn(n, 4, ys[1].middle, xr[0].middle, neighbours(1))
            at_turn(n, 8, ys[1].finish, neighbours(3))
            at_turn(n, 10, xr[0].finish)

        dot3(tokens_of[:4], 0, False, before)

    def batch(n, carry):
        other, j = lax.div(n + 1, 2), lax.div(n, 2)
        at_turn(n, 0, from_sib(*(own[q][0] for q in range(4))))
        at_turn(n, 1, neighbours(0, 2), ys[0].middle, from_sib(low_sib[0], low_sib[2], high_sib[0], high_sib[2]))
        at_turn(n, 2, from_sib(low_sib[1], low_sib[3], high_sib[1], high_sib[3]))
        dot2([(other, nxt(z, 3 * other), j), (2 * other, nxt(z, other), 1 - other + j)])
        at_turn(n, 0, ys[0].start)
        at_turn(n, 1, ys[1].start, ys[0].finish, xr[0].start, early)
        at_turn(n, 2, ys[2].start)
        return carry

    def last_batch(j, carry):
        at_turn(j, 0, opposite(0, 2), ys[2].middle, from_sib(opp_sib[0], opp_sib[2]))
        at_turn(
            j, 1, ys[2].finish, xr[1].start, xr[2].start, opposite(1, 3), ys[3].middle,
            from_sib(opp_sib[1], opp_sib[3]),
        )
        dot2([(3, opp, j)])
        at_turn(j, 0, ys[3].start)
        at_turn(j, 1, ys[4].start)
        return carry

    lax.fori_loop(0, 3, batch, 0)
    lax.fori_loop(0, 2, last_batch, 0)
    xr[1].middle()
    xr[2].middle()
    ys[3].finish()
    xr[3].start()

    def before_late(n):
        at_turn(n, 2, ys[4].middle, xr[3].middle)
        at_turn(n, 4, ys[4].finish, xr[4].start)
        at_turn(n, 6, xr[4].middle, xr[1].finish, xr[2].finish, xr[3].finish)

    dot3(tokens_of[4:], 16 * hb, True, before_late)
    xr[4].finish()

    for copy in made:
        if copy is not None:
            copy.wait_send()


def write_out(ig_ref, wg_ref, ig_out, wg_out, sem):
    rows = wg_ref.shape[0] // 4
    copies = [pltpu.make_async_copy(ig_ref, ig_out, sem.at[4])]
    for n in range(4):
        part = pl.ds(n * rows, rows)
        copies.append(pltpu.make_async_copy(wg_ref.at[part], wg_out.at[part], sem.at[n]))
    for copy in copies:
        copy.start()
    for copy in copies:
        copy.wait()


def per_device(acts, up_weight, out_grad):
    tb, feats = acts.shape
    ob, hid = out_grad.shape
    tokens = 16 * tb
    hb = tb // 2
    vmem = lambda *shape: pltpu.VMEM(shape, BF16)
    in_hbm = pl.BlockSpec(memory_space=pltpu.HBM)
    in_vmem = pl.BlockSpec(memory_space=pltpu.VMEM)
    flops = 3 * 2 * tokens * feats * hid
    acts, up_weight, out_grad = (
        pltpu.with_memory_space_constraint(a, pltpu.HBM) for a in (acts, up_weight, out_grad)
    )
    input_grad, weight_grad = pl.pallas_call(
        kernel,
        out_shape=(
            vmem(1, 2, hb, feats),
            vmem(feats, hid),
        ),
        in_specs=[in_hbm] * 3,
        out_specs=(in_vmem, in_vmem),
        scratch_shapes=[
            vmem(4, 4, 2, hb, feats),
            vmem(hid, feats),
            vmem(ob, hid),
            vmem(feats, tokens),
            vmem(4, 4, 2, hb, hid),
            vmem(4, 2, 2, hb, hid),
            vmem(2, 3, 2, hb, hid),
            vmem(4, 4, 2, hb, hid),
            vmem(4, 2, 4, hb, feats),
            vmem(3, 4, 2, hb // 2, feats),
            vmem(3, 4, 2, hb // 2, feats),
            vmem(4, 2, hb, feats),
            vmem(4, 4, 2, hb // 2, feats),
            pltpu.SemaphoreType.DMA((9,)),
            pltpu.SemaphoreType.DMA((N_SEMS,)),
            pltpu.SemaphoreType.DMA((N_SEMS,)),
        ],
        compiler_params=pltpu.CompilerParams(
            collective_id=0, has_side_effects=True, vmem_limit_bytes=50 * 2**20
        ),
        cost_estimate=pl.CostEstimate(flops=flops, bytes_accessed=4 * feats * hid, transcendentals=2 * ob * hid),
    )(acts, up_weight, out_grad)
    return pl.pallas_call(
        write_out,
        out_shape=(
            jax.ShapeDtypeStruct((tb, feats), BF16),
            jax.ShapeDtypeStruct((feats, hid), BF16),
        ),
        in_specs=[in_vmem] * 2,
        out_specs=(in_hbm, in_hbm),
        scratch_shapes=[pltpu.SemaphoreType.DMA((5,))],
        compiler_params=pltpu.CompilerParams(vmem_limit_bytes=2 * 2**20),
        cost_estimate=pl.CostEstimate(flops=0, bytes_accessed=2 * feats * hid, transcendentals=0),
    )(input_grad.reshape(tb, feats), weight_grad)


def solution(mesh):
    in_specs = (P("col", "row"), P("row", "col"), P("row", "col"))
    out_specs = (P("col", "row"), P("row", "col"))
    return jax.shard_map(
        per_device, mesh=mesh, in_specs=in_specs, out_specs=out_specs, check_vma=False
    )
```

```python
import functools

import jax
import jax.numpy as jnp
from jax import lax
from jax.experimental import pallas as pl
from jax.experimental.pallas import tpu as pltpu
from jax.sharding import PartitionSpec as P

F32, BF16 = jnp.float32, jnp.bfloat16
MESH = pl.DeviceIdType.MESH
N_SEMS = 160


def gelu_slope(pre):
    cdf = 0.5 * (1.0 + lax.erf(pre * 0.7071067811865476))
    dens = jnp.exp(-0.5 * pre * pre) * 0.3989422804014327
    return cdf + pre * dens


def tile_of(size, want):
    return want if size % want == 0 else size


def kernel(
    acts_ref, w_ref, og_ref, ig_ref, wg_ref,
    acts, w_t, og, acts_t, part, sib_in, z_in_m, z_in_p, hidden, ig, y_in_m, y_in_p, xs, x_in,
    local_sem, send_sem, recv_sem,
):
    tb, feats = acts_ref.shape
    ob, hid = og_ref.shape
    quarter = ob // 4
    tv, tn, t3 = tile_of(hid // 2, 512), tile_of(hid // 2, 768), tile_of(hid, 256)
    tf, tm = tile_of(feats, 768), tile_of(feats, 256)
    w = wg_ref

    row, col = lax.axis_index("row"), lax.axis_index("col")
    z, k = lax.div(row, 2), lax.rem(row, 2)
    x, y = lax.div(col, 4), lax.rem(col, 4)
    nxt = lambda v, by: lax.rem(v + by, 4)
    sib = {"row": z * 2 + (1 - k)}
    zp, zm = {"row": nxt(z, 1) * 2 + k}, {"row": nxt(z, 3) * 2 + k}
    xp, xm = {"col": nxt(x, 1) * 4 + y}, {"col": nxt(x, 3) * 4 + y}
    yp, ym = {"col": x * 4 + nxt(y, 1)}, {"col": x * 4 + nxt(y, 3)}

    sent = []

    def ready(src, dst, to):
        i = len(sent)
        sent.append(None)
        return pltpu.make_async_remote_copy(
            src_ref=src, dst_ref=dst, send_sem=send_sem.at[i], recv_sem=recv_sem.at[i],
            device_id=to, device_id_type=MESH,
        )

    def send(src, dst, to):
        copy = ready(src, dst, to)
        copy.start()
        sent[-1] = copy
        return copy

    hb = tb // 2

    def step_of(group):
        away = nxt(group, 4 - z)
        odd, far = lax.rem(away, 2), lax.div(away, 2)
        return odd * (2 - lax.rem(far + y, 2)) + (1 - odd) * (3 - 3 * far)

    barrier = pltpu.get_barrier_semaphore()
    for to in (sib, zp, zm, xp, xm, yp, ym):
        pl.semaphore_signal(barrier, inc=1, device_id=to, device_id_type=MESH)
    load_acts = [
        pltpu.make_async_copy(acts_ref.at[pl.ds(j * hb, hb)], acts.at[step_of(x), y, j], local_sem.at[j])
        for j in range(2)
    ]
    load_og = pltpu.make_async_copy(og_ref, og, local_sem.at[2])
    load_w = [
        pltpu.make_async_copy(w_ref.at[pl.ds(m * tm, tm)], w.at[pl.ds(m * tm, tm)], local_sem.at[3 + m])
        for m in range(feats // tm)
    ]
    for load in (*load_acts, *load_w, load_og):
        load.start()
    for load in load_acts:
        load.wait()
    pl.semaphore_wait(barrier, 7)

    low16, high16 = pl.ds(0, hb // 2), pl.ds(hb // 2, hb // 2)

    def ag_start(block, to_p, to_m):
        a = lambda by: block(by, low16)
        b = lambda by: block(by, high16)
        pa = send(a(0), a(0), to_p)
        mb = send(b(0), b(0), to_m)
        pb = send(b(0), b(0), to_p)
        ma = send(a(0), a(0), to_m)
        return a, b, pa, mb, pb, ma, to_p, to_m

    def ag_forward(state):
        a, b, pa, mb, pb, ma, to_p, to_m = state
        pa.wait_recv()
        fa = send(a(3), a(3), to_p)
        mb.wait_recv()
        fb = send(b(1), b(1), to_m)
        return pb, ma, fa, fb

    def ag_finish(copies):
        for copy in copies:
            copy.wait_recv()

    def x_gather(j):
        return ag_start(lambda by, rows: acts.at[step_of(nxt(x, by)), y, j, rows], xp, xm)

    def y_gather(s, j0, nj):
        return ag_start(lambda by, rows: acts.at[s, nxt(y, by), pl.ds(j0, nj), rows], yp, ym)

    def turn_w(m, loaded=False):
        if not loaded:
            load_w[m].wait()

        def tile(n, carry):
            cols = pl.ds(pl.multiple_of(n * tm, tm), tm)
            w_t[cols, m * tm:(m + 1) * tm] = w[m * tm:(m + 1) * tm, cols].T
            return carry

        lax.fori_loop(0, hid // tm, tile, 0)

    def dot1(s, j0, nj):
        js = pl.ds(j0, nj)
        sem = len(sent)

        def to_sib(cols):
            return pltpu.make_async_remote_copy(
                src_ref=part.at[s, pl.ds(2 * (1 - k), 2), js, :, cols], dst_ref=sib_in.at[s, :, js, :, cols],
                send_sem=send_sem.at[sem], recv_sem=recv_sem.at[sem], device_id=sib, device_id_type=MESH,
            )

        def tile(n, carry):
            cols = pl.ds(pl.multiple_of(n * tn, tn), tn)
            share = jnp.dot(
                acts[s, :, js].reshape(4 * nj * hb, feats), w[:, cols], preferred_element_type=F32
            )
            part[s, :, js, :, cols] = share.astype(BF16).reshape(4, nj, hb, tn)
            to_sib(cols).start()
            return carry

        lax.fori_loop(0, hid // tn, tile, 0)
        sent.append(to_sib(pl.ds(0, hid)))
        return sent[-1]

    def add_into(dst, src):
        def tile(n, carry):
            cols = pl.ds(pl.multiple_of(n * tv, tv), tv)
            for j in range(dst.shape[0]):
                total = dst[j, :, cols].astype(F32) + src[j, :, cols].astype(F32)
                dst[j, :, cols] = total.astype(BF16)
            return carry

        lax.fori_loop(0, hid // tv, tile, 0)

    def core_sum(s, copy, j0, nj):
        copy.wait_recv()
        js = pl.ds(j0, nj)
        for way in range(2):
            add_into(part.at[s, 2 * k + way, js], sib_in.at[s, way, js])

    mine = lambda s, way: part.at[s, 2 * k + way]
    gx = x_gather(0)
    turn_w(0)
    gx0 = ag_forward(gx)
    gx = x_gather(1)
    turn_w(1)
    ag_finish(gx0)
    g = y_gather(0, 0, 1)
    turn_w(2)
    gx1 = ag_forward(gx)
    g0 = ag_forward(g)
    turn_w(3)
    ag_finish(gx1)
    g = y_gather(0, 1, 1)
    for load in load_w[4:]:
        load.wait()
    ag_finish(g0)
    opp_p, opp_m = [], []
    c = dot1(0, 0, 1)
    g0 = ag_forward(g)
    g = y_gather(1, 0, 2)
    core_sum(0, c, 0, 1)
    opp_p.append(send(mine(0, 0).at[0], z_in_m.at[0, 0], zp))
    opp_m.append(send(mine(0, 1).at[0], z_in_p.at[0, 0], zm))
    ag_finish(g0)
    c = dot1(0, 1, 1)
    g0 = ag_forward(g)
    g = y_gather(2, 0, 2)
    core_sum(0, c, 1, 1)
    opp_p.append(send(mine(0, 0).at[1], z_in_m.at[0, 1], zp))
    opp_m.append(send(mine(0, 1).at[1], z_in_p.at[0, 1], zm))
    ag_finish(g0)
    c = dot1(1, 0, 2)
    g0 = ag_forward(g)
    g = y_gather(3, 0, 2)
    core_sum(1, c, 0, 2)
    dir_p = send(mine(1, 1), z_in_m.at[1], zp)
    dir_m = send(mine(1, 0), z_in_p.at[1], zm)
    ag_finish(g0)
    c = dot1(2, 0, 2)
    g0 = ag_forward(g)
    core_sum(2, c, 0, 2)
    acc_p, acc_m = [], []
    for j in range(2):
        one = pl.ds(j, 1)
        opp_p[j].wait_recv()
        add_into(mine(2, 0).at[one], z_in_m.at[0, one])
        acc_p.append(send(mine(2, 0).at[j], z_in_m.at[2, j], zp))
        opp_m[j].wait_recv()
        add_into(mine(2, 1).at[one], z_in_p.at[0, one])
        acc_m.append(send(mine(2, 1).at[j], z_in_p.at[2, j], zm))
    ag_finish(g0)
    c = dot1(3, 0, 2)
    core_sum(3, c, 0, 2)
    load_og.wait()

    low, high, opp = nxt(z, 3), nxt(z, 1), nxt(z, 2)
    tokens_of = [(z, 0), (z, 1), (low, 0), (high, 0), (low, 1), (high, 1), (opp, 0), (opp, 1)]
    held_in = [(3, 3), (3, 3), (1, 2), (2, 1), (1, 2), (2, 1), (0, 0), (0, 0)]

    def turn(n, carry):
        cols = pl.ds(pl.multiple_of(n * tm, tm), tm)
        for t, steps in enumerate(held_in):
            rows = [acts[steps[b % 2], b, tokens_of[t][1], :, cols] for b in range(4)]
            acts_t[cols, t * 4 * hb:(t + 1) * 4 * hb] = jnp.concatenate(rows, axis=0).T
        return carry

    lax.fori_loop(0, feats // tm, turn, 0)
    for m in range(4, feats // tm):
        turn_w(m, True)

    dir_p.wait_recv()
    dir_m.wait_recv()
    piece = lambda zz, kk, q: hidden.at[zz, 2 * kk + q // 2, q % 2]

    def slope_piece(q, from_m, from_p):
        start = q * quarter

        def tile(n, carry):
            cols = pl.ds(pl.multiple_of(n * tv, tv), tv)
            own = part[3, 2 * k + q // 2, q % 2, :, cols]
            pre = own.astype(F32) + from_m[:, cols].astype(F32) + from_p[:, cols].astype(F32)
            grad = og[start:start + quarter, cols].astype(F32) * gelu_slope(pre)
            hidden[z, 2 * k + q // 2, q % 2, :, cols] = grad.astype(BF16)
            return carry

        lax.fori_loop(0, hid // tv, tile, 0)
        here = piece(z, k, q)
        return send(here, here, sib), send(here, here, zp), send(here, here, zm)

    arrivals = (0, 2, 1, 3)
    own_sends = {}
    for j in range(2):
        acc_p[j].wait_recv()
        own_sends[j] = slope_piece(j, z_in_m.at[2, j], z_in_p.at[1, j])
        acc_m[j].wait_recv()
        own_sends[2 + j] = slope_piece(2 + j, z_in_m.at[1, j], z_in_p.at[2, j])

    def dot2(units):
        def tile(n, carry):
            cols = pl.ds(pl.multiple_of(n * tf, tf), tf)
            rows = [hidden[g, :, j].reshape(4 * hb, hid) for _, g, js in units for j in js]
            rows = rows[0] if len(rows) == 1 else jnp.concatenate(rows, axis=0)
            share = jnp.dot(rows, w_t[:, cols], preferred_element_type=F32).astype(BF16)
            at_row = 0
            for s, _, js in units:
                for j in js:
                    ig[s, j, :, :, cols] = share[at_row:at_row + 4 * hb].reshape(4, hb, tf)
                    at_row += 4 * hb
            return carry

        lax.fori_loop(0, feats // tf, tile, 0)

    def sum_into(out, terms):
        def tile(n, carry):
            cols = pl.ds(pl.multiple_of(n * tv, tv), tv)
            for p in range(out.shape[0]):
                for q in range(out.shape[1]):
                    total = terms[0][p, q, :, cols].astype(F32)
                    for term in terms[1:]:
                        total = total + term[p, q, :, cols].astype(F32)
                    out[p, q, :, cols] = total.astype(BF16)
            return carry

        lax.fori_loop(0, feats // tv, tile, 0)

    ha, hz = pl.ds(0, hb // 2), pl.ds(hb // 2, hb // 2)

    def y_start(s0, ns, j0, nj):
        ss, js = pl.ds(s0, ns), pl.ds(j0, nj)
        blk = lambda by, rows: ig.at[ss, js, nxt(y, by), rows]
        im = lambda n: y_in_m.at[n, ss, js]
        ip = lambda n: y_in_p.at[n, ss, js]
        op = send(blk(2, ha), im(0), yp)
        om = send(blk(2, hz), ip(0), ym)
        dp = send(blk(1, hz), im(1), yp)
        dm = send(blk(3, ha), ip(1), ym)
        return ss, js, blk, im, ip, op, om, dp, dm

    def y_middle(state):
        ss, js, blk, im, ip, op, om, dp, dm = state
        op.wait_recv()
        sum_into(blk(1, ha), [blk(1, ha), im(0)])
        ap = send(blk(1, ha), im(2), yp)
        om.wait_recv()
        sum_into(blk(3, hz), [blk(3, hz), ip(0)])
        am = send(blk(3, hz), ip(2), ym)
        return ss, js, blk, im, ip, (dp, dm, ap, am)

    def y_finish(state):
        ss, js, blk, im, ip, copies = state
        for copy in copies:
            copy.wait_recv()
        sum_into(xs.at[ss, js, ha], [blk(0, ha), im(2), ip(1)])
        sum_into(xs.at[ss, js, hz], [blk(0, hz), im(1), ip(2)])

    def x_copies(s, g, j0, nj):
        one, js = pl.ds(s, 1), pl.ds(j0, nj)
        mine_x = lambda rows: xs.at[one, js, rows]
        slot = lambda n: x_in.at[n, one, js]
        make = lambda rows, n, to: ready(mine_x(rows), slot(n), to)
        copies = (
            make(ha, 0, xp), make(hz, 0, xm), make(hz, 0, xp), make(ha, 1, xp), make(ha, 2, xm), make(hz, 3, xm)
        )
        return nxt(x, 4 - g), mine_x, slot, copies, (j0, nj)

    def x_start(s, g, j0, nj):
        state = x_copies(s, g, j0, nj)
        away, _, _, copies, _ = state

        @pl.when(away == 2)
        def _():
            copies[0].start()
            copies[1].start()

        @pl.when(away == 3)
        def _():
            copies[2].start()

        @pl.when(away == 1)
        def _():
            copies[4].start()

        return state

    def x_middle(state):
        away, mine_x, slot, copies, _ = state

        @pl.when(away == 3)
        def _():
            copies[0].wait_recv()
            sum_into(mine_x(ha), [mine_x(ha), slot(0)])
            copies[3].start()

        @pl.when(away == 1)
        def _():
            copies[1].wait_recv()
            sum_into(mine_x(hz), [mine_x(hz), slot(0)])
            copies[5].start()

    def x_finish(state):
        away, mine_x, slot, copies, (j0, nj) = state
        result = lambda rows: ig_ref.at[pl.ds(0, 1), pl.ds(j0, nj), rows]

        @pl.when(away == 0)
        def _():
            for n in (2, 3, 4, 5):
                copies[n].wait_recv()
            sum_into(result(ha), [mine_x(ha), slot(1), slot(2)])
            sum_into(result(hz), [mine_x(hz), slot(0), slot(3)])

        for role, used in ((2, (0, 1)), (3, (2, 3)), (1, (4, 5))):
            @pl.when(away == role)
            def _(used=used):
                for n in used:
                    copies[n].wait_send()

    blocks = hid // t3

    def dot3(lo, hi):
        def tile(n, carry):
            cols = pl.ds(pl.multiple_of(n * t3, t3), t3)
            units = jnp.concatenate([hidden[g, :, j, :, cols].reshape(4 * hb, t3) for g, j in tokens_of], axis=0)
            total = jnp.dot(acts_t[...], units, preferred_element_type=F32)
            wg_ref[:, cols] = total.astype(BF16)
            return carry

        lax.fori_loop(lo * blocks // 6, hi * blocks // 6, tile, 0)

    def neighbours(qs):
        copies = []
        for q in qs:
            own_sends[q][1].wait_recv()
            here = piece(low, k, q)
            if q < 2:
                fwd[q] = send(here, here, zp)
            copies.append(send(here, here, sib))
            own_sends[q][2].wait_recv()
            here = piece(high, k, q)
            if q >= 2:
                fwd[q] = send(here, here, zm)
            copies.append(send(here, here, sib))
        return copies

    def opposite(qs):
        copies = []
        for q in qs:
            fwd[q].wait_recv()
            here = piece(opp, k, q)
            copies.append(send(here, here, sib))
        return copies

    def arrived(copies):
        for copy in copies:
            copy.wait_recv()

    fwd = {}
    arrived([own_sends[q][0] for q in arrivals])
    dot2([(0, z, (0, 1))])
    y0 = y_start(0, 1, 0, 2)
    from_sib = neighbours((0, 2))
    y0 = y_middle(y0)
    arrived(from_sib)
    dot2([(1, low, (0,)), (2, high, (0,))])
    y1 = y_start(1, 2, 0, 1)
    y_finish(y0)
    x0 = x_start(0, z, 0, 2)
    from_sib = neighbours((1, 3))
    y1 = y_middle(y1)
    x_middle(x0)
    arrived(from_sib)
    dot2([(1, low, (1,)), (2, high, (1,))])
    y2 = y_start(1, 2, 1, 1)
    from_sib = opposite((0, 2))
    y_finish(y1)
    arrived(from_sib)
    dot2([(3, opp, (0,))])
    y3 = y_start(3, 1, 0, 1)
    y2 = y_middle(y2)
    from_sib = opposite((1, 3))
    x_finish(x0)
    arrived(from_sib)
    dot2([(3, opp, (1,))])
    y4 = y_start(3, 1, 1, 1)
    y3 = y_middle(y3)
    y_finish(y2)
    x1 = x_start(1, low, 0, 2)
    x2 = x_start(2, high, 0, 2)
    dot3(0, 1)
    y4 = y_middle(y4)
    y_finish(y3)
    x3 = x_start(3, opp, 0, 1)
    x_middle(x1)
    x_middle(x2)
    dot3(1, 2)
    y_finish(y4)
    x4 = x_start(3, opp, 1, 1)
    x_middle(x3)
    dot3(2, 3)
    x_middle(x4)
    x_finish(x1)
    x_finish(x2)
    x_finish(x3)
    dot3(3, 6)
    x_finish(x4)

    for copy in sent:
        if copy is not None:
            copy.wait_send()


def write_out(ig_ref, wg_ref, ig_out, wg_out, sem):
    rows = wg_ref.shape[0] // 4
    copies = [pltpu.make_async_copy(ig_ref, ig_out, sem.at[4])]
    for n in range(4):
        part = pl.ds(n * rows, rows)
        copies.append(pltpu.make_async_copy(wg_ref.at[part], wg_out.at[part], sem.at[n]))
    for copy in copies:
        copy.start()
    for copy in copies:
        copy.wait()


def per_device(acts, up_weight, out_grad):
    tb, feats = acts.shape
    ob, hid = out_grad.shape
    tokens = 16 * tb
    hb = tb // 2
    vmem = lambda *shape: pltpu.VMEM(shape, BF16)
    in_hbm = pl.BlockSpec(memory_space=pltpu.HBM)
    in_vmem = pl.BlockSpec(memory_space=pltpu.VMEM)
    flops = 3 * 2 * tokens * feats * hid
    acts, up_weight, out_grad = (
        pltpu.with_memory_space_constraint(a, pltpu.HBM) for a in (acts, up_weight, out_grad)
    )
    input_grad, weight_grad = pl.pallas_call(
        kernel,
        out_shape=(
            vmem(1, 2, hb, feats),
            vmem(feats, hid),
        ),
        in_specs=[in_hbm] * 3,
        out_specs=(in_vmem, in_vmem),
        scratch_shapes=[
            vmem(4, 4, 2, hb, feats),
            vmem(hid, feats),
            vmem(ob, hid),
            vmem(feats, tokens),
            vmem(4, 4, 2, hb, hid),
            vmem(4, 2, 2, hb, hid),
            vmem(3, 2, hb, hid),
            vmem(3, 2, hb, hid),
            vmem(4, 4, 2, hb, hid),
            vmem(4, 2, 4, hb, feats),
            vmem(3, 4, 2, hb // 2, feats),
            vmem(3, 4, 2, hb // 2, feats),
            vmem(4, 2, hb, feats),
            vmem(4, 4, 2, hb // 2, feats),
            pltpu.SemaphoreType.DMA((9,)),
            pltpu.SemaphoreType.DMA((N_SEMS,)),
            pltpu.SemaphoreType.DMA((N_SEMS,)),
        ],
        compiler_params=pltpu.CompilerParams(
            collective_id=0, has_side_effects=True, vmem_limit_bytes=50 * 2**20
        ),
        cost_estimate=pl.CostEstimate(flops=flops, bytes_accessed=4 * feats * hid, transcendentals=2 * ob * hid),
    )(acts, up_weight, out_grad)
    return pl.pallas_call(
        write_out,
        out_shape=(
            jax.ShapeDtypeStruct((tb, feats), BF16),
            jax.ShapeDtypeStruct((feats, hid), BF16),
        ),
        in_specs=[in_vmem] * 2,
        out_specs=(in_hbm, in_hbm),
        scratch_shapes=[pltpu.SemaphoreType.DMA((5,))],
        compiler_params=pltpu.CompilerParams(vmem_limit_bytes=2 * 2**20),
        cost_estimate=pl.CostEstimate(flops=0, bytes_accessed=2 * feats * hid, transcendentals=0),
    )(input_grad.reshape(tb, feats), weight_grad)


def solution(mesh):
    in_specs = (P("col", "row"), P("row", "col"), P("row", "col"))
    out_specs = (P("col", "row"), P("row", "col"))
    return jax.shard_map(
        per_device, mesh=mesh, in_specs=in_specs, out_specs=out_specs, check_vma=False
    )
```

```python
import functools

import jax
import jax.numpy as jnp
from jax import lax
from jax.experimental import pallas as pl
from jax.experimental.pallas import tpu as pltpu
from jax.sharding import PartitionSpec as P

F32, BF16 = jnp.float32, jnp.bfloat16
MESH = pl.DeviceIdType.MESH
N_SEMS = 160


def gelu_slope(pre):
    cdf = 0.5 * (1.0 + lax.erf(pre * 0.7071067811865476))
    dens = jnp.exp(-0.5 * pre * pre) * 0.3989422804014327
    return cdf + pre * dens


def tile_of(size, want):
    return want if size % want == 0 else size


def weight_block(acts_t, hidden, cols):
    units = hidden[:, :, :, :, cols]
    units = units.reshape(acts_t.shape[1], units.shape[-1])
    return jnp.dot(acts_t[...], units, preferred_element_type=F32).astype(BF16)


def kernel(
    acts_ref, w_ref, og_ref, ig_ref, wg_ref, acts_t, hidden,
    acts, w_t, og, part, sib_in, z_in_m, z_in_p, ig, y_in_m, y_in_p, xs, x_in,
    local_sem, send_sem, recv_sem,
):
    tb, feats = acts_ref.shape
    ob, hid = og_ref.shape
    quarter = ob // 4
    tv, tn, t3 = tile_of(hid // 2, 512), tile_of(hid // 2, 768), tile_of(hid, 256)
    tf, tm = tile_of(feats, 768), tile_of(feats, 256)
    w = wg_ref

    row, col = lax.axis_index("row"), lax.axis_index("col")
    z, k = lax.div(row, 2), lax.rem(row, 2)
    x, y = lax.div(col, 4), lax.rem(col, 4)
    nxt = lambda v, by: lax.rem(v + by, 4)
    sib = {"row": z * 2 + (1 - k)}
    zp, zm = {"row": nxt(z, 1) * 2 + k}, {"row": nxt(z, 3) * 2 + k}
    xp, xm = {"col": nxt(x, 1) * 4 + y}, {"col": nxt(x, 3) * 4 + y}
    yp, ym = {"col": x * 4 + nxt(y, 1)}, {"col": x * 4 + nxt(y, 3)}

    sent = []

    def ready(src, dst, to):
        i = len(sent)
        sent.append(None)
        return pltpu.make_async_remote_copy(
            src_ref=src, dst_ref=dst, send_sem=send_sem.at[i], recv_sem=recv_sem.at[i],
            device_id=to, device_id_type=MESH,
        )

    def send(src, dst, to):
        copy = ready(src, dst, to)
        copy.start()
        sent[-1] = copy
        return copy

    hb = tb // 2

    def step_of(group):
        away = nxt(group, 4 - z)
        odd, far = lax.rem(away, 2), lax.div(away, 2)
        return odd * (2 - lax.rem(far + y, 2)) + (1 - odd) * (3 - 3 * far)

    barrier = pltpu.get_barrier_semaphore()
    for to in (sib, zp, zm, xp, xm, yp, ym):
        pl.semaphore_signal(barrier, inc=1, device_id=to, device_id_type=MESH)
    load_acts = [
        pltpu.make_async_copy(acts_ref.at[pl.ds(j * hb, hb)], acts.at[step_of(x), y, j], local_sem.at[j])
        for j in range(2)
    ]
    load_og = pltpu.make_async_copy(og_ref, og, local_sem.at[2])
    load_w = [
        pltpu.make_async_copy(w_ref.at[pl.ds(m * tm, tm)], w.at[pl.ds(m * tm, tm)], local_sem.at[3 + m])
        for m in range(feats // tm)
    ]
    for load in (*load_acts, *load_w, load_og):
        load.start()
    for load in load_acts:
        load.wait()
    pl.semaphore_wait(barrier, 7)

    low16, high16 = pl.ds(0, hb // 2), pl.ds(hb // 2, hb // 2)

    def ag_start(block, to_p, to_m):
        a = lambda by: block(by, low16)
        b = lambda by: block(by, high16)
        pa = send(a(0), a(0), to_p)
        mb = send(b(0), b(0), to_m)
        pb = send(b(0), b(0), to_p)
        ma = send(a(0), a(0), to_m)
        return a, b, pa, mb, pb, ma, to_p, to_m

    def ag_forward(state):
        a, b, pa, mb, pb, ma, to_p, to_m = state
        pa.wait_recv()
        fa = send(a(3), a(3), to_p)
        mb.wait_recv()
        fb = send(b(1), b(1), to_m)
        return pb, ma, fa, fb

    def ag_finish(copies):
        for copy in copies:
            copy.wait_recv()

    def x_gather(j):
        return ag_start(lambda by, rows: acts.at[step_of(nxt(x, by)), y, j, rows], xp, xm)

    def y_gather(s, j0, nj):
        return ag_start(lambda by, rows: acts.at[s, nxt(y, by), pl.ds(j0, nj), rows], yp, ym)

    def turn_w(m, loaded=False):
        if not loaded:
            load_w[m].wait()

        def tile(n, carry):
            cols = pl.ds(pl.multiple_of(n * tm, tm), tm)
            w_t[cols, m * tm:(m + 1) * tm] = w[m * tm:(m + 1) * tm, cols].T
            return carry

        lax.fori_loop(0, hid // tm, tile, 0)

    def dot1(s, j0, nj):
        js = pl.ds(j0, nj)
        sem = len(sent)

        def to_sib(cols):
            return pltpu.make_async_remote_copy(
                src_ref=part.at[s, pl.ds(2 * (1 - k), 2), js, :, cols], dst_ref=sib_in.at[s, :, js, :, cols],
                send_sem=send_sem.at[sem], recv_sem=recv_sem.at[sem], device_id=sib, device_id_type=MESH,
            )

        def tile(n, carry):
            cols = pl.ds(pl.multiple_of(n * tn, tn), tn)
            share = jnp.dot(
                acts[s, :, js].reshape(4 * nj * hb, feats), w[:, cols], preferred_element_type=F32
            )
            part[s, :, js, :, cols] = share.astype(BF16).reshape(4, nj, hb, tn)
            to_sib(cols).start()
            return carry

        lax.fori_loop(0, hid // tn, tile, 0)
        sent.append(to_sib(pl.ds(0, hid)))
        return sent[-1]

    def add_into(dst, src):
        def tile(n, carry):
            cols = pl.ds(pl.multiple_of(n * tv, tv), tv)
            for j in range(dst.shape[0]):
                total = dst[j, :, cols].astype(F32) + src[j, :, cols].astype(F32)
                dst[j, :, cols] = total.astype(BF16)
            return carry

        lax.fori_loop(0, hid // tv, tile, 0)

    def core_sum(s, copy, j0, nj):
        copy.wait_recv()
        js = pl.ds(j0, nj)
        for way in range(2):
            add_into(part.at[s, 2 * k + way, js], sib_in.at[s, way, js])

    mine = lambda s, way: part.at[s, 2 * k + way]
    gx = x_gather(0)
    turn_w(0)
    gx0 = ag_forward(gx)
    gx = x_gather(1)
    turn_w(1)
    ag_finish(gx0)
    g = y_gather(0, 0, 1)
    turn_w(2)
    gx1 = ag_forward(gx)
    g0 = ag_forward(g)
    turn_w(3)
    ag_finish(gx1)
    g = y_gather(0, 1, 1)
    for load in load_w[4:]:
        load.wait()
    ag_finish(g0)
    opp_p, opp_m = [], []
    c = dot1(0, 0, 1)
    g0 = ag_forward(g)
    g = y_gather(1, 0, 2)
    core_sum(0, c, 0, 1)
    opp_p.append(send(mine(0, 0).at[0], z_in_m.at[0, 0], zp))
    opp_m.append(send(mine(0, 1).at[0], z_in_p.at[0, 0], zm))
    ag_finish(g0)
    c = dot1(0, 1, 1)
    g0 = ag_forward(g)
    g = y_gather(2, 0, 2)
    core_sum(0, c, 1, 1)
    opp_p.append(send(mine(0, 0).at[1], z_in_m.at[0, 1], zp))
    opp_m.append(send(mine(0, 1).at[1], z_in_p.at[0, 1], zm))
    ag_finish(g0)
    c = dot1(1, 0, 2)
    g0 = ag_forward(g)
    g = y_gather(3, 0, 2)
    core_sum(1, c, 0, 2)
    dir_p = send(mine(1, 1), z_in_m.at[1], zp)
    dir_m = send(mine(1, 0), z_in_p.at[1], zm)
    ag_finish(g0)
    c = dot1(2, 0, 2)
    g0 = ag_forward(g)
    core_sum(2, c, 0, 2)
    acc_p, acc_m = [], []
    for j in range(2):
        one = pl.ds(j, 1)
        opp_p[j].wait_recv()
        add_into(mine(2, 0).at[one], z_in_m.at[0, one])
        acc_p.append(send(mine(2, 0).at[j], z_in_m.at[2, j], zp))
        opp_m[j].wait_recv()
        add_into(mine(2, 1).at[one], z_in_p.at[0, one])
        acc_m.append(send(mine(2, 1).at[j], z_in_p.at[2, j], zm))
    ag_finish(g0)
    c = dot1(3, 0, 2)
    core_sum(3, c, 0, 2)
    load_og.wait()

    low, high, opp = nxt(z, 3), nxt(z, 1), nxt(z, 2)
    held_in = [(z, 3, 3), (low, 1, 2), (high, 2, 1), (opp, 0, 0)]

    def turn(n, carry):
        cols = pl.ds(pl.multiple_of(n * tm, tm), tm)
        for g, even, odd in held_in:
            rows = [acts[(even, odd)[b % 2], b, :, :, cols].reshape(tb, tm) for b in range(4)]
            acts_t[cols, pl.ds(pl.multiple_of(g * 4 * tb, 4 * tb), 4 * tb)] = jnp.concatenate(rows, axis=0).T
        return carry

    lax.fori_loop(0, feats // tm, turn, 0)
    for m in range(4, feats // tm):
        turn_w(m, True)

    dir_p.wait_recv()
    dir_m.wait_recv()
    piece = lambda zz, kk, q: hidden.at[zz, 2 * kk + q // 2, q % 2]

    def slope_piece(q, from_m, from_p):
        start = q * quarter

        def tile(n, carry):
            cols = pl.ds(pl.multiple_of(n * tv, tv), tv)
            own = part[3, 2 * k + q // 2, q % 2, :, cols]
            pre = own.astype(F32) + from_m[:, cols].astype(F32) + from_p[:, cols].astype(F32)
            grad = og[start:start + quarter, cols].astype(F32) * gelu_slope(pre)
            hidden[z, 2 * k + q // 2, q % 2, :, cols] = grad.astype(BF16)
            return carry

        lax.fori_loop(0, hid // tv, tile, 0)
        here = piece(z, k, q)
        return send(here, here, sib), send(here, here, zp), send(here, here, zm)

    arrivals = (0, 2, 1, 3)
    own_sends = {}
    for j in range(2):
        acc_p[j].wait_recv()
        own_sends[j] = slope_piece(j, z_in_m.at[2, j], z_in_p.at[1, j])
        acc_m[j].wait_recv()
        own_sends[2 + j] = slope_piece(2 + j, z_in_m.at[1, j], z_in_p.at[2, j])

    def dot2(units):
        def tile(n, carry):
            cols = pl.ds(pl.multiple_of(n * tf, tf), tf)
            rows = [hidden[g, :, j].reshape(4 * hb, hid) for _, g, js in units for j in js]
            rows = rows[0] if len(rows) == 1 else jnp.concatenate(rows, axis=0)
            share = jnp.dot(rows, w_t[:, cols], preferred_element_type=F32).astype(BF16)
            at_row = 0
            for s, _, js in units:
                for j in js:
                    ig[s, j, :, :, cols] = share[at_row:at_row + 4 * hb].reshape(4, hb, tf)
                    at_row += 4 * hb
            return carry

        lax.fori_loop(0, feats // tf, tile, 0)

    def sum_into(out, terms):
        def tile(n, carry):
            cols = pl.ds(pl.multiple_of(n * tv, tv), tv)
            for p in range(out.shape[0]):
                for q in range(out.shape[1]):
                    total = terms[0][p, q, :, cols].astype(F32)
                    for term in terms[1:]:
                        total = total + term[p, q, :, cols].astype(F32)
                    out[p, q, :, cols] = total.astype(BF16)
            return carry

        lax.fori_loop(0, feats // tv, tile, 0)

    ha, hz = pl.ds(0, hb // 2), pl.ds(hb // 2, hb // 2)

    def y_start(s0, ns, j0, nj):
        ss, js = pl.ds(s0, ns), pl.ds(j0, nj)
        blk = lambda by, rows: ig.at[ss, js, nxt(y, by), rows]
        im = lambda n: y_in_m.at[n, ss, js]
        ip = lambda n: y_in_p.at[n, ss, js]
        op = send(blk(2, ha), im(0), yp)
        om = send(blk(2, hz), ip(0), ym)
        dp = send(blk(1, hz), im(1), yp)
        dm = send(blk(3, ha), ip(1), ym)
        return ss, js, blk, im, ip, op, om, dp, dm

    def y_middle(state):
        ss, js, blk, im, ip, op, om, dp, dm = state
        op.wait_recv()
        sum_into(blk(1, ha), [blk(1, ha), im(0)])
        ap = send(blk(1, ha), im(2), yp)
        om.wait_recv()
        sum_into(blk(3, hz), [blk(3, hz), ip(0)])
        am = send(blk(3, hz), ip(2), ym)
        return ss, js, blk, im, ip, (dp, dm, ap, am)

    def y_finish(state):
        ss, js, blk, im, ip, copies = state
        for copy in copies:
            copy.wait_recv()
        sum_into(xs.at[ss, js, ha], [blk(0, ha), im(2), ip(1)])
        sum_into(xs.at[ss, js, hz], [blk(0, hz), im(1), ip(2)])

    def x_copies(s, g, j0, nj):
        one, js = pl.ds(s, 1), pl.ds(j0, nj)
        mine_x = lambda rows: xs.at[one, js, rows]
        slot = lambda n: x_in.at[n, one, js]
        make = lambda rows, n, to: ready(mine_x(rows), slot(n), to)
        copies = (
            make(ha, 0, xp), make(hz, 0, xm), make(hz, 0, xp), make(ha, 1, xp), make(ha, 2, xm), make(hz, 3, xm)
        )
        return nxt(x, 4 - g), mine_x, slot, copies, (j0, nj)

    def x_start(s, g, j0, nj):
        state = x_copies(s, g, j0, nj)
        away, _, _, copies, _ = state

        @pl.when(away == 2)
        def _():
            copies[0].start()
            copies[1].start()

        @pl.when(away == 3)
        def _():
            copies[2].start()

        @pl.when(away == 1)
        def _():
            copies[4].start()

        return state

    def x_middle(state):
        away, mine_x, slot, copies, _ = state

        @pl.when(away == 3)
        def _():
            copies[0].wait_recv()
            sum_into(mine_x(ha), [mine_x(ha), slot(0)])
            copies[3].start()

        @pl.when(away == 1)
        def _():
            copies[1].wait_recv()
            sum_into(mine_x(hz), [mine_x(hz), slot(0)])
            copies[5].start()

    def x_finish(state):
        away, mine_x, slot, copies, (j0, nj) = state
        result = lambda rows: ig_ref.at[pl.ds(0, 1), pl.ds(j0, nj), rows]

        @pl.when(away == 0)
        def _():
            for n in (2, 3, 4, 5):
                copies[n].wait_recv()
            sum_into(result(ha), [mine_x(ha), slot(1), slot(2)])
            sum_into(result(hz), [mine_x(hz), slot(0), slot(3)])

        for role, used in ((2, (0, 1)), (3, (2, 3)), (1, (4, 5))):
            @pl.when(away == role)
            def _(used=used):
                for n in used:
                    copies[n].wait_send()

    blocks = hid // t3 * 3 // 4

    def dot3(lo, hi):
        def tile(n, carry):
            cols = pl.ds(pl.multiple_of(n * t3, t3), t3)
            wg_ref[:, cols] = weight_block(acts_t, hidden, cols)
            return carry

        lax.fori_loop(lo * blocks // 9, hi * blocks // 9, tile, 0)

    def neighbours(qs):
        copies = []
        for q in qs:
            own_sends[q][1].wait_recv()
            here = piece(low, k, q)
            if q < 2:
                fwd[q] = send(here, here, zp)
            copies.append(send(here, here, sib))
            own_sends[q][2].wait_recv()
            here = piece(high, k, q)
            if q >= 2:
                fwd[q] = send(here, here, zm)
            copies.append(send(here, here, sib))
        return copies

    def opposite(qs):
        copies = []
        for q in qs:
            fwd[q].wait_recv()
            here = piece(opp, k, q)
            copies.append(send(here, here, sib))
        return copies

    def arrived(copies):
        for copy in copies:
            copy.wait_recv()

    fwd = {}
    arrived([own_sends[q][0] for q in arrivals])
    dot2([(0, z, (0, 1))])
    y0 = y_start(0, 1, 0, 2)
    from_sib = neighbours((0, 2))
    y0 = y_middle(y0)
    arrived(from_sib)
    dot2([(1, low, (0,)), (2, high, (0,))])
    y1 = y_start(1, 2, 0, 1)
    y_finish(y0)
    x0 = x_start(0, z, 0, 2)
    from_sib = neighbours((1, 3))
    y1 = y_middle(y1)
    x_middle(x0)
    arrived(from_sib)
    dot2([(1, low, (1,)), (2, high, (1,))])
    y2 = y_start(1, 2, 1, 1)
    from_sib = opposite((0, 2))
    y_finish(y1)
    arrived(from_sib)
    dot2([(3, opp, (0,))])
    y3 = y_start(3, 1, 0, 1)
    y2 = y_middle(y2)
    from_sib = opposite((1, 3))
    x_finish(x0)
    arrived(from_sib)
    dot2([(3, opp, (1,))])
    y4 = y_start(3, 1, 1, 1)
    y3 = y_middle(y3)
    y_finish(y2)
    x1 = x_start(1, low, 0, 2)
    x2 = x_start(2, high, 0, 2)
    dot3(0, 2)
    y4 = y_middle(y4)
    y_finish(y3)
    x3 = x_start(3, opp, 0, 1)
    x_middle(x1)
    x_middle(x2)
    dot3(2, 4)
    y_finish(y4)
    x4 = x_start(3, opp, 1, 1)
    x_middle(x3)
    dot3(4, 6)
    x_middle(x4)
    x_finish(x1)
    x_finish(x2)
    x_finish(x3)
    dot3(6, 9)
    x_finish(x4)

    for copy in sent:
        if copy is not None:
            copy.wait_send()


def write_out(ig_ref, wg_ref, acts_t, hidden, ig_out, wg_out, stage, sem):
    feats, width = stage.shape[1:]
    done = wg_ref.shape[1] - stage.shape[0] * width
    rows = feats // 4
    copies = [pltpu.make_async_copy(ig_ref, ig_out, sem.at[4])]
    for n in range(4):
        part = (pl.ds(n * rows, rows), pl.ds(0, done))
        copies.append(pltpu.make_async_copy(wg_ref.at[part], wg_out.at[part], sem.at[n]))
    for copy in copies:
        copy.start()
    for n in range(stage.shape[0]):
        cols = pl.ds(done + n * width, width)
        stage[n] = weight_block(acts_t, hidden, cols)
        copies.append(pltpu.make_async_copy(stage.at[n], wg_out.at[:, cols], sem.at[5 + n]))
        copies[-1].start()
    for copy in copies:
        copy.wait()


def per_device(acts, up_weight, out_grad):
    tb, feats = acts.shape
    ob, hid = out_grad.shape
    tokens = 16 * tb
    hb = tb // 2
    vmem = lambda *shape: pltpu.VMEM(shape, BF16)
    in_hbm = pl.BlockSpec(memory_space=pltpu.HBM)
    in_vmem = pl.BlockSpec(memory_space=pltpu.VMEM)
    flops = 3 * 2 * tokens * feats * hid
    blocks = hid // tile_of(hid, 256)
    acts, up_weight, out_grad = (
        pltpu.with_memory_space_constraint(a, pltpu.HBM) for a in (acts, up_weight, out_grad)
    )
    input_grad, weight_grad, acts_t, hidden = pl.pallas_call(
        kernel,
        out_shape=(
            vmem(1, 2, hb, feats),
            vmem(feats, hid),
            vmem(feats, tokens),
            vmem(4, 4, 2, hb, hid),
        ),
        in_specs=[in_hbm] * 3,
        out_specs=(in_vmem,) * 4,
        scratch_shapes=[
            vmem(4, 4, 2, hb, feats),
            vmem(hid, feats),
            vmem(ob, hid),
            vmem(4, 4, 2, hb, hid),
            vmem(4, 2, 2, hb, hid),
            vmem(3, 2, hb, hid),
            vmem(3, 2, hb, hid),
            vmem(4, 2, 4, hb, feats),
            vmem(3, 4, 2, hb // 2, feats),
            vmem(3, 4, 2, hb // 2, feats),
            vmem(4, 2, hb, feats),
            vmem(4, 4, 2, hb // 2, feats),
            pltpu.SemaphoreType.DMA((9,)),
            pltpu.SemaphoreType.DMA((N_SEMS,)),
            pltpu.SemaphoreType.DMA((N_SEMS,)),
        ],
        compiler_params=pltpu.CompilerParams(
            collective_id=0, has_side_effects=True, vmem_limit_bytes=41 * 2**20
        ),
        cost_estimate=pl.CostEstimate(flops=flops, bytes_accessed=4 * feats * hid, transcendentals=2 * ob * hid),
    )(acts, up_weight, out_grad)
    return pl.pallas_call(
        write_out,
        out_shape=(
            jax.ShapeDtypeStruct((tb, feats), BF16),
            jax.ShapeDtypeStruct((feats, hid), BF16),
        ),
        in_specs=[in_vmem] * 4,
        out_specs=(in_hbm, in_hbm),
        scratch_shapes=[vmem(blocks // 4, feats, hid // blocks), pltpu.SemaphoreType.DMA((5 + blocks // 4,))],
        compiler_params=pltpu.CompilerParams(vmem_limit_bytes=10 * 2**20),
        cost_estimate=pl.CostEstimate(flops=flops // 12, bytes_accessed=2 * feats * hid, transcendentals=0),
    )(input_grad.reshape(tb, feats), weight_grad, acts_t, hidden)


def solution(mesh):
    in_specs = (P("col", "row"), P("row", "col"), P("row", "col"))
    out_specs = (P("col", "row"), P("row", "col"))
    return jax.shard_map(
        per_device, mesh=mesh, in_specs=in_specs, out_specs=out_specs, check_vma=False
    )
```

```python
import functools

import jax
import jax.numpy as jnp
from jax import lax
from jax.experimental import pallas as pl
from jax.experimental.pallas import tpu as pltpu
from jax.sharding import PartitionSpec as P

F32, BF16 = jnp.float32, jnp.bfloat16
MESH = pl.DeviceIdType.MESH
N_SEMS = 160


def gelu_slope(pre):
    cdf = 0.5 * (1.0 + lax.erf(pre * 0.7071067811865476))
    dens = jnp.exp(-0.5 * pre * pre) * 0.3989422804014327
    return cdf + pre * dens


def tile_of(size, want):
    return want if size % want == 0 else size


def weight_block(acts_t, hidden, cols):
    units = hidden[:, :, :, :, cols]
    units = units.reshape(acts_t.shape[1], units.shape[-1])
    return jnp.dot(acts_t[...], units, preferred_element_type=F32).astype(BF16)


def kernel(
    acts_ref, w_ref, og_ref, ig_ref, wg_ref, acts_t, hidden,
    acts, w_t, og, part, sib_in, z_in_m, z_in_p, ig, y_in_m, y_in_p, xs, x_in,
    local_sem, send_sem, recv_sem,
):
    tb, feats = acts_ref.shape
    ob, hid = og_ref.shape
    quarter = ob // 4
    tv, tn, t3 = tile_of(hid // 2, 512), tile_of(hid // 2, 768), tile_of(hid, 256)
    tf, tm = tile_of(feats, 768), tile_of(feats, 256)
    w = wg_ref

    row, col = lax.axis_index("row"), lax.axis_index("col")
    z, k = lax.div(row, 2), lax.rem(row, 2)
    x, y = lax.div(col, 4), lax.rem(col, 4)
    nxt = lambda v, by: lax.rem(v + by, 4)
    sib = {"row": z * 2 + (1 - k)}
    zp, zm = {"row": nxt(z, 1) * 2 + k}, {"row": nxt(z, 3) * 2 + k}
    xp, xm = {"col": nxt(x, 1) * 4 + y}, {"col": nxt(x, 3) * 4 + y}
    yp, ym = {"col": x * 4 + nxt(y, 1)}, {"col": x * 4 + nxt(y, 3)}

    sent = []

    def ready(src, dst, to):
        i = len(sent)
        sent.append(None)
        return pltpu.make_async_remote_copy(
            src_ref=src, dst_ref=dst, send_sem=send_sem.at[i], recv_sem=recv_sem.at[i],
            device_id=to, device_id_type=MESH,
        )

    def send(src, dst, to):
        copy = ready(src, dst, to)
        copy.start()
        sent[-1] = copy
        return copy

    hb = tb // 2

    def step_of(group):
        away = nxt(group, 4 - z)
        odd, far = lax.rem(away, 2), lax.div(away, 2)
        return odd * (2 - lax.rem(far + y, 2)) + (1 - odd) * (3 - 3 * far)

    barrier = pltpu.get_barrier_semaphore()
    for to in (sib, zp, zm, xp, xm, yp, ym):
        pl.semaphore_signal(barrier, inc=1, device_id=to, device_id_type=MESH)
    load_acts = [
        pltpu.make_async_copy(acts_ref.at[pl.ds(j * hb, hb)], acts.at[step_of(x), y, j], local_sem.at[j])
        for j in range(2)
    ]
    load_og = pltpu.make_async_copy(og_ref, og, local_sem.at[2])
    load_w = [
        pltpu.make_async_copy(w_ref.at[pl.ds(m * tm, tm)], w.at[pl.ds(m * tm, tm)], local_sem.at[3 + m])
        for m in range(feats // tm)
    ]
    for load in (*load_acts, *load_w, load_og):
        load.start()
    for load in load_acts:
        load.wait()
    pl.semaphore_wait(barrier, 7)

    low16, high16 = pl.ds(0, hb // 2), pl.ds(hb // 2, hb // 2)

    def ag_start(block, to_p, to_m):
        a = lambda by: block(by, low16)
        b = lambda by: block(by, high16)
        pa = send(a(0), a(0), to_p)
        mb = send(b(0), b(0), to_m)
        pb = send(b(0), b(0), to_p)
        ma = send(a(0), a(0), to_m)
        return a, b, pa, mb, pb, ma, to_p, to_m

    def ag_forward(state):
        a, b, pa, mb, pb, ma, to_p, to_m = state
        pa.wait_recv()
        fa = send(a(3), a(3), to_p)
        mb.wait_recv()
        fb = send(b(1), b(1), to_m)
        return pb, ma, fa, fb

    def ag_finish(copies):
        for copy in copies:
            copy.wait_recv()

    def x_gather(j):
        return ag_start(lambda by, rows: acts.at[step_of(nxt(x, by)), y, j, rows], xp, xm)

    def y_gather(s, j0, nj):
        return ag_start(lambda by, rows: acts.at[s, nxt(y, by), pl.ds(j0, nj), rows], yp, ym)

    def turn_w(m):
        load_w[m].wait()

        def tile(n, carry):
            cols = pl.ds(pl.multiple_of(n * tm, tm), tm)
            w_t[cols, m * tm:(m + 1) * tm] = w[m * tm:(m + 1) * tm, cols].T
            return carry

        lax.fori_loop(0, hid // tm, tile, 0)

    def dot1(s, j0, nj):
        js = pl.ds(j0, nj)
        sem = len(sent)

        def to_sib(cols):
            return pltpu.make_async_remote_copy(
                src_ref=part.at[s, pl.ds(2 * (1 - k), 2), js, :, cols], dst_ref=sib_in.at[s, :, js, :, cols],
                send_sem=send_sem.at[sem], recv_sem=recv_sem.at[sem], device_id=sib, device_id_type=MESH,
            )

        def tile(n, carry):
            cols = pl.ds(pl.multiple_of(n * tn, tn), tn)
            share = jnp.dot(
                acts[s, :, js].reshape(4 * nj * hb, feats), w[:, cols], preferred_element_type=F32
            )
            part[s, :, js, :, cols] = share.astype(BF16).reshape(4, nj, hb, tn)
            to_sib(cols).start()
            return carry

        lax.fori_loop(0, hid // tn, tile, 0)
        sent.append(to_sib(pl.ds(0, hid)))
        return sent[-1]

    def add_into(dst, src):
        def tile(n, carry):
            cols = pl.ds(pl.multiple_of(n * tv, tv), tv)
            for j in range(dst.shape[0]):
                total = dst[j, :, cols].astype(F32) + src[j, :, cols].astype(F32)
                dst[j, :, cols] = total.astype(BF16)
            return carry

        lax.fori_loop(0, hid // tv, tile, 0)

    def core_sum(s, copy, j0, nj):
        copy.wait_recv()
        js = pl.ds(j0, nj)
        for way in range(2):
            add_into(part.at[s, 2 * k + way, js], sib_in.at[s, way, js])

    mine = lambda s, way: part.at[s, 2 * k + way]
    gx = x_gather(0)
    turn_w(0)
    gx0 = ag_forward(gx)
    gx = x_gather(1)
    turn_w(1)
    ag_finish(gx0)
    g = y_gather(0, 0, 1)
    turn_w(2)
    gx1 = ag_forward(gx)
    g0 = ag_forward(g)
    turn_w(3)
    ag_finish(gx1)
    g = y_gather(0, 1, 1)
    for m in range(4, feats // tm):
        turn_w(m)
    ag_finish(g0)
    opp_p, opp_m = [], []
    c = dot1(0, 0, 1)
    g0 = ag_forward(g)
    g = y_gather(1, 0, 2)
    core_sum(0, c, 0, 1)
    opp_p.append(send(mine(0, 0).at[0], z_in_m.at[0, 0], zp))
    opp_m.append(send(mine(0, 1).at[0], z_in_p.at[0, 0], zm))
    ag_finish(g0)
    c = dot1(0, 1, 1)
    g0 = ag_forward(g)
    g = y_gather(2, 0, 2)
    core_sum(0, c, 1, 1)
    opp_p.append(send(mine(0, 0).at[1], z_in_m.at[0, 1], zp))
    opp_m.append(send(mine(0, 1).at[1], z_in_p.at[0, 1], zm))
    ag_finish(g0)
    c = dot1(1, 0, 2)
    g0 = ag_forward(g)
    g = y_gather(3, 0, 2)
    core_sum(1, c, 0, 2)
    dir_p = send(mine(1, 1), z_in_m.at[1], zp)
    dir_m = send(mine(1, 0), z_in_p.at[1], zm)
    ag_finish(g0)
    c = dot1(2, 0, 2)
    g0 = ag_forward(g)
    core_sum(2, c, 0, 2)
    acc_p, acc_m = [], []
    for j in range(2):
        one = pl.ds(j, 1)
        opp_p[j].wait_recv()
        add_into(mine(2, 0).at[one], z_in_m.at[0, one])
        acc_p.append(send(mine(2, 0).at[j], z_in_m.at[2, j], zp))
        opp_m[j].wait_recv()
        add_into(mine(2, 1).at[one], z_in_p.at[0, one])
        acc_m.append(send(mine(2, 1).at[j], z_in_p.at[2, j], zm))
    ag_finish(g0)
    c = dot1(3, 0, 2)
    core_sum(3, c, 0, 2)
    load_og.wait()

    low, high, opp = nxt(z, 3), nxt(z, 1), nxt(z, 2)
    held_in = [(z, 3, 3), (low, 1, 2), (high, 2, 1), (opp, 0, 0)]

    def turn(n, carry):
        cols = pl.ds(pl.multiple_of(n * tm, tm), tm)
        for g, even, odd in held_in:
            rows = [acts[(even, odd)[b % 2], b, :, :, cols].reshape(tb, tm) for b in range(4)]
            acts_t[cols, pl.ds(pl.multiple_of(g * 4 * tb, 4 * tb), 4 * tb)] = jnp.concatenate(rows, axis=0).T
        return carry

    dir_p.wait_recv()
    dir_m.wait_recv()
    piece = lambda zz, kk, q: hidden.at[zz, 2 * kk + q // 2, q % 2]

    def slope_piece(q, from_m, from_p):
        start = q * quarter

        def tile(n, carry):
            cols = pl.ds(pl.multiple_of(n * tv, tv), tv)
            own = part[3, 2 * k + q // 2, q % 2, :, cols]
            pre = own.astype(F32) + from_m[:, cols].astype(F32) + from_p[:, cols].astype(F32)
            grad = og[start:start + quarter, cols].astype(F32) * gelu_slope(pre)
            hidden[z, 2 * k + q // 2, q % 2, :, cols] = grad.astype(BF16)
            return carry

        lax.fori_loop(0, hid // tv, tile, 0)
        here = piece(z, k, q)
        return send(here, here, sib), send(here, here, zp), send(here, here, zm)

    arrivals = (0, 2, 1, 3)
    own_sends = {}
    for j in range(2):
        acc_p[j].wait_recv()
        own_sends[j] = slope_piece(j, z_in_m.at[2, j], z_in_p.at[1, j])
        acc_m[j].wait_recv()
        own_sends[2 + j] = slope_piece(2 + j, z_in_m.at[1, j], z_in_p.at[2, j])

    def dot2(units):
        def tile(n, carry):
            cols = pl.ds(pl.multiple_of(n * tf, tf), tf)
            rows = [hidden[g, :, j].reshape(4 * hb, hid) for _, g, js in units for j in js]
            rows = rows[0] if len(rows) == 1 else jnp.concatenate(rows, axis=0)
            share = jnp.dot(rows, w_t[:, cols], preferred_element_type=F32).astype(BF16)
            at_row = 0
            for s, _, js in units:
                for j in js:
                    ig[s, j, :, :, cols] = share[at_row:at_row + 4 * hb].reshape(4, hb, tf)
                    at_row += 4 * hb
            return carry

        lax.fori_loop(0, feats // tf, tile, 0)

    def sum_into(out, terms):
        def tile(n, carry):
            cols = pl.ds(pl.multiple_of(n * tv, tv), tv)
            for p in range(out.shape[0]):
                for q in range(out.shape[1]):
                    total = terms[0][p, q, :, cols].astype(F32)
                    for term in terms[1:]:
                        total = total + term[p, q, :, cols].astype(F32)
                    out[p, q, :, cols] = total.astype(BF16)
            return carry

        lax.fori_loop(0, feats // tv, tile, 0)

    ha, hz = pl.ds(0, hb // 2), pl.ds(hb // 2, hb // 2)

    def y_start(s0, ns, j0, nj):
        ss, js = pl.ds(s0, ns), pl.ds(j0, nj)
        blk = lambda by, rows: ig.at[ss, js, nxt(y, by), rows]
        im = lambda n: y_in_m.at[n, ss, js]
        ip = lambda n: y_in_p.at[n, ss, js]
        op = send(blk(2, ha), im(0), yp)
        om = send(blk(2, hz), ip(0), ym)
        dp = send(blk(1, hz), im(1), yp)
        dm = send(blk(3, ha), ip(1), ym)
        return ss, js, blk, im, ip, op, om, dp, dm

    def y_middle(state):
        ss, js, blk, im, ip, op, om, dp, dm = state
        op.wait_recv()
        sum_into(blk(1, ha), [blk(1, ha), im(0)])
        ap = send(blk(1, ha), im(2), yp)
        om.wait_recv()
        sum_into(blk(3, hz), [blk(3, hz), ip(0)])
        am = send(blk(3, hz), ip(2), ym)
        return ss, js, blk, im, ip, (dp, dm, ap, am)

    def y_finish(state):
        ss, js, blk, im, ip, copies = state
        for copy in copies:
            copy.wait_recv()
        sum_into(xs.at[ss, js, ha], [blk(0, ha), im(2), ip(1)])
        sum_into(xs.at[ss, js, hz], [blk(0, hz), im(1), ip(2)])

    def x_copies(s, g, j0, nj):
        one, js = pl.ds(s, 1), pl.ds(j0, nj)
        mine_x = lambda rows: xs.at[one, js, rows]
        slot = lambda n: x_in.at[n, one, js]
        make = lambda rows, n, to: ready(mine_x(rows), slot(n), to)
        copies = (
            make(ha, 0, xp), make(hz, 0, xm), make(hz, 0, xp), make(ha, 1, xp), make(ha, 2, xm), make(hz, 3, xm)
        )
        return nxt(x, 4 - g), mine_x, slot, copies, (j0, nj)

    def x_start(s, g, j0, nj):
        state = x_copies(s, g, j0, nj)
        away, _, _, copies, _ = state

        @pl.when(away == 2)
        def _():
            copies[0].start()
            copies[1].start()

        @pl.when(away == 3)
        def _():
            copies[2].start()

        @pl.when(away == 1)
        def _():
            copies[4].start()

        return state

    def x_middle(state):
        away, mine_x, slot, copies, _ = state

        @pl.when(away == 3)
        def _():
            copies[0].wait_recv()
            sum_into(mine_x(ha), [mine_x(ha), slot(0)])
            copies[3].start()

        @pl.when(away == 1)
        def _():
            copies[1].wait_recv()
            sum_into(mine_x(hz), [mine_x(hz), slot(0)])
            copies[5].start()

    def x_finish(state):
        away, mine_x, slot, copies, (j0, nj) = state
        result = lambda rows: ig_ref.at[pl.ds(0, 1), pl.ds(j0, nj), rows]

        @pl.when(away == 0)
        def _():
            for n in (2, 3, 4, 5):
                copies[n].wait_recv()
            sum_into(result(ha), [mine_x(ha), slot(1), slot(2)])
            sum_into(result(hz), [mine_x(hz), slot(0), slot(3)])

        for role, used in ((2, (0, 1)), (3, (2, 3)), (1, (4, 5))):
            @pl.when(away == role)
            def _(used=used):
                for n in used:
                    copies[n].wait_send()

    blocks = hid // t3 * 3 // 4

    def dot3(lo, hi):
        def tile(n, carry):
            cols = pl.ds(pl.multiple_of(n * t3, t3), t3)
            wg_ref[:, cols] = weight_block(acts_t, hidden, cols)
            return carry

        lax.fori_loop(lo * blocks // 9, hi * blocks // 9, tile, 0)

    def neighbours(qs):
        copies = []
        for q in qs:
            own_sends[q][1].wait_recv()
            here = piece(low, k, q)
            if q < 2:
                fwd[q] = send(here, here, zp)
            copies.append(send(here, here, sib))
            own_sends[q][2].wait_recv()
            here = piece(high, k, q)
            if q >= 2:
                fwd[q] = send(here, here, zm)
            copies.append(send(here, here, sib))
        return copies

    def opposite(qs):
        copies = []
        for q in qs:
            fwd[q].wait_recv()
            here = piece(opp, k, q)
            copies.append(send(here, here, sib))
        return copies

    def arrived(copies):
        for copy in copies:
            copy.wait_recv()

    fwd = {}
    arrived([own_sends[q][0] for q in arrivals])
    dot2([(0, z, (0, 1))])
    y0 = y_start(0, 1, 0, 2)
    lax.fori_loop(0, feats // tm, turn, 0)
    from_sib = neighbours((0, 2))
    y0 = y_middle(y0)
    arrived(from_sib)
    dot2([(1, low, (0,)), (2, high, (0,))])
    y1 = y_start(1, 2, 0, 1)
    y_finish(y0)
    x0 = x_start(0, z, 0, 2)
    from_sib = neighbours((1, 3))
    y1 = y_middle(y1)
    x_middle(x0)
    arrived(from_sib)
    dot2([(1, low, (1,)), (2, high, (1,))])
    y2 = y_start(1, 2, 1, 1)
    from_sib = opposite((0, 2))
    y_finish(y1)
    arrived(from_sib)
    dot2([(3, opp, (0,))])
    y3 = y_start(3, 1, 0, 1)
    y2 = y_middle(y2)
    from_sib = opposite((1, 3))
    x_finish(x0)
    arrived(from_sib)
    dot2([(3, opp, (1,))])
    y4 = y_start(3, 1, 1, 1)
    y3 = y_middle(y3)
    y_finish(y2)
    x1 = x_start(1, low, 0, 2)
    x2 = x_start(2, high, 0, 2)
    dot3(0, 2)
    y4 = y_middle(y4)
    y_finish(y3)
    x3 = x_start(3, opp, 0, 1)
    x_middle(x1)
    x_middle(x2)
    dot3(2, 4)
    y_finish(y4)
    x4 = x_start(3, opp, 1, 1)
    x_middle(x3)
    dot3(4, 6)
    x_middle(x4)
    x_finish(x1)
    x_finish(x2)
    x_finish(x3)
    dot3(6, 9)
    x_finish(x4)

    for copy in sent:
        if copy is not None:
            copy.wait_send()


def write_out(ig_ref, wg_ref, acts_t, hidden, ig_out, wg_out, stage, sem):
    feats, width = stage.shape[1:]
    done = wg_ref.shape[1] - stage.shape[0] * width
    rows = feats // 4
    copies = [pltpu.make_async_copy(ig_ref, ig_out, sem.at[4])]
    for n in range(4):
        part = (pl.ds(n * rows, rows), pl.ds(0, done))
        copies.append(pltpu.make_async_copy(wg_ref.at[part], wg_out.at[part], sem.at[n]))
    for copy in copies:
        copy.start()
    for n in range(stage.shape[0]):
        cols = pl.ds(done + n * width, width)
        stage[n] = weight_block(acts_t, hidden, cols)
        copies.append(pltpu.make_async_copy(stage.at[n], wg_out.at[:, cols], sem.at[5 + n]))
        copies[-1].start()
    for copy in copies:
        copy.wait()


def per_device(acts, up_weight, out_grad):
    tb, feats = acts.shape
    ob, hid = out_grad.shape
    tokens = 16 * tb
    hb = tb // 2
    vmem = lambda *shape: pltpu.VMEM(shape, BF16)
    in_hbm = pl.BlockSpec(memory_space=pltpu.HBM)
    in_vmem = pl.BlockSpec(memory_space=pltpu.VMEM)
    flops = 3 * 2 * tokens * feats * hid
    blocks = hid // tile_of(hid, 256)
    acts, up_weight, out_grad = (
        pltpu.with_memory_space_constraint(a, pltpu.HBM) for a in (acts, up_weight, out_grad)
    )
    input_grad, weight_grad, acts_t, hidden = pl.pallas_call(
        kernel,
        out_shape=(
            vmem(1, 2, hb, feats),
            vmem(feats, hid),
            vmem(feats, tokens),
            vmem(4, 4, 2, hb, hid),
        ),
        in_specs=[in_hbm] * 3,
        out_specs=(in_vmem,) * 4,
        scratch_shapes=[
            vmem(4, 4, 2, hb, feats),
            vmem(hid, feats),
            vmem(ob, hid),
            vmem(4, 4, 2, hb, hid),
            vmem(4, 2, 2, hb, hid),
            vmem(3, 2, hb, hid),
            vmem(3, 2, hb, hid),
            vmem(4, 2, 4, hb, feats),
            vmem(3, 4, 2, hb // 2, feats),
            vmem(3, 4, 2, hb // 2, feats),
            vmem(4, 2, hb, feats),
            vmem(4, 4, 2, hb // 2, feats),
            pltpu.SemaphoreType.DMA((9,)),
            pltpu.SemaphoreType.DMA((N_SEMS,)),
            pltpu.SemaphoreType.DMA((N_SEMS,)),
        ],
        compiler_params=pltpu.CompilerParams(
            collective_id=0, has_side_effects=True, vmem_limit_bytes=41 * 2**20
        ),
        cost_estimate=pl.CostEstimate(flops=flops, bytes_accessed=4 * feats * hid, transcendentals=2 * ob * hid),
    )(acts, up_weight, out_grad)
    return pl.pallas_call(
        write_out,
        out_shape=(
            jax.ShapeDtypeStruct((tb, feats), BF16),
            jax.ShapeDtypeStruct((feats, hid), BF16),
        ),
        in_specs=[in_vmem] * 4,
        out_specs=(in_hbm, in_hbm),
        scratch_shapes=[vmem(blocks // 4, feats, hid // blocks), pltpu.SemaphoreType.DMA((5 + blocks // 4,))],
        compiler_params=pltpu.CompilerParams(vmem_limit_bytes=10 * 2**20),
        cost_estimate=pl.CostEstimate(flops=flops // 12, bytes_accessed=2 * feats * hid, transcendentals=0),
    )(input_grad.reshape(tb, feats), weight_grad, acts_t, hidden)


def solution(mesh):
    in_specs = (P("col", "row"), P("row", "col"), P("row", "col"))
    out_specs = (P("col", "row"), P("row", "col"))
    return jax.shard_map(
        per_device, mesh=mesh, in_specs=in_specs, out_specs=out_specs, check_vma=False
    )
```

```python
import functools

import jax
import jax.numpy as jnp
from jax import lax
from jax.experimental import pallas as pl
from jax.experimental.pallas import tpu as pltpu
from jax.sharding import PartitionSpec as P

F32, BF16 = jnp.float32, jnp.bfloat16
MESH = pl.DeviceIdType.MESH
N_SEMS = 160


def gelu_slope(pre):
    cdf = 0.5 * (1.0 + lax.erf(pre * 0.7071067811865476))
    dens = jnp.exp(-0.5 * pre * pre) * 0.3989422804014327
    return cdf + pre * dens


def tile_of(size, want):
    return want if size % want == 0 else size


def weight_block(acts_t, hidden, cols):
    units = hidden[:, :, :, :, cols]
    units = units.reshape(acts_t.shape[1], units.shape[-1])
    return jnp.dot(acts_t[...], units, preferred_element_type=F32).astype(BF16)


def kernel(
    acts_ref, w_ref, og_ref, ig_ref, wg_ref, acts_t, hidden,
    acts, w_t, og, part, sib_in, z_in_m, z_in_p, ig, y_in_m, y_in_p, xs, x_in,
    local_sem, send_sem, recv_sem,
):
    tb, feats = acts_ref.shape
    ob, hid = og_ref.shape
    quarter = ob // 4
    tv, tn, t3 = tile_of(hid // 2, 512), tile_of(hid // 2, 768), tile_of(hid, 256)
    tf, tm = tile_of(feats, 768), tile_of(feats, 256)
    w = wg_ref

    row, col = lax.axis_index("row"), lax.axis_index("col")
    z, k = lax.div(row, 2), lax.rem(row, 2)
    x, y = lax.div(col, 4), lax.rem(col, 4)
    nxt = lambda v, by: lax.rem(v + by, 4)
    sib = {"row": z * 2 + (1 - k)}
    zp, zm = {"row": nxt(z, 1) * 2 + k}, {"row": nxt(z, 3) * 2 + k}
    xp, xm = {"col": nxt(x, 1) * 4 + y}, {"col": nxt(x, 3) * 4 + y}
    yp, ym = {"col": x * 4 + nxt(y, 1)}, {"col": x * 4 + nxt(y, 3)}

    sent = []

    def ready(src, dst, to):
        i = len(sent)
        sent.append(None)
        return pltpu.make_async_remote_copy(
            src_ref=src, dst_ref=dst, send_sem=send_sem.at[i], recv_sem=recv_sem.at[i],
            device_id=to, device_id_type=MESH,
        )

    def send(src, dst, to):
        copy = ready(src, dst, to)
        copy.start()
        sent[-1] = copy
        return copy

    hb = tb // 2

    def step_of(group):
        away = nxt(group, 4 - z)
        odd, far = lax.rem(away, 2), lax.div(away, 2)
        return odd * (2 - lax.rem(far + y, 2)) + (1 - odd) * (3 - 3 * far)

    barrier = pltpu.get_barrier_semaphore()
    for to in (sib, zp, zm, xp, xm, yp, ym):
        pl.semaphore_signal(barrier, inc=1, device_id=to, device_id_type=MESH)
    load_acts = [
        pltpu.make_async_copy(acts_ref.at[pl.ds(j * hb, hb)], acts.at[step_of(x), y, j], local_sem.at[j])
        for j in range(2)
    ]
    load_og = pltpu.make_async_copy(og_ref, og, local_sem.at[2])
    load_w = [
        pltpu.make_async_copy(w_ref.at[pl.ds(m * tm, tm)], w.at[pl.ds(m * tm, tm)], local_sem.at[3 + m])
        for m in range(feats // tm)
    ]
    for load in (*load_acts, *load_w, load_og):
        load.start()
    for load in load_acts:
        load.wait()
    pl.semaphore_wait(barrier, 7)

    low16, high16 = pl.ds(0, hb // 2), pl.ds(hb // 2, hb // 2)

    def ag_start(block, to_p, to_m):
        a = lambda by: block(by, low16)
        b = lambda by: block(by, high16)
        pa = send(a(0), a(0), to_p)
        mb = send(b(0), b(0), to_m)
        pb = send(b(0), b(0), to_p)
        ma = send(a(0), a(0), to_m)
        return a, b, pa, mb, pb, ma, to_p, to_m

    def ag_forward(state):
        a, b, pa, mb, pb, ma, to_p, to_m = state
        pa.wait_recv()
        fa = send(a(3), a(3), to_p)
        mb.wait_recv()
        fb = send(b(1), b(1), to_m)
        return pb, ma, fa, fb

    def ag_finish(copies):
        for copy in copies:
            copy.wait_recv()

    def x_gather(j):
        return ag_start(lambda by, rows: acts.at[step_of(nxt(x, by)), y, j, rows], xp, xm)

    def y_gather(s, j0, nj):
        return ag_start(lambda by, rows: acts.at[s, nxt(y, by), pl.ds(j0, nj), rows], yp, ym)

    def turn_w(m):
        load_w[m].wait()

        def tile(n, carry):
            cols = pl.ds(pl.multiple_of(n * tm, tm), tm)
            w_t[cols, m * tm:(m + 1) * tm] = w[m * tm:(m + 1) * tm, cols].T
            return carry

        lax.fori_loop(0, hid // tm, tile, 0)

    def dot1(s, j0, nj):
        js = pl.ds(j0, nj)
        sem = len(sent)

        def to_sib(cols):
            return pltpu.make_async_remote_copy(
                src_ref=part.at[s, pl.ds(2 * (1 - k), 2), js, :, cols], dst_ref=sib_in.at[s, :, js, :, cols],
                send_sem=send_sem.at[sem], recv_sem=recv_sem.at[sem], device_id=sib, device_id_type=MESH,
            )

        def tile(n, carry):
            cols = pl.ds(pl.multiple_of(n * tn, tn), tn)
            share = jnp.dot(
                acts[s, :, js].reshape(4 * nj * hb, feats), w[:, cols], preferred_element_type=F32
            )
            part[s, :, js, :, cols] = share.astype(BF16).reshape(4, nj, hb, tn)
            to_sib(cols).start()
            return carry

        lax.fori_loop(0, hid // tn, tile, 0)
        sent.append(to_sib(pl.ds(0, hid)))
        return sent[-1]

    def add_into(dst, src):
        def tile(n, carry):
            cols = pl.ds(pl.multiple_of(n * tv, tv), tv)
            for j in range(dst.shape[0]):
                total = dst[j, :, cols].astype(F32) + src[j, :, cols].astype(F32)
                dst[j, :, cols] = total.astype(BF16)
            return carry

        lax.fori_loop(0, hid // tv, tile, 0)

    def core_sum(s, copy, j0, nj):
        copy.wait_recv()
        js = pl.ds(j0, nj)
        for way in range(2):
            add_into(part.at[s, 2 * k + way, js], sib_in.at[s, way, js])

    mine = lambda s, way: part.at[s, 2 * k + way]
    gx = x_gather(0)
    turn_w(0)
    gx0 = ag_forward(gx)
    gx = x_gather(1)
    turn_w(1)
    ag_finish(gx0)
    g = y_gather(0, 0, 1)
    turn_w(2)
    gx1 = ag_forward(gx)
    g0 = ag_forward(g)
    turn_w(3)
    ag_finish(gx1)
    g = y_gather(0, 1, 1)
    for m in range(4, feats // tm):
        turn_w(m)
    ag_finish(g0)
    opp_p, opp_m = [], []
    c = dot1(0, 0, 1)
    g0 = ag_forward(g)
    g = y_gather(1, 0, 1)
    core_sum(0, c, 0, 1)
    opp_p.append(send(mine(0, 0).at[0], z_in_m.at[0, 0], zp))
    opp_m.append(send(mine(0, 1).at[0], z_in_p.at[0, 0], zm))
    ag_finish(g0)
    c = dot1(0, 1, 1)
    g0 = ag_forward(g)
    g = y_gather(1, 1, 1)
    core_sum(0, c, 1, 1)
    opp_p.append(send(mine(0, 0).at[1], z_in_m.at[0, 1], zp))
    opp_m.append(send(mine(0, 1).at[1], z_in_p.at[0, 1], zm))
    dir_p, dir_m = [], []
    for j in range(2):
        ag_finish(g0)
        c = dot1(1, j, 1)
        g0 = ag_forward(g)
        g = y_gather(2 + j, 0, 2)
        core_sum(1, c, j, 1)
        dir_p.append(send(mine(1, 1).at[j], z_in_m.at[1, j], zp))
        dir_m.append(send(mine(1, 0).at[j], z_in_p.at[1, j], zm))
    ag_finish(g0)
    c = dot1(2, 0, 2)
    g0 = ag_forward(g)
    core_sum(2, c, 0, 2)
    acc_p, acc_m = [], []
    for j in range(2):
        one = pl.ds(j, 1)
        opp_p[j].wait_recv()
        add_into(mine(2, 0).at[one], z_in_m.at[0, one])
        acc_p.append(send(mine(2, 0).at[j], z_in_m.at[2, j], zp))
        opp_m[j].wait_recv()
        add_into(mine(2, 1).at[one], z_in_p.at[0, one])
        acc_m.append(send(mine(2, 1).at[j], z_in_p.at[2, j], zm))
    ag_finish(g0)
    c = dot1(3, 0, 2)
    core_sum(3, c, 0, 2)
    load_og.wait()

    low, high, opp = nxt(z, 3), nxt(z, 1), nxt(z, 2)
    held_in = [(z, 3, 3), (low, 1, 2), (high, 2, 1), (opp, 0, 0)]

    def turn(n, carry):
        cols = pl.ds(pl.multiple_of(n * tm, tm), tm)
        for g, even, odd in held_in:
            rows = [acts[(even, odd)[b % 2], b, :, :, cols].reshape(tb, tm) for b in range(4)]
            acts_t[cols, pl.ds(pl.multiple_of(g * 4 * tb, 4 * tb), 4 * tb)] = jnp.concatenate(rows, axis=0).T
        return carry

    for copy in (*dir_p, *dir_m):
        copy.wait_recv()
    piece = lambda zz, kk, q: hidden.at[zz, 2 * kk + q // 2, q % 2]

    def slope_piece(q, from_m, from_p):
        start = q * quarter

        def tile(n, carry):
            cols = pl.ds(pl.multiple_of(n * tv, tv), tv)
            own = part[3, 2 * k + q // 2, q % 2, :, cols]
            pre = own.astype(F32) + from_m[:, cols].astype(F32) + from_p[:, cols].astype(F32)
            grad = og[start:start + quarter, cols].astype(F32) * gelu_slope(pre)
            hidden[z, 2 * k + q // 2, q % 2, :, cols] = grad.astype(BF16)
            return carry

        lax.fori_loop(0, hid // tv, tile, 0)
        here = piece(z, k, q)
        return send(here, here, sib), send(here, here, zp), send(here, here, zm)

    arrivals = (0, 2, 1, 3)
    own_sends = {}
    for j in range(2):
        acc_p[j].wait_recv()
        own_sends[j] = slope_piece(j, z_in_m.at[2, j], z_in_p.at[1, j])
        acc_m[j].wait_recv()
        own_sends[2 + j] = slope_piece(2 + j, z_in_m.at[1, j], z_in_p.at[2, j])

    def dot2(units):
        def tile(n, carry):
            cols = pl.ds(pl.multiple_of(n * tf, tf), tf)
            rows = [hidden[g, :, j].reshape(4 * hb, hid) for _, g, js in units for j in js]
            rows = rows[0] if len(rows) == 1 else jnp.concatenate(rows, axis=0)
            share = jnp.dot(rows, w_t[:, cols], preferred_element_type=F32).astype(BF16)
            at_row = 0
            for s, _, js in units:
                for j in js:
                    ig[s, j, :, :, cols] = share[at_row:at_row + 4 * hb].reshape(4, hb, tf)
                    at_row += 4 * hb
            return carry

        lax.fori_loop(0, feats // tf, tile, 0)

    def sum_into(out, terms):
        def tile(n, carry):
            cols = pl.ds(pl.multiple_of(n * tv, tv), tv)
            for p in range(out.shape[0]):
                for q in range(out.shape[1]):
                    total = terms[0][p, q, :, cols].astype(F32)
                    for term in terms[1:]:
                        total = total + term[p, q, :, cols].astype(F32)
                    out[p, q, :, cols] = total.astype(BF16)
            return carry

        lax.fori_loop(0, feats // tv, tile, 0)

    ha, hz = pl.ds(0, hb // 2), pl.ds(hb // 2, hb // 2)

    def y_start(s0, ns, j0, nj):
        ss, js = pl.ds(s0, ns), pl.ds(j0, nj)
        blk = lambda by, rows: ig.at[ss, js, nxt(y, by), rows]
        im = lambda n: y_in_m.at[n, ss, js]
        ip = lambda n: y_in_p.at[n, ss, js]
        op = send(blk(2, ha), im(0), yp)
        om = send(blk(2, hz), ip(0), ym)
        dp = send(blk(1, hz), im(1), yp)
        dm = send(blk(3, ha), ip(1), ym)
        return ss, js, blk, im, ip, op, om, dp, dm

    def y_middle(state):
        ss, js, blk, im, ip, op, om, dp, dm = state
        op.wait_recv()
        sum_into(blk(1, ha), [blk(1, ha), im(0)])
        ap = send(blk(1, ha), im(2), yp)
        om.wait_recv()
        sum_into(blk(3, hz), [blk(3, hz), ip(0)])
        am = send(blk(3, hz), ip(2), ym)
        return ss, js, blk, im, ip, (dp, dm, ap, am)

    def y_finish(state):
        ss, js, blk, im, ip, copies = state
        for copy in copies:
            copy.wait_recv()
        sum_into(xs.at[ss, js, ha], [blk(0, ha), im(2), ip(1)])
        sum_into(xs.at[ss, js, hz], [blk(0, hz), im(1), ip(2)])

    def x_copies(s, g, j0, nj):
        one, js = pl.ds(s, 1), pl.ds(j0, nj)
        mine_x = lambda rows: xs.at[one, js, rows]
        slot = lambda n: x_in.at[n, one, js]
        make = lambda rows, n, to: ready(mine_x(rows), slot(n), to)
        copies = (
            make(ha, 0, xp), make(hz, 0, xm), make(hz, 0, xp), make(ha, 1, xp), make(ha, 2, xm), make(hz, 3, xm)
        )
        return nxt(x, 4 - g), mine_x, slot, copies, (j0, nj)

    def x_start(s, g, j0, nj):
        state = x_copies(s, g, j0, nj)
        away, _, _, copies, _ = state

        @pl.when(away == 2)
        def _():
            copies[0].start()
            copies[1].start()

        @pl.when(away == 3)
        def _():
            copies[2].start()

        @pl.when(away == 1)
        def _():
            copies[4].start()

        return state

    def x_middle(state):
        away, mine_x, slot, copies, _ = state

        @pl.when(away == 3)
        def _():
            copies[0].wait_recv()
            sum_into(mine_x(ha), [mine_x(ha), slot(0)])
            copies[3].start()

        @pl.when(away == 1)
        def _():
            copies[1].wait_recv()
            sum_into(mine_x(hz), [mine_x(hz), slot(0)])
            copies[5].start()

    def x_finish(state):
        away, mine_x, slot, copies, (j0, nj) = state
        result = lambda rows: ig_ref.at[pl.ds(0, 1), pl.ds(j0, nj), rows]

        @pl.when(away == 0)
        def _():
            for n in (2, 3, 4, 5):
                copies[n].wait_recv()
            sum_into(result(ha), [mine_x(ha), slot(1), slot(2)])
            sum_into(result(hz), [mine_x(hz), slot(0), slot(3)])

        for role, used in ((2, (0, 1)), (3, (2, 3)), (1, (4, 5))):
            @pl.when(away == role)
            def _(used=used):
                for n in used:
                    copies[n].wait_send()

    blocks = hid // t3 * 3 // 4

    def dot3(lo, hi):
        def tile(n, carry):
            cols = pl.ds(pl.multiple_of(n * t3, t3), t3)
            wg_ref[:, cols] = weight_block(acts_t, hidden, cols)
            return carry

        lax.fori_loop(lo * blocks // 9, hi * blocks // 9, tile, 0)

    def neighbours(qs):
        copies = []
        for q in qs:
            own_sends[q][1].wait_recv()
            here = piece(low, k, q)
            if q < 2:
                fwd[q] = send(here, here, zp)
            copies.append(send(here, here, sib))
            own_sends[q][2].wait_recv()
            here = piece(high, k, q)
            if q >= 2:
                fwd[q] = send(here, here, zm)
            copies.append(send(here, here, sib))
        return copies

    def opposite(qs):
        copies = []
        for q in qs:
            fwd[q].wait_recv()
            here = piece(opp, k, q)
            copies.append(send(here, here, sib))
        return copies

    def arrived(copies):
        for copy in copies:
            copy.wait_recv()

    fwd = {}
    arrived([own_sends[q][0] for q in arrivals])
    dot2([(0, z, (0, 1))])
    y0 = y_start(0, 1, 0, 2)
    lax.fori_loop(0, feats // tm, turn, 0)
    from_sib = neighbours((0, 2))
    y0 = y_middle(y0)
    arrived(from_sib)
    dot2([(1, low, (0,)), (2, high, (0,))])
    y1 = y_start(1, 2, 0, 1)
    y_finish(y0)
    x0 = x_start(0, z, 0, 2)
    from_sib = neighbours((1, 3))
    y1 = y_middle(y1)
    x_middle(x0)
    arrived(from_sib)
    dot2([(1, low, (1,)), (2, high, (1,))])
    y2 = y_start(1, 2, 1, 1)
    from_sib = opposite((0, 2))
    y_finish(y1)
    arrived(from_sib)
    dot2([(3, opp, (0,))])
    y3 = y_start(3, 1, 0, 1)
    y2 = y_middle(y2)
    from_sib = opposite((1, 3))
    x_finish(x0)
    arrived(from_sib)
    dot2([(3, opp, (1,))])
    y4 = y_start(3, 1, 1, 1)
    y3 = y_middle(y3)
    y_finish(y2)
    x1 = x_start(1, low, 0, 2)
    x2 = x_start(2, high, 0, 2)
    dot3(0, 2)
    y4 = y_middle(y4)
    y_finish(y3)
    x3 = x_start(3, opp, 0, 1)
    x_middle(x1)
    x_middle(x2)
    dot3(2, 4)
    y_finish(y4)
    x4 = x_start(3, opp, 1, 1)
    x_middle(x3)
    dot3(4, 6)
    x_middle(x4)
    x_finish(x1)
    x_finish(x2)
    x_finish(x3)
    dot3(6, 9)
    x_finish(x4)

    for copy in sent:
        if copy is not None:
            copy.wait_send()


def write_out(ig_ref, wg_ref, acts_t, hidden, ig_out, wg_out, stage, sem):
    feats, width = stage.shape[1:]
    done = wg_ref.shape[1] - stage.shape[0] * width
    rows = feats // 4
    copies = [pltpu.make_async_copy(ig_ref, ig_out, sem.at[4])]
    for n in range(4):
        part = (pl.ds(n * rows, rows), pl.ds(0, done))
        copies.append(pltpu.make_async_copy(wg_ref.at[part], wg_out.at[part], sem.at[n]))
    for copy in copies:
        copy.start()
    for n in range(stage.shape[0]):
        cols = pl.ds(done + n * width, width)
        stage[n] = weight_block(acts_t, hidden, cols)
        copies.append(pltpu.make_async_copy(stage.at[n], wg_out.at[:, cols], sem.at[5 + n]))
        copies[-1].start()
    for copy in copies:
        copy.wait()


def per_device(acts, up_weight, out_grad):
    tb, feats = acts.shape
    ob, hid = out_grad.shape
    tokens = 16 * tb
    hb = tb // 2
    vmem = lambda *shape: pltpu.VMEM(shape, BF16)
    in_hbm = pl.BlockSpec(memory_space=pltpu.HBM)
    in_vmem = pl.BlockSpec(memory_space=pltpu.VMEM)
    flops = 3 * 2 * tokens * feats * hid
    blocks = hid // tile_of(hid, 256)
    acts, up_weight, out_grad = (
        pltpu.with_memory_space_constraint(a, pltpu.HBM) for a in (acts, up_weight, out_grad)
    )
    input_grad, weight_grad, acts_t, hidden = pl.pallas_call(
        kernel,
        out_shape=(
            vmem(1, 2, hb, feats),
            vmem(feats, hid),
            vmem(feats, tokens),
            vmem(4, 4, 2, hb, hid),
        ),
        in_specs=[in_hbm] * 3,
        out_specs=(in_vmem,) * 4,
        scratch_shapes=[
            vmem(4, 4, 2, hb, feats),
            vmem(hid, feats),
            vmem(ob, hid),
            vmem(4, 4, 2, hb, hid),
            vmem(4, 2, 2, hb, hid),
            vmem(3, 2, hb, hid),
            vmem(3, 2, hb, hid),
            vmem(4, 2, 4, hb, feats),
            vmem(3, 4, 2, hb // 2, feats),
            vmem(3, 4, 2, hb // 2, feats),
            vmem(4, 2, hb, feats),
            vmem(4, 4, 2, hb // 2, feats),
            pltpu.SemaphoreType.DMA((9,)),
            pltpu.SemaphoreType.DMA((N_SEMS,)),
            pltpu.SemaphoreType.DMA((N_SEMS,)),
        ],
        compiler_params=pltpu.CompilerParams(
            collective_id=0, has_side_effects=True, vmem_limit_bytes=41 * 2**20
        ),
        cost_estimate=pl.CostEstimate(flops=flops, bytes_accessed=4 * feats * hid, transcendentals=2 * ob * hid),
    )(acts, up_weight, out_grad)
    return pl.pallas_call(
        write_out,
        out_shape=(
            jax.ShapeDtypeStruct((tb, feats), BF16),
            jax.ShapeDtypeStruct((feats, hid), BF16),
        ),
        in_specs=[in_vmem] * 4,
        out_specs=(in_hbm, in_hbm),
        scratch_shapes=[vmem(blocks // 4, feats, hid // blocks), pltpu.SemaphoreType.DMA((5 + blocks // 4,))],
        compiler_params=pltpu.CompilerParams(vmem_limit_bytes=10 * 2**20),
        cost_estimate=pl.CostEstimate(flops=flops // 12, bytes_accessed=2 * feats * hid, transcendentals=0),
    )(input_grad.reshape(tb, feats), weight_grad, acts_t, hidden)


def solution(mesh):
    in_specs = (P("col", "row"), P("row", "col"), P("row", "col"))
    out_specs = (P("col", "row"), P("row", "col"))
    return jax.shard_map(
        per_device, mesh=mesh, in_specs=in_specs, out_specs=out_specs, check_vma=False
    )
```

```python
import functools

import jax
import jax.numpy as jnp
from jax import lax
from jax.experimental import pallas as pl
from jax.experimental.pallas import tpu as pltpu
from jax.sharding import PartitionSpec as P

F32, BF16 = jnp.float32, jnp.bfloat16
MESH = pl.DeviceIdType.MESH
N_SEMS = 160


def gelu_slope(pre):
    cdf = 0.5 * (1.0 + lax.erf(pre * 0.7071067811865476))
    dens = jnp.exp(-0.5 * pre * pre) * 0.3989422804014327
    return cdf + pre * dens


def tile_of(size, want):
    return want if size % want == 0 else size


def weight_block(acts_t, hidden, cols):
    units = hidden[:, :, :, :, cols]
    units = units.reshape(acts_t.shape[1], units.shape[-1])
    return jnp.dot(acts_t[...], units, preferred_element_type=F32).astype(BF16)


def kernel(
    acts_ref, w_ref, og_ref, ig_ref, wg_ref, acts_t, hidden,
    acts, w_t, og, part, sib_in, z_in_m, z_in_p, ig, y_in_m, y_in_p, xs, x_in,
    local_sem, send_sem, recv_sem,
):
    tb, feats = acts_ref.shape
    ob, hid = og_ref.shape
    quarter = ob // 4
    tv, tn, t3 = tile_of(hid // 2, 512), tile_of(hid // 2, 768), tile_of(hid, 256)
    tf, tm = tile_of(feats, 768), tile_of(feats, 256)
    w = wg_ref

    row, col = lax.axis_index("row"), lax.axis_index("col")
    z, k = lax.div(row, 2), lax.rem(row, 2)
    x, y = lax.div(col, 4), lax.rem(col, 4)
    nxt = lambda v, by: lax.rem(v + by, 4)
    sib = {"row": z * 2 + (1 - k)}
    zp, zm = {"row": nxt(z, 1) * 2 + k}, {"row": nxt(z, 3) * 2 + k}
    xp, xm = {"col": nxt(x, 1) * 4 + y}, {"col": nxt(x, 3) * 4 + y}
    yp, ym = {"col": x * 4 + nxt(y, 1)}, {"col": x * 4 + nxt(y, 3)}

    sent = []

    def ready(src, dst, to):
        i = len(sent)
        sent.append(None)
        return pltpu.make_async_remote_copy(
            src_ref=src, dst_ref=dst, send_sem=send_sem.at[i], recv_sem=recv_sem.at[i],
            device_id=to, device_id_type=MESH,
        )

    def send(src, dst, to):
        copy = ready(src, dst, to)
        copy.start()
        sent[-1] = copy
        return copy

    hb = tb // 2

    def step_of(group):
        away = nxt(group, 4 - z)
        odd, far = lax.rem(away, 2), lax.div(away, 2)
        return odd * (2 - lax.rem(far + y, 2)) + (1 - odd) * (3 - 3 * far)

    barrier = pltpu.get_barrier_semaphore()
    for to in (sib, zp, zm, xp, xm, yp, ym):
        pl.semaphore_signal(barrier, inc=1, device_id=to, device_id_type=MESH)
    load_acts = [
        pltpu.make_async_copy(acts_ref.at[pl.ds(j * hb, hb)], acts.at[step_of(x), y, j], local_sem.at[j])
        for j in range(2)
    ]
    load_og = pltpu.make_async_copy(og_ref, og, local_sem.at[2])
    load_w = [
        pltpu.make_async_copy(w_ref.at[pl.ds(m * tm, tm)], w.at[pl.ds(m * tm, tm)], local_sem.at[3 + m])
        for m in range(feats // tm)
    ]
    for load in (*load_acts, *load_w, load_og):
        load.start()
    for load in load_acts:
        load.wait()
    pl.semaphore_wait(barrier, 7)

    low16, high16 = pl.ds(0, hb // 2), pl.ds(hb // 2, hb // 2)

    def ag_start(block, to_p, to_m):
        a = lambda by: block(by, low16)
        b = lambda by: block(by, high16)
        pa = send(a(0), a(0), to_p)
        mb = send(b(0), b(0), to_m)
        pb = send(b(0), b(0), to_p)
        ma = send(a(0), a(0), to_m)
        return a, b, pa, mb, pb, ma, to_p, to_m

    def ag_forward(state):
        a, b, pa, mb, pb, ma, to_p, to_m = state
        pa.wait_recv()
        fa = send(a(3), a(3), to_p)
        mb.wait_recv()
        fb = send(b(1), b(1), to_m)
        return pb, ma, fa, fb

    def ag_finish(copies):
        for copy in copies:
            copy.wait_recv()

    def x_gather(j):
        return ag_start(lambda by, rows: acts.at[step_of(nxt(x, by)), y, j, rows], xp, xm)

    def y_gather(s, j0, nj):
        return ag_start(lambda by, rows: acts.at[s, nxt(y, by), pl.ds(j0, nj), rows], yp, ym)

    def turn_w(m):
        load_w[m].wait()

        def tile(n, carry):
            cols = pl.ds(pl.multiple_of(n * tm, tm), tm)
            w_t[cols, m * tm:(m + 1) * tm] = w[m * tm:(m + 1) * tm, cols].T
            return carry

        lax.fori_loop(0, hid // tm, tile, 0)

    def dot1(s, j0, nj):
        js = pl.ds(j0, nj)
        sem = len(sent)

        def to_sib(cols):
            return pltpu.make_async_remote_copy(
                src_ref=part.at[s, pl.ds(2 * (1 - k), 2), js, :, cols], dst_ref=sib_in.at[s, :, js, :, cols],
                send_sem=send_sem.at[sem], recv_sem=recv_sem.at[sem], device_id=sib, device_id_type=MESH,
            )

        def tile(n, carry):
            cols = pl.ds(pl.multiple_of(n * tn, tn), tn)
            share = jnp.dot(
                acts[s, :, js].reshape(4 * nj * hb, feats), w[:, cols], preferred_element_type=F32
            )
            part[s, :, js, :, cols] = share.astype(BF16).reshape(4, nj, hb, tn)
            to_sib(cols).start()
            return carry

        lax.fori_loop(0, hid // tn, tile, 0)
        sent.append(to_sib(pl.ds(0, hid)))
        return sent[-1]

    def add_into(dst, src):
        def tile(n, carry):
            cols = pl.ds(pl.multiple_of(n * tv, tv), tv)
            for j in range(dst.shape[0]):
                total = dst[j, :, cols].astype(F32) + src[j, :, cols].astype(F32)
                dst[j, :, cols] = total.astype(BF16)
            return carry

        lax.fori_loop(0, hid // tv, tile, 0)

    def core_sum(s, copy, j0, nj):
        copy.wait_recv()
        js = pl.ds(j0, nj)
        for way in range(2):
            add_into(part.at[s, 2 * k + way, js], sib_in.at[s, way, js])

    mine = lambda s, way: part.at[s, 2 * k + way]
    gx = x_gather(0)
    turn_w(0)
    gx0 = ag_forward(gx)
    gx = x_gather(1)
    turn_w(1)
    ag_finish(gx0)
    g = y_gather(0, 0, 1)
    turn_w(2)
    gx1 = ag_forward(gx)
    g0 = ag_forward(g)
    turn_w(3)
    ag_finish(gx1)
    g = y_gather(0, 1, 1)
    for m in range(4, feats // tm):
        turn_w(m)
    ag_finish(g0)
    g0 = ag_forward(g)
    g = y_gather(1, 0, 2)
    ag_finish(g0)
    c = dot1(0, 0, 2)
    g0 = ag_forward(g)
    g = y_gather(2, 0, 2)
    core_sum(0, c, 0, 2)
    opp_p = [send(mine(0, 0).at[j], z_in_m.at[0, j], zp) for j in range(2)]
    opp_m = [send(mine(0, 1).at[j], z_in_p.at[0, j], zm) for j in range(2)]
    ag_finish(g0)
    c = dot1(1, 0, 2)
    g0 = ag_forward(g)
    g = y_gather(3, 0, 2)
    core_sum(1, c, 0, 2)
    dir_p = send(mine(1, 1), z_in_m.at[1], zp)
    dir_m = send(mine(1, 0), z_in_p.at[1], zm)
    ag_finish(g0)
    c = dot1(2, 0, 2)
    g0 = ag_forward(g)
    core_sum(2, c, 0, 2)
    acc_p, acc_m = [], []
    for j in range(2):
        one = pl.ds(j, 1)
        opp_p[j].wait_recv()
        add_into(mine(2, 0).at[one], z_in_m.at[0, one])
        acc_p.append(send(mine(2, 0).at[j], z_in_m.at[2, j], zp))
        opp_m[j].wait_recv()
        add_into(mine(2, 1).at[one], z_in_p.at[0, one])
        acc_m.append(send(mine(2, 1).at[j], z_in_p.at[2, j], zm))
    ag_finish(g0)
    c = dot1(3, 0, 2)
    core_sum(3, c, 0, 2)
    load_og.wait()

    low, high, opp = nxt(z, 3), nxt(z, 1), nxt(z, 2)
    held_in = [(z, 3, 3), (low, 1, 2), (high, 2, 1), (opp, 0, 0)]

    def turn(n, carry):
        cols = pl.ds(pl.multiple_of(n * tm, tm), tm)
        for g, even, odd in held_in:
            rows = [acts[(even, odd)[b % 2], b, :, :, cols].reshape(tb, tm) for b in range(4)]
            acts_t[cols, pl.ds(pl.multiple_of(g * 4 * tb, 4 * tb), 4 * tb)] = jnp.concatenate(rows, axis=0).T
        return carry

    dir_p.wait_recv()
    dir_m.wait_recv()
    piece = lambda zz, kk, q: hidden.at[zz, 2 * kk + q // 2, q % 2]

    def slope_piece(q, from_m, from_p):
        start = q * quarter

        def tile(n, carry):
            cols = pl.ds(pl.multiple_of(n * tv, tv), tv)
            own = part[3, 2 * k + q // 2, q % 2, :, cols]
            pre = own.astype(F32) + from_m[:, cols].astype(F32) + from_p[:, cols].astype(F32)
            grad = og[start:start + quarter, cols].astype(F32) * gelu_slope(pre)
            hidden[z, 2 * k + q // 2, q % 2, :, cols] = grad.astype(BF16)
            return carry

        lax.fori_loop(0, hid // tv, tile, 0)
        here = piece(z, k, q)
        return send(here, here, sib), send(here, here, zp), send(here, here, zm)

    arrivals = (0, 2, 1, 3)
    own_sends = {}
    for j in range(2):
        acc_p[j].wait_recv()
        own_sends[j] = slope_piece(j, z_in_m.at[2, j], z_in_p.at[1, j])
        acc_m[j].wait_recv()
        own_sends[2 + j] = slope_piece(2 + j, z_in_m.at[1, j], z_in_p.at[2, j])

    def dot2(units):
        def tile(n, carry):
            cols = pl.ds(pl.multiple_of(n * tf, tf), tf)
            rows = [hidden[g, :, j].reshape(4 * hb, hid) for _, g, js in units for j in js]
            rows = rows[0] if len(rows) == 1 else jnp.concatenate(rows, axis=0)
            share = jnp.dot(rows, w_t[:, cols], preferred_element_type=F32).astype(BF16)
            at_row = 0
            for s, _, js in units:
                for j in js:
                    ig[s, j, :, :, cols] = share[at_row:at_row + 4 * hb].reshape(4, hb, tf)
                    at_row += 4 * hb
            return carry

        lax.fori_loop(0, feats // tf, tile, 0)

    def sum_into(out, terms):
        def tile(n, carry):
            cols = pl.ds(pl.multiple_of(n * tv, tv), tv)
            for p in range(out.shape[0]):
                for q in range(out.shape[1]):
                    total = terms[0][p, q, :, cols].astype(F32)
                    for term in terms[1:]:
                        total = total + term[p, q, :, cols].astype(F32)
                    out[p, q, :, cols] = total.astype(BF16)
            return carry

        lax.fori_loop(0, feats // tv, tile, 0)

    ha, hz = pl.ds(0, hb // 2), pl.ds(hb // 2, hb // 2)

    def y_start(s0, ns, j0, nj):
        ss, js = pl.ds(s0, ns), pl.ds(j0, nj)
        blk = lambda by, rows: ig.at[ss, js, nxt(y, by), rows]
        im = lambda n: y_in_m.at[n, ss, js]
        ip = lambda n: y_in_p.at[n, ss, js]
        op = send(blk(2, ha), im(0), yp)
        om = send(blk(2, hz), ip(0), ym)
        dp = send(blk(1, hz), im(1), yp)
        dm = send(blk(3, ha), ip(1), ym)
        return ss, js, blk, im, ip, op, om, dp, dm

    def y_middle(state):
        ss, js, blk, im, ip, op, om, dp, dm = state
        op.wait_recv()
        sum_into(blk(1, ha), [blk(1, ha), im(0)])
        ap = send(blk(1, ha), im(2), yp)
        om.wait_recv()
        sum_into(blk(3, hz), [blk(3, hz), ip(0)])
        am = send(blk(3, hz), ip(2), ym)
        return ss, js, blk, im, ip, (dp, dm, ap, am)

    def y_finish(state):
        ss, js, blk, im, ip, copies = state
        for copy in copies:
            copy.wait_recv()
        sum_into(xs.at[ss, js, ha], [blk(0, ha), im(2), ip(1)])
        sum_into(xs.at[ss, js, hz], [blk(0, hz), im(1), ip(2)])

    def x_copies(s, g, j0, nj):
        one, js = pl.ds(s, 1), pl.ds(j0, nj)
        mine_x = lambda rows: xs.at[one, js, rows]
        slot = lambda n: x_in.at[n, one, js]
        make = lambda rows, n, to: ready(mine_x(rows), slot(n), to)
        copies = (
            make(ha, 0, xp), make(hz, 0, xm), make(hz, 0, xp), make(ha, 1, xp), make(ha, 2, xm), make(hz, 3, xm)
        )
        return nxt(x, 4 - g), mine_x, slot, copies, (j0, nj)

    def x_start(s, g, j0, nj):
        state = x_copies(s, g, j0, nj)
        away, _, _, copies, _ = state

        @pl.when(away == 2)
        def _():
            copies[0].start()
            copies[1].start()

        @pl.when(away == 3)
        def _():
            copies[2].start()

        @pl.when(away == 1)
        def _():
            copies[4].start()

        return state

    def x_middle(state):
        away, mine_x, slot, copies, _ = state

        @pl.when(away == 3)
        def _():
            copies[0].wait_recv()
            sum_into(mine_x(ha), [mine_x(ha), slot(0)])
            copies[3].start()

        @pl.when(away == 1)
        def _():
            copies[1].wait_recv()
            sum_into(mine_x(hz), [mine_x(hz), slot(0)])
            copies[5].start()

    def x_finish(state):
        away, mine_x, slot, copies, (j0, nj) = state
        result = lambda rows: ig_ref.at[pl.ds(0, 1), pl.ds(j0, nj), rows]

        @pl.when(away == 0)
        def _():
            for n in (2, 3, 4, 5):
                copies[n].wait_recv()
            sum_into(result(ha), [mine_x(ha), slot(1), slot(2)])
            sum_into(result(hz), [mine_x(hz), slot(0), slot(3)])

        for role, used in ((2, (0, 1)), (3, (2, 3)), (1, (4, 5))):
            @pl.when(away == role)
            def _(used=used):
                for n in used:
                    copies[n].wait_send()

    blocks = hid // t3 * 3 // 4

    def dot3(lo, hi):
        def tile(n, carry):
            cols = pl.ds(pl.multiple_of(n * t3, t3), t3)
            wg_ref[:, cols] = weight_block(acts_t, hidden, cols)
            return carry

        lax.fori_loop(lo * blocks // 9, hi * blocks // 9, tile, 0)

    def neighbours(qs):
        copies = []
        for q in qs:
            own_sends[q][1].wait_recv()
            here = piece(low, k, q)
            if q < 2:
                fwd[q] = send(here, here, zp)
            copies.append(send(here, here, sib))
            own_sends[q][2].wait_recv()
            here = piece(high, k, q)
            if q >= 2:
                fwd[q] = send(here, here, zm)
            copies.append(send(here, here, sib))
        return copies

    def opposite(qs):
        copies = []
        for q in qs:
            fwd[q].wait_recv()
            here = piece(opp, k, q)
            copies.append(send(here, here, sib))
        return copies

    def arrived(copies):
        for copy in copies:
            copy.wait_recv()

    fwd = {}
    arrived([own_sends[q][0] for q in arrivals])
    dot2([(0, z, (0, 1))])
    y0 = y_start(0, 1, 0, 2)
    lax.fori_loop(0, feats // tm, turn, 0)
    from_sib = neighbours((0, 2))
    y0 = y_middle(y0)
    arrived(from_sib)
    dot2([(1, low, (0,)), (2, high, (0,))])
    y1 = y_start(1, 2, 0, 1)
    y_finish(y0)
    x0 = x_start(0, z, 0, 2)
    from_sib = neighbours((1, 3))
    y1 = y_middle(y1)
    x_middle(x0)
    arrived(from_sib)
    dot2([(1, low, (1,)), (2, high, (1,))])
    y2 = y_start(1, 2, 1, 1)
    from_sib = opposite((0, 2))
    y_finish(y1)
    arrived(from_sib)
    dot2([(3, opp, (0,))])
    y3 = y_start(3, 1, 0, 1)
    y2 = y_middle(y2)
    from_sib = opposite((1, 3))
    x_finish(x0)
    arrived(from_sib)
    dot2([(3, opp, (1,))])
    y4 = y_start(3, 1, 1, 1)
    y3 = y_middle(y3)
    y_finish(y2)
    x1 = x_start(1, low, 0, 2)
    x2 = x_start(2, high, 0, 2)
    dot3(0, 2)
    y4 = y_middle(y4)
    y_finish(y3)
    x3 = x_start(3, opp, 0, 1)
    x_middle(x1)
    x_middle(x2)
    dot3(2, 4)
    y_finish(y4)
    x4 = x_start(3, opp, 1, 1)
    x_middle(x3)
    dot3(4, 6)
    x_middle(x4)
    x_finish(x1)
    x_finish(x2)
    x_finish(x3)
    dot3(6, 9)
    x_finish(x4)

    for copy in sent:
        if copy is not None:
            copy.wait_send()


def write_out(ig_ref, wg_ref, acts_t, hidden, ig_out, wg_out, stage, sem):
    feats, width = stage.shape[1:]
    done = wg_ref.shape[1] - stage.shape[0] * width
    rows = feats // 4
    copies = [pltpu.make_async_copy(ig_ref, ig_out, sem.at[4])]
    for n in range(4):
        part = (pl.ds(n * rows, rows), pl.ds(0, done))
        copies.append(pltpu.make_async_copy(wg_ref.at[part], wg_out.at[part], sem.at[n]))
    for copy in copies:
        copy.start()
    for n in range(stage.shape[0]):
        cols = pl.ds(done + n * width, width)
        stage[n] = weight_block(acts_t, hidden, cols)
        copies.append(pltpu.make_async_copy(stage.at[n], wg_out.at[:, cols], sem.at[5 + n]))
        copies[-1].start()
    for copy in copies:
        copy.wait()


def per_device(acts, up_weight, out_grad):
    tb, feats = acts.shape
    ob, hid = out_grad.shape
    tokens = 16 * tb
    hb = tb // 2
    vmem = lambda *shape: pltpu.VMEM(shape, BF16)
    in_hbm = pl.BlockSpec(memory_space=pltpu.HBM)
    in_vmem = pl.BlockSpec(memory_space=pltpu.VMEM)
    flops = 3 * 2 * tokens * feats * hid
    blocks = hid // tile_of(hid, 256)
    acts, up_weight, out_grad = (
        pltpu.with_memory_space_constraint(a, pltpu.HBM) for a in (acts, up_weight, out_grad)
    )
    input_grad, weight_grad, acts_t, hidden = pl.pallas_call(
        kernel,
        out_shape=(
            vmem(1, 2, hb, feats),
            vmem(feats, hid),
            vmem(feats, tokens),
            vmem(4, 4, 2, hb, hid),
        ),
        in_specs=[in_hbm] * 3,
        out_specs=(in_vmem,) * 4,
        scratch_shapes=[
            vmem(4, 4, 2, hb, feats),
            vmem(hid, feats),
            vmem(ob, hid),
            vmem(4, 4, 2, hb, hid),
            vmem(4, 2, 2, hb, hid),
            vmem(3, 2, hb, hid),
            vmem(3, 2, hb, hid),
            vmem(4, 2, 4, hb, feats),
            vmem(3, 4, 2, hb // 2, feats),
            vmem(3, 4, 2, hb // 2, feats),
            vmem(4, 2, hb, feats),
            vmem(4, 4, 2, hb // 2, feats),
            pltpu.SemaphoreType.DMA((9,)),
            pltpu.SemaphoreType.DMA((N_SEMS,)),
            pltpu.SemaphoreType.DMA((N_SEMS,)),
        ],
        compiler_params=pltpu.CompilerParams(
            collective_id=0, has_side_effects=True, vmem_limit_bytes=41 * 2**20
        ),
        cost_estimate=pl.CostEstimate(flops=flops, bytes_accessed=4 * feats * hid, transcendentals=2 * ob * hid),
    )(acts, up_weight, out_grad)
    return pl.pallas_call(
        write_out,
        out_shape=(
            jax.ShapeDtypeStruct((tb, feats), BF16),
            jax.ShapeDtypeStruct((feats, hid), BF16),
        ),
        in_specs=[in_vmem] * 4,
        out_specs=(in_hbm, in_hbm),
        scratch_shapes=[vmem(blocks // 4, feats, hid // blocks), pltpu.SemaphoreType.DMA((5 + blocks // 4,))],
        compiler_params=pltpu.CompilerParams(vmem_limit_bytes=10 * 2**20),
        cost_estimate=pl.CostEstimate(flops=flops // 12, bytes_accessed=2 * feats * hid, transcendentals=0),
    )(input_grad.reshape(tb, feats), weight_grad, acts_t, hidden)


def solution(mesh):
    in_specs = (P("col", "row"), P("row", "col"), P("row", "col"))
    out_specs = (P("col", "row"), P("row", "col"))
    return jax.shard_map(
        per_device, mesh=mesh, in_specs=in_specs, out_specs=out_specs, check_vma=False
    )
```
